256 devices in a mesh: tm: 8 (over z), height: 4 (over x_hi, core), width: 8 (over y, x_lo).
Axes of the slice: x: 4 (x_hi: 2, x_lo: 2; x = x_hi * 2 + x_lo), y: 4, z: 8, core: 2. Of those that a mesh axis runs over, the one named last changes fastest.
Arguments:
- features: bfloat16 [16, 128, 512, 128], P('tm', 'height', 'width'), may hold values from -6 to 6
- gain_fine: float32 [128], replicated, may hold values from 0.25 to 1.75
- conv_fine: bfloat16 [3, 3, 3, 128, 128], replicated, may hold values from -0.109375 to 0.109375
- down_fine: bfloat16 [1024, 256], replicated, may hold values from -0.1875 to 0.1875
- gain_coarse: float32 [256], replicated, may hold values from 0.25 to 1.75
- conv_coarse: bfloat16 [3, 3, 3, 256, 256], replicated, may hold values from -0.078125 to 0.078125
- down_coarse: bfloat16 [1024, 512], replicated, may hold values from -0.1875 to 0.1875
- gain_latent: float32 [512], replicated, may hold values from 0.25 to 1.75
- w_query: bfloat16 [512, 512], replicated, as said below
- w_key: bfloat16 [512, 512], replicated, as said below
- w_value: bfloat16 [512, 512], replicated, may hold values from -0.25 to 0.25
- w_out: bfloat16 [512, 512], replicated, may hold values from -0.25 to 0.25
Outputs:
- latent: bfloat16 [8, 32, 128, 512], P('tm', 'height', 'width')
The draws below stay inside these ranges and needn't reach their ends.
Inputs may be any that keep to these rules, and one draw needn't show every extreme that they name: `w_query`: a projection with entries of order 2.5 over the square root of 512. `w_key`: a projection.
All inputs are finite; a program needn't handle non-finite values.
Results may differ from the reference program's by a relative error of at most 0.015.
Values may be sent and summed in bfloat16 or wider, within the bound.
No kernel may reach another device: no remote copies, remote signals or barrier semaphores. Data moves between devices by JAX's collectives and lax.ppermute only.
A program may use at most 192 MiB of HBM per device.

```python
import math
import jax
import jax.numpy as jnp
from jax import lax

C0 = 128
C1 = 256
C2 = 512
FRAMES = 16
ROWS = 128
COLS = 512


def shared_rows(key):
    return jax.random.normal(key, (C2, C2), jnp.float32) / math.sqrt(C2)


def draw_w_query(key, part):
    common = shared_rows(key)
    return (2.5 * common).astype(jnp.bfloat16)


def draw_w_key(key, part):
    key = jax.random.fold_in(key, 7)
    own_rows = jax.random.normal(key, (C2, C2), jnp.float32) / math.sqrt(C2)
    mixture = own_rows
    return mixture.astype(jnp.bfloat16)


def level_of(own_key, dims, cuts, smallest, largest):
    level = 1.0
    for axis_at, parts in cuts:
        heights = jax.random.uniform(jax.random.fold_in(jax.random.fold_in(own_key, 6), axis_at), (parts,), jnp.float32, smallest / len(cuts), largest / len(cuts))
        level = level * jnp.repeat(jnp.exp(heights), dims[axis_at] // parts).reshape((-1,) + (1,) * (len(dims) - 1 - axis_at))
    return level


def centred(key, dims, deviation, bound, pieces=(), dtype=jnp.bfloat16):
    drawn = jax.random.normal(key, dims, jnp.float32) * deviation
    if len(pieces) > 0:
        drawn = level_of(key, dims, pieces, -0.22, 0.18) * drawn
    return jnp.clip(drawn, min=-bound, max=bound).astype(dtype)


def setup_inputs(seed: int = 0) -> dict:
    key_of = jax.random.split(jax.random.key(seed), 13)
    features = centred(key_of[0], (FRAMES, ROWS, COLS, C0), 1.0, 6.0, ((0, 8), (1, 4), (2, 8)))
    gain_fine = jnp.clip(1.0 + 0.15 * jax.random.normal(key_of[1], (C0,), jnp.float32), 0.25, 1.75)
    conv_fine = centred(key_of[2], (3, 3, 3, C0, C0), (27 * C0) ** -0.5, 0.109375)
    down_fine = centred(key_of[3], (8 * C0, C1), (8 * C0) ** -0.5, 0.1875)
    gain_coarse = jnp.clip(1.0 + 0.15 * jax.random.normal(key_of[4], (C1,), jnp.float32), 0.25, 1.75)
    conv_coarse = centred(key_of[5], (3, 3, 3, C1, C1), (27 * C1) ** -0.5, 0.078125)
    down_coarse = centred(key_of[6], (4 * C1, C2), (4 * C1) ** -0.5, 0.1875)
    gain_latent = jnp.clip(1.0 + 0.15 * jax.random.normal(key_of[7], (C2,), jnp.float32), 0.25, 1.75)
    w_query = draw_w_query(jax.random.fold_in(key_of[12], 71), 0)
    w_key = draw_w_key(jax.random.fold_in(key_of[12], 71), 0)
    w_value = centred(key_of[10], (C2, C2), C2 ** -0.5, 0.25)
    w_out = centred(key_of[11], (C2, C2), C2 ** -0.5, 0.25)
    return {"features": features, "gain_fine": gain_fine, "conv_fine": conv_fine, "down_fine": down_fine, "gain_coarse": gain_coarse, "conv_coarse": conv_coarse, "down_coarse": down_coarse, "gain_latent": gain_latent, "w_query": w_query, "w_key": w_key, "w_value": w_value, "w_out": w_out}


EPSILON = 1e-06

def channel_norm(inputs, gain):
    values_f = inputs.astype(jnp.float32)
    return values_f * lax.rsqrt(lax.optimization_barrier(jnp.mean(values_f * values_f, axis=-1, keepdims=True)) + EPSILON) * gain.astype(jnp.float32)

def project(inputs, weight):
    flat = inputs.reshape(-1, inputs.shape[-1])
    result = jnp.dot(flat, weight, preferred_element_type=jnp.float32)
    return result.reshape(inputs.shape[:-1] + (weight.shape[-1],))

def causal_conv(padded, weight, frames):
    height = padded.shape[1] - 2
    breadth = padded.shape[2] - 2
    summed = jnp.zeros((frames, height, breadth, weight.shape[-1]), jnp.float32)
    for shift_t in range(3):
        for shift_h in range(3):
            for shift_w in range(3):
                window = padded[shift_t:shift_t + frames, shift_h:shift_h + height, shift_w:shift_w + breadth]
                summed = summed + project(window, weight[shift_t, shift_h, shift_w])
    return summed

def conv_level(active, weight):
    first_frame = active[:1]
    stacked = jnp.concatenate([first_frame, first_frame, active], 0)
    padded = jnp.pad(stacked, ((0, 0), (1, 1), (1, 1), (0, 0)))
    outputs = [causal_conv(padded[index:index + 3], weight, 1) for index in range(active.shape[0])]
    return jnp.concatenate(outputs, 0)

def fold_space_time(hidden):
    frames, height, breadth, channels = hidden.shape
    grouped = hidden.reshape(frames // 2, 2, height // 2, 2, breadth // 2, 2, channels)
    grouped = grouped.transpose(0, 2, 4, 1, 3, 5, 6)
    return grouped.reshape(frames // 2, height // 2, breadth // 2, 8 * channels)

def fold_space(hidden):
    frames, height, breadth, channels = hidden.shape
    grouped = hidden.reshape(frames, height // 2, 2, breadth // 2, 2, channels)
    grouped = grouped.transpose(0, 1, 3, 2, 4, 5)
    return grouped.reshape(frames, height // 2, breadth // 2, 4 * channels)

def frame_attention(operands):
    queries, key_rows, value_rows = operands
    scores = jnp.dot(queries, key_rows.T, preferred_element_type=jnp.float32) / math.sqrt(queries.shape[-1])
    expo = jnp.exp(scores - lax.optimization_barrier(jnp.max(scores, axis=-1, keepdims=True)))
    row_total = lax.optimization_barrier(jnp.sum(expo, axis=-1, keepdims=True))
    summed = jnp.dot(expo.astype(jnp.bfloat16), value_rows, preferred_element_type=jnp.float32)
    return (summed / row_total).astype(jnp.bfloat16)

def reference(features, gain_fine, conv_fine, down_fine, gain_coarse, conv_coarse, down_coarse, gain_latent, w_query, w_key, w_value, w_out):
    active_fine = jax.nn.silu(channel_norm(features, gain_fine)).astype(jnp.bfloat16)
    hidden_fine = (features.astype(jnp.float32) + conv_level(active_fine, conv_fine)).astype(jnp.bfloat16)
    reduced = project(fold_space_time(hidden_fine), down_fine).astype(jnp.bfloat16)
    active_coarse = jax.nn.silu(channel_norm(reduced, gain_coarse)).astype(jnp.bfloat16)
    hidden_coarse = (reduced.astype(jnp.float32) + conv_level(active_coarse, conv_coarse)).astype(jnp.bfloat16)
    latent_in = project(fold_space(hidden_coarse), down_coarse).astype(jnp.bfloat16)
    normed = channel_norm(latent_in, gain_latent).astype(jnp.bfloat16)
    frames, height, breadth, channels = normed.shape
    tokens_flat = normed.reshape(frames, height * breadth, channels)
    queries = project(tokens_flat, w_query).astype(jnp.bfloat16)
    key_rows = project(tokens_flat, w_key).astype(jnp.bfloat16)
    value_rows = project(tokens_flat, w_value).astype(jnp.bfloat16)
    attended = lax.map(frame_attention, (queries, key_rows, value_rows))
    combined = latent_in.astype(jnp.float32) + project(attended, w_out).reshape(latent_in.shape)
    return combined.astype(jnp.bfloat16)
```

```python
import math

import jax
import jax.numpy as jnp
from jax import lax
from jax.sharding import Mesh, PartitionSpec as P

EPSILON = 1e-06
BF16 = jnp.bfloat16
F32 = jnp.float32
HEIGHT = ("hx", "core")
ALL_GATHER = ("hx", "width")


def swapped(value, axis, count, first):
    pairs = []
    for low in range(first, count - 1, 2):
        pairs += [(low, low + 1), (low + 1, low)]
    return lax.ppermute(value, axis, pairs)


def halo(block, axis, dim, width, count):
    even = lax.axis_index(axis) % 2 == 0
    low = lax.slice_in_dim(block, 0, width, axis=dim)
    high = lax.slice_in_dim(block, block.shape[dim] - width, None, axis=dim)
    got_inner = swapped(jnp.where(even, high, low), axis, count, 0)
    got_outer = swapped(jnp.where(even, low, high), axis, count, 1)
    before = jnp.where(even, got_outer, got_inner)
    after = jnp.where(even, got_inner, got_outer)
    return jnp.concatenate([before, block, after], axis=dim)


def channel_norm(inputs, gain):
    values = inputs.astype(F32)
    return values * lax.rsqrt(jnp.mean(values * values, axis=-1, keepdims=True) + EPSILON) * gain


def composed_fine(conv_fine, down_fine, at_start):
    taps = conv_fine.astype(F32)
    k0, k1, k2 = taps[0], taps[1], taps[2]
    both = k0 + k1
    k2s = jnp.where(at_start, both + k2, k2)
    k1s = jnp.where(at_start, both, k1)
    zero = jnp.zeros_like(k0)
    left = jnp.stack([k2s, zero, k0, k1], 0)
    right = jnp.stack([k1s, k2, zero, k0], 0)
    lhs = jnp.concatenate([left, right], -1).astype(BF16)
    lhs = lhs.transpose(0, 3, 1, 2, 4).reshape(512, 3, 3, 256)
    down = down_fine.reshape(2, 2, 2, 128, 256).transpose(1, 2, 0, 3, 4).reshape(2, 2, 256, 256)
    down = down[::-1, ::-1]
    out = lax.conv_general_dilated(
        lhs, down, (1, 1), ((1, 1), (1, 1)),
        dimension_numbers=("NHWC", "HWIO", "NHWC"), preferred_element_type=F32,
    ).astype(BF16)
    out = out.reshape(2, 256, 4, 4, 256).transpose(2, 3, 1, 0, 4)
    return out.reshape(4, 4, 256, 512)


def fold(field):
    rows, cols, channels = field.shape
    grouped = field.reshape(rows // 2, 2, cols // 2, 2, channels).transpose(0, 2, 1, 3, 4)
    return grouped.reshape(rows // 2 * (cols // 2), 4 * channels)


def dot(a, b):
    return jnp.dot(a, b, preferred_element_type=F32)


def per_device(
    features, gain_fine, conv_fine, down_fine, gain_coarse, conv_coarse, down_coarse,
    gain_latent, w_query, w_key, w_value, w_out,
):
    tm = lax.axis_index("tm")
    at_start = tm == 0
    h, w = lax.axis_index(HEIGHT), lax.axis_index("width")
    padded = halo(features, HEIGHT, 1, 3, 4)
    padded = halo(padded, "width", 2, 3, 8)
    weight = composed_fine(conv_fine, down_fine, at_start)
    scale = 1.0 / math.sqrt(512)
    w_score = (jnp.einsum("ab,cb->ac", w_query, w_key, preferred_element_type=F32) * scale).astype(BF16)
    w_mix = dot(w_value, w_out).astype(BF16)
    active = jax.nn.silu(channel_norm(padded, gain_fine)).astype(BF16)
    active = jnp.concatenate([active[0], active[1]], -1)
    out = lax.conv_general_dilated(
        active[None], weight, (2, 2), "VALID",
        dimension_numbers=("NHWC", "HWIO", "NHWC"), preferred_element_type=F32,
    )[0]
    sent = lax.ppermute(out[..., 256:].astype(BF16), "tm", [(i, i + 1) for i in range(7)])
    plain = jnp.concatenate([padded[0], padded[1]], -1)[1:37, 1:69]
    down = down_fine.reshape(2, 2, 2, 128, 256).transpose(1, 2, 0, 3, 4).reshape(1024, 256)
    own = out[..., :256] + dot(fold(plain), down).reshape(18, 34, 256)
    reduced = (own + sent.astype(F32)).astype(BF16)
    rows = jnp.arange(18)[:, None, None]
    cols = jnp.arange(34)[None, :, None]
    inside = ((rows > 0) | (h > 0)) & ((rows < 17) | (h < 3)) & ((cols > 0) | (w > 0)) & ((cols < 33) | (w < 7))
    active_coarse = jnp.where(inside, jax.nn.silu(channel_norm(reduced, gain_coarse)), 0.0).astype(BF16)
    kernel = conv_coarse.transpose(1, 2, 3, 0, 4).reshape(3, 3, 256, 768)
    conv = lax.conv_general_dilated(
        active_coarse[None], kernel, (1, 1), "VALID",
        dimension_numbers=("NHWC", "HWIO", "NHWC"), preferred_element_type=F32,
    )[0]
    c0, c1, c2 = conv[..., :256], conv[..., 256:512], conv[..., 512:]
    c1 = jnp.where(at_start, c1 + c0, c1)
    c2 = jnp.where(at_start, c2 + c1, c2)
    far = dot(fold(c0.astype(BF16)), down_coarse).astype(BF16)
    near = dot(fold(c1.astype(BF16)), down_coarse).astype(BF16)
    near = lax.ppermute(near, "tm", [(i, i + 1) for i in range(7)])
    far = lax.ppermute(far, "tm", [(i, i + 2) for i in range(6)])
    hidden = (reduced[1:17, 1:33].astype(F32) + c2).astype(BF16)
    latent_in = (dot(fold(hidden), down_coarse) + near.astype(F32) + far.astype(F32)).astype(BF16)
    normed = channel_norm(latent_in, gain_latent).astype(BF16)
    other = swapped(normed, "core", 2, 0)
    copies = jnp.broadcast_to(normed[None], (16,) + normed.shape)
    keys = lax.all_to_all(copies, ALL_GATHER, 0, 0, tiled=True).reshape(2048, 512)
    queries = dot(jnp.concatenate([normed, other], 0), w_score).astype(BF16)
    scores = jnp.einsum("qc,kc->qk", queries, keys, preferred_element_type=F32)
    top = jnp.max(scores, -1, keepdims=True)
    expo = jnp.exp(scores - top)
    total = jnp.sum(expo, -1, keepdims=True)
    mixed = dot(expo.astype(BF16), keys) / total
    level = top + jnp.log(total)
    theirs = swapped(mixed[128:].astype(BF16), "core", 2, 0)
    their_level = swapped(jnp.broadcast_to(level[128:], (128, 128)), "core", 2, 0)[:, :1]
    share = jax.nn.sigmoid(level[:128] - their_level)
    attended = (mixed[:128] * share + theirs.astype(F32) * (1.0 - share)).astype(BF16)
    return (latent_in.astype(F32) + dot(attended, w_mix)).astype(BF16).reshape(1, 8, 16, 512)


def solution(mesh):
    split = Mesh(mesh.devices.reshape(8, 2, 2, 8), ("tm", "hx", "core", "width"))
    placed = (P("tm", HEIGHT, "width", None),) + (P(),) * 11
    return jax.shard_map(
        per_device, mesh=split, in_specs=placed,
        out_specs=P("tm", HEIGHT, "width", None), check_vma=False,
    )
```

```python
import functools
import math

import jax
import jax.numpy as jnp
from jax import lax
from jax.experimental import pallas as pl
from jax.experimental.pallas import tpu as pltpu
from jax.sharding import Mesh, PartitionSpec as P

EPSILON = 1e-06
BF16 = jnp.bfloat16
F32 = jnp.float32
HEIGHT = ("hx", "core")
GATHER = ("hx", "width")
VMEM_LIMIT = 48 * 1024 * 1024
VM = pl.BlockSpec(memory_space=pltpu.VMEM)
HB = pl.BlockSpec(memory_space=pl.ANY)
SM = pl.BlockSpec(memory_space=pltpu.SMEM)


def call(kernel, out, ins, scratch=(), flops=0, name=None):
    return pl.pallas_call(
        kernel,
        out_shape=out,
        in_specs=ins,
        out_specs=jax.tree.map(lambda _: VM, out),
        scratch_shapes=list(scratch),
        compiler_params=pltpu.CompilerParams(vmem_limit_bytes=VMEM_LIMIT),
        cost_estimate=pl.CostEstimate(flops=flops, bytes_accessed=4 << 20, transcendentals=0),
        name=name,
    )


def shape(dims, dtype):
    return jax.ShapeDtypeStruct(dims, dtype)


def dot(a, b):
    return jnp.dot(a, b, preferred_element_type=F32)


def scaled(values, gain):
    mean = jnp.mean(values * values, axis=-1, keepdims=True)
    return values * lax.rsqrt(mean + EPSILON) * gain


def silu(values):
    return values * jax.nn.sigmoid(values)


def compose_kernel(own, flag_ref, conv_ref, down_ref, out_ref, acc):
    acc[...] = jnp.zeros_like(acc)
    start = flag_ref[0] == 0
    for i in range(3):
        k0, k1, k2 = (conv_ref[s, i].reshape(384, 128) for s in range(3))
        if own:
            f0, f1, f2 = (k.astype(F32) for k in (k0, k1, k2))
            k2s = jnp.where(start, f0 + f1 + f2, f2).astype(BF16)
            k1s = jnp.where(start, f0 + f1, f1).astype(BF16)
            wide, narrow, wide_at, narrow_at, half = jnp.concatenate([k2s, k1s], -1), k2, 0, 1, 1
        else:
            wide, narrow, wide_at, narrow_at, half = jnp.concatenate([k1, k0], -1), k0, 1, 0, 0
        for r in range(2):
            for c in range(2):
                at = (r * 2 + c) * 128
                halves = [down_ref[f * 512 + at : f * 512 + at + 128, :] for f in range(2)]
                both = dot(wide, jnp.concatenate(halves, 0))
                one = dot(narrow, halves[half])
                for j in range(3):
                    tap = (i + r) * 4 + j + c
                    rows = slice(j * 128, j * 128 + 128)
                    acc[tap, wide_at * 128 : wide_at * 128 + 128, :] += both[rows]
                    acc[tap, narrow_at * 128 : narrow_at * 128 + 128, :] += one[rows]
    out_ref[...] = acc[...].astype(BF16)


def compose(own, tm, conv_fine, down_fine):
    return call(
        functools.partial(compose_kernel, own),
        shape((16, 256, 256), BF16),
        [SM, VM, VM],
        [pltpu.VMEM((16, 256, 256), F32)],
        flops=900_000_000,
        name="compose_own" if own else "compose_next",
    )(tm, conv_fine.reshape(3, 3, 3, 128, 128), down_fine)


COLS = 104
PITCH = 48
FLAT = 624


def fine_kernel(own, x_ref, up_ref, low_ref, left_ref, right_ref, gain_ref, weight_hbm, *rest):
    if own:
        down_ref, out_ref, act, planes, weight, sem, raw, raw_planes = rest
    else:
        out_ref, act, planes, weight, sem, flat = rest
    fetch = pltpu.make_async_copy(weight_hbm, weight, sem)
    fetch.start()
    gain = gain_ref[...].reshape(1, 1, 128)

    def put(values, f, rows, cols):
        values = values.astype(F32)
        act[f, rows, cols, :] = silu(scaled(values, gain))
        if own:
            raw[f, rows, cols, :] = values

    for f in range(2):
        put(up_ref[f], f, pl.ds(0, 3), pl.ds(8, 64))
        put(low_ref[f], f, pl.ds(35, 3), pl.ds(8, 64))
        put(left_ref[f], f, pl.ds(0, 38), pl.ds(4, 4))
        put(right_ref[f], f, pl.ds(0, 38), pl.ds(72, 4))

        def inner(step, carry, f=f):
            put(x_ref[f, pl.ds(step * 4, 4)], f, pl.ds(3 + step * 4, 4), pl.ds(8, 64))
            return carry

        lax.fori_loop(0, 8, inner, 0)

    def build(q, carry):
        for rp in range(2):
            for v in range(4):
                both = [act[f, 2 * q + rp, pl.ds(5 + v, 40, stride=2), :].astype(BF16) for f in range(2)]
                planes[rp, v, q, pl.ds(0, 40), :] = jnp.concatenate(both, -1)
        if own:
            for rp in range(2):
                for v in range(2):
                    both = [raw[f, 2 * q + rp, pl.ds(6 + v, 40, stride=2), :].astype(BF16) for f in range(2)]
                    raw_planes[rp, v, q, pl.ds(0, 40), :] = jnp.concatenate(both, -1)
        return carry

    lax.fori_loop(0, 19, build, 0)
    fetch.wait()
    group = 6
    size = group * PITCH
    for base in range(0, 18, group):
        parts = []
        for u in range(4):
            for v in range(4):
                parts.append(planes[u % 2, v, pl.ds(base + u // 2, group)].reshape(size, 256))
        total = dot(jnp.concatenate(parts, -1), weight[...].reshape(4096, 256))
        if own:
            parts, folds = [], []
            for r in range(2):
                for c in range(2):
                    parts.append(raw_planes[(r + 1) % 2, c, pl.ds(base + (r + 1) // 2, group)].reshape(size, 256))
                    for f in range(2):
                        at = (f * 4 + r * 2 + c) * 128
                        folds.append(down_ref[at : at + 128, :])
            total = total + dot(jnp.concatenate(parts, -1), jnp.concatenate(folds, 0))
            out_ref[base : base + group] = total.reshape(group, PITCH, 256)
        else:
            total = total.reshape(group, PITCH, 256)
            for k in range(group):
                flat[pl.ds((base + k) * 34, 34), :] = total[k, :34]
    if not own:
        flat[pl.ds(612, 12), :] = jnp.zeros((12, 256), F32)
        out_ref[...] = flat[...].astype(BF16)


def fine(own, pieces, gain, weight, down=None):
    scratch = [
        pltpu.VMEM((2, 38, COLS, 128), F32),
        pltpu.VMEM((2, 4, 19, PITCH, 256), BF16),
        pltpu.VMEM((16, 256, 256), BF16),
        pltpu.SemaphoreType.DMA(()),
    ]
    if own:
        scratch += [pltpu.VMEM((2, 38, COLS, 128), F32), pltpu.VMEM((2, 2, 19, PITCH, 256), BF16)]
        out = shape((18, PITCH, 256), F32)
    else:
        scratch += [pltpu.VMEM((FLAT, 256), F32)]
        out = shape((FLAT, 256), BF16)
    return call(
        functools.partial(fine_kernel, own),
        out,
        [VM] * 6 + [HB] + ([VM] if own else []),
        scratch,
        flops=2_000_000_000,
        name="fine_own" if own else "fine_next",
    )(*pieces, gain.reshape(1, 128), weight, *([down] if own else []))


def coarse_kernel(
    flag_ref, own_ref, got_ref, gain_ref, conv_hbm, down_hbm,
    near_ref, far_ref, latent_ref,
    got, reduced, act, shifted, conv, down, sems,
):
    fetch_conv = pltpu.make_async_copy(conv_hbm, conv, sems.at[0])
    fetch_down = pltpu.make_async_copy(down_hbm, down, sems.at[1])
    fetch_conv.start()
    fetch_down.start()
    gain = gain_ref[...]
    got[...] = got_ref[...].astype(F32)

    for row in range(18):
        value = own_ref[row, pl.ds(0, 40), :] + got[pl.ds(row * 34, 40), :]
        value = value.astype(BF16).astype(F32)
        active = silu(scaled(value, gain))
        for half in range(2):
            reduced[half, row, pl.ds(0, 40), :] = value[:, half * 128 : half * 128 + 128]
            act[half, row, pl.ds(0, 40), :] = active[:, half * 128 : half * 128 + 128]

    @pl.when(flag_ref[1] == 0)
    def _():
        act[:, 0] = jnp.zeros((2, PITCH, 128), F32)

    @pl.when(flag_ref[1] == 3)
    def _():
        act[:, 17] = jnp.zeros((2, PITCH, 128), F32)

    @pl.when(flag_ref[2] == 0)
    def _():
        act[:, :, pl.ds(0, 1), :] = jnp.zeros((2, 18, 1, 128), F32)

    @pl.when(flag_ref[2] == 7)
    def _():
        act[:, :, pl.ds(33, 1), :] = jnp.zeros((2, 18, 1, 128), F32)

    def build(row, carry):
        for v in range(4):
            halves = [act[half, row, pl.ds(v, 16, stride=2), :] for half in range(2)]
            shifted[v, row] = jnp.concatenate(halves, -1).astype(BF16)
        return carry

    lax.fori_loop(0, 18, build, 0)
    sides = []
    for p in range(2):
        parts = [shifted[p + j, i : i + 16].reshape(256, 256) for i in range(3) for j in range(3)]
        sides.append(jnp.concatenate(parts, -1))
    lhs = jnp.concatenate(sides, 0)
    fetch_conv.wait()
    start = (flag_ref[0] == 0).astype(F32)
    c0 = dot(lhs, conv[0].reshape(2304, 256))
    c1 = dot(lhs, conv[1].reshape(2304, 256)) + c0 * start
    c2 = dot(lhs, conv[2].reshape(2304, 256)) + c1 * start
    plain = []
    for p in range(2):
        for row in range(16):
            halves = [reduced[half, row + 1, pl.ds(1 + p, 16, stride=2), :] for half in range(2)]
            plain.append(jnp.concatenate(halves, -1))
    c2 = c2 + jnp.concatenate(plain, 0)
    fetch_down.wait()

    def folded(field):
        field = field.astype(BF16).reshape(2, 8, 2, 16, 256)
        parts = [field[p, :, r].reshape(128, 256) for r in range(2) for p in range(2)]
        return jnp.concatenate(parts, -1)

    far_ref[...] = dot(folded(c0), down[...]).astype(BF16)
    near_ref[...] = dot(folded(c1), down[...]).astype(BF16)
    latent_ref[...] = dot(folded(c2), down[...])


def coarse(flags, own, got, gain, conv, down):
    return call(
        coarse_kernel,
        (shape((128, 512), BF16), shape((128, 512), BF16), shape((128, 512), F32)),
        [SM, VM, VM, VM, HB, HB],
        [
            pltpu.VMEM((FLAT, 256), F32),
            pltpu.VMEM((2, 18, PITCH, 128), F32),
            pltpu.VMEM((2, 18, PITCH, 128), F32),
            pltpu.VMEM((4, 18, 16, 256), BF16),
            pltpu.VMEM((3, 9, 256, 256), BF16),
            pltpu.VMEM((1024, 512), BF16),
            pltpu.SemaphoreType.DMA((2,)),
        ],
        flops=2_200_000_000,
        name="coarse",
    )(flags, own, got, gain.reshape(1, 256), conv.reshape(3, 9, 256, 256), down)


def latent_kernel(own_ref, near_ref, far_ref, gain_ref, latent_ref, copies_ref):
    latent = (own_ref[...] + near_ref[...].astype(F32) + far_ref[...].astype(F32)).astype(BF16)
    latent_ref[...] = latent
    normed = scaled(latent.astype(F32), gain_ref[...]).astype(BF16)
    for k in range(copies_ref.shape[0]):
        copies_ref[k] = normed


def attend_kernel(mine_ref, other_ref, keys_ref, score_ref, mixed_ref, level_ref, sent_ref, sent_level_ref):
    tokens = jnp.concatenate([mine_ref[...], other_ref[...]], 0)
    queries = dot(tokens, score_ref[...]).astype(BF16)
    keys = keys_ref[...]
    scores = lax.dot_general(queries, keys, (((1,), (1,)), ((), ())), preferred_element_type=F32)
    top = jnp.max(scores, -1, keepdims=True)
    expo = jnp.exp(scores - top)
    total = jnp.sum(expo, -1, keepdims=True)
    mixed = dot(expo.astype(BF16), keys) / total
    level = top + jnp.log(total)
    mixed_ref[...] = mixed[:128]
    sent_ref[...] = mixed[128:].astype(BF16)
    level = jnp.broadcast_to(level, (256, 128))
    level_ref[...] = level[:128]
    sent_level_ref[...] = level[128:]


def merge_kernel(mixed_ref, level_ref, theirs_ref, their_level_ref, latent_ref, mix_ref, out_ref):
    share = jax.nn.sigmoid(level_ref[...] - their_level_ref[...])[:, :1]
    attended = mixed_ref[...] * share + theirs_ref[...].astype(F32) * (1.0 - share)
    out_ref[...] = (latent_ref[...].astype(F32) + dot(attended.astype(BF16), mix_ref[...])).astype(BF16)


def swapped(value, axis, count, first):
    pairs = []
    for low in range(first, count - 1, 2):
        pairs += [(low, low + 1), (low + 1, low)]
    return lax.ppermute(value, axis, pairs)


def sides(block, axis, dim, width, count):
    odd = lax.axis_index(axis) % 2
    last = block.shape[dim] - width
    inner = lax.dynamic_slice_in_dim(block, (1 - odd) * last, width, axis=dim)
    outer = lax.dynamic_slice_in_dim(block, odd * last, width, axis=dim)
    got_inner = swapped(inner, axis, count, 0)
    got_outer = swapped(outer, axis, count, 1)
    even = odd == 0
    return jnp.where(even, got_outer, got_inner), jnp.where(even, got_inner, got_outer)


def per_device(
    features, gain_fine, conv_fine, down_fine, gain_coarse, conv_coarse, down_coarse,
    gain_latent, w_query, w_key, w_value, w_out,
):
    tm = lax.axis_index("tm").astype(jnp.int32)
    flags = jnp.stack([tm, lax.axis_index(HEIGHT).astype(jnp.int32), lax.axis_index("width").astype(jnp.int32)])
    above, below = sides(features, HEIGHT, 1, 3, 4)
    edge = [lax.slice_in_dim(part, 0, 4, axis=2) for part in (above, features, below)]
    far_edge = [lax.slice_in_dim(part, 60, 64, axis=2) for part in (above, features, below)]
    odd = lax.axis_index("width") % 2 == 1
    first, last = jnp.concatenate(edge, 1), jnp.concatenate(far_edge, 1)
    got_inner = swapped(jnp.where(odd, first, last), "width", 8, 0)
    got_outer = swapped(jnp.where(odd, last, first), "width", 8, 1)
    left, right = jnp.where(odd, got_inner, got_outer), jnp.where(odd, got_outer, got_inner)
    pieces = (features, above, below, left, right)
    weight_next = compose(False, flags, conv_fine, down_fine)
    weight_own = compose(True, flags, conv_fine, down_fine)
    scale = 1.0 / math.sqrt(512)
    w_score = (jnp.einsum("ab,cb->ac", w_query, w_key, preferred_element_type=F32) * scale).astype(BF16)
    w_mix = dot(w_value, w_out).astype(BF16)
    sent = fine(False, pieces, gain_fine, weight_next)
    got = lax.ppermute(sent, "tm", [(i, i + 1) for i in range(7)])
    own = fine(True, pieces, gain_fine, weight_own, down_fine)
    near, far, latent_own = coarse(flags, own, got, gain_coarse, conv_coarse, down_coarse)
    near = lax.ppermute(near, "tm", [(i, i + 1) for i in range(7)])
    far = lax.ppermute(far, "tm", [(i, i + 2) for i in range(6)])
    latent_in, copies = call(
        latent_kernel,
        (shape((128, 512), BF16), shape((16, 128, 512), BF16)),
        [VM] * 4,
        flops=10_000_000,
        name="latent",
    )(latent_own, near, far, gain_latent.reshape(1, 512))
    other = swapped(copies[0], "core", 2, 0)
    keys = lax.all_to_all(copies, GATHER, 0, 0, tiled=True).reshape(2048, 512)
    wide = shape((128, 128), F32)
    mixed, level, theirs, their_level = call(
        attend_kernel,
        (shape((128, 512), F32), wide, shape((128, 512), BF16), wide),
        [VM] * 4,
        flops=1_200_000_000,
        name="attend",
    )(copies[0], other, keys, w_score)
    theirs = swapped(theirs, "core", 2, 0)
    their_level = swapped(their_level, "core", 2, 0)
    out = call(merge_kernel, shape((128, 512), BF16), [VM] * 6, flops=70_000_000, name="merge")(
        mixed, level, theirs, their_level, latent_in, w_mix
    )
    return out.reshape(1, 8, 16, 512)


def solution(mesh):
    split = Mesh(mesh.devices.reshape(8, 2, 2, 8), ("tm", "hx", "core", "width"))
    placed = (P("tm", HEIGHT, "width", None),) + (P(),) * 11
    return jax.shard_map(
        per_device, mesh=split, in_specs=placed,
        out_specs=P("tm", HEIGHT, "width", None), check_vma=False,
    )
```

```python
import functools
import math

import jax
import jax.numpy as jnp
from jax import lax
from jax.experimental import pallas as pl
from jax.experimental.pallas import tpu as pltpu
from jax.sharding import Mesh, PartitionSpec as P

EPSILON = 1e-06
BF16 = jnp.bfloat16
F32 = jnp.float32
HEIGHT = ("hx", "core")
GATHER = "width"
VMEM_LIMIT = 36 * 1024 * 1024
VM = pl.BlockSpec(memory_space=pltpu.VMEM)
HB = pl.BlockSpec(memory_space=pl.ANY)
SM = pl.BlockSpec(memory_space=pltpu.SMEM)


def call(kernel, out, ins, scratch=(), flops=0, name=None):
    return pl.pallas_call(
        kernel,
        out_shape=out,
        in_specs=ins,
        out_specs=jax.tree.map(lambda _: VM, out),
        scratch_shapes=list(scratch),
        compiler_params=pltpu.CompilerParams(vmem_limit_bytes=VMEM_LIMIT),
        cost_estimate=pl.CostEstimate(flops=flops, bytes_accessed=4 << 20, transcendentals=0),
        name=name,
    )


def shape(dims, dtype):
    return jax.ShapeDtypeStruct(dims, dtype)


def dot(a, b):
    return jnp.dot(a, b, preferred_element_type=F32)


def scaled(values, gain):
    mean = jnp.mean(values * values, axis=-1, keepdims=True)
    return values * lax.rsqrt(mean + EPSILON) * gain


def silu(values):
    return values * jax.nn.sigmoid(values)


def compose_kernel(own, flag_ref, conv_ref, down_ref, out_ref, acc):
    acc[...] = jnp.zeros_like(acc)
    start = flag_ref[0] == 0
    for i in range(3):
        k0, k1, k2 = (conv_ref[s, i].reshape(384, 128) for s in range(3))
        if own:
            f0, f1, f2 = (k.astype(F32) for k in (k0, k1, k2))
            k2s = jnp.where(start, f0 + f1 + f2, f2).astype(BF16)
            k1s = jnp.where(start, f0 + f1, f1).astype(BF16)
            wide, narrow, wide_at, narrow_at, half = jnp.concatenate([k2s, k1s], -1), k2, 0, 1, 1
        else:
            wide, narrow, wide_at, narrow_at, half = jnp.concatenate([k1, k0], -1), k0, 1, 0, 0
        for r in range(2):
            for c in range(2):
                at = (r * 2 + c) * 128
                halves = [down_ref[f * 512 + at : f * 512 + at + 128, :] for f in range(2)]
                both = dot(wide, jnp.concatenate(halves, 0))
                one = dot(narrow, halves[half])
                for j in range(3):
                    tap = (i + r) * 4 + j + c
                    rows = slice(j * 128, j * 128 + 128)
                    acc[tap, wide_at * 128 : wide_at * 128 + 128, :] += both[rows]
                    acc[tap, narrow_at * 128 : narrow_at * 128 + 128, :] += one[rows]
    out_ref[...] = acc[...].astype(BF16)


def compose(own, tm, conv_fine, down_fine):
    return call(
        functools.partial(compose_kernel, own),
        shape((16, 256, 256), BF16),
        [SM, VM, VM],
        [pltpu.VMEM((16, 256, 256), F32)],
        flops=900_000_000,
        name="compose_own" if own else "compose_next",
    )(tm, conv_fine.reshape(3, 3, 3, 128, 128), down_fine)


COLS = 104
PITCH = 48
FLAT = 624


def fine_kernel(own, x_ref, up_ref, low_ref, left_ref, right_ref, gain_ref, weight_hbm, *rest):
    if own:
        down_ref, out_ref, act, planes, weight, sem, raw, raw_planes = rest
    else:
        out_ref, act, planes, weight, sem, flat = rest
    fetch = pltpu.make_async_copy(weight_hbm, weight, sem)
    fetch.start()
    gain = gain_ref[...].reshape(1, 1, 128)

    def put(values, f, rows, cols):
        values = values.astype(F32)
        act[f, rows, cols, :] = silu(scaled(values, gain))
        if own:
            raw[f, rows, cols, :] = values

    for f in range(2):
        put(up_ref[f], f, pl.ds(0, 3), pl.ds(8, 64))
        put(low_ref[f], f, pl.ds(35, 3), pl.ds(8, 64))
        put(left_ref[f], f, pl.ds(0, 38), pl.ds(4, 4))
        put(right_ref[f], f, pl.ds(0, 38), pl.ds(72, 4))

        def inner(step, carry, f=f):
            put(x_ref[f, pl.ds(step * 4, 4)], f, pl.ds(3 + step * 4, 4), pl.ds(8, 64))
            return carry

        lax.fori_loop(0, 8, inner, 0)

    def build(q, carry):
        for rp in range(2):
            for v in range(4):
                both = [act[f, 2 * q + rp, pl.ds(5 + v, 40, stride=2), :].astype(BF16) for f in range(2)]
                planes[rp, v, q, pl.ds(0, 40), :] = jnp.concatenate(both, -1)
        if own:
            for rp in range(2):
                for v in range(2):
                    both = [raw[f, 2 * q + rp, pl.ds(6 + v, 40, stride=2), :].astype(BF16) for f in range(2)]
                    raw_planes[rp, v, q, pl.ds(0, 40), :] = jnp.concatenate(both, -1)
        return carry

    lax.fori_loop(0, 19, build, 0)
    fetch.wait()
    group = 6
    size = group * PITCH
    for base in range(0, 18, group):
        parts = []
        for u in range(4):
            for v in range(4):
                parts.append(planes[u % 2, v, pl.ds(base + u // 2, group)].reshape(size, 256))
        total = dot(jnp.concatenate(parts, -1), weight[...].reshape(4096, 256))
        if own:
            parts, folds = [], []
            for r in range(2):
                for c in range(2):
                    parts.append(raw_planes[(r + 1) % 2, c, pl.ds(base + (r + 1) // 2, group)].reshape(size, 256))
                    for f in range(2):
                        at = (f * 4 + r * 2 + c) * 128
                        folds.append(down_ref[at : at + 128, :])
            total = total + dot(jnp.concatenate(parts, -1), jnp.concatenate(folds, 0))
            out_ref[base : base + group] = total.reshape(group, PITCH, 256)
        else:
            total = total.reshape(group, PITCH, 256)
            for k in range(group):
                flat[pl.ds((base + k) * 34, 34), :] = total[k, :34]
    if not own:
        flat[pl.ds(612, 12), :] = jnp.zeros((12, 256), F32)
        out_ref[...] = flat[...].astype(BF16)


def fine(own, pieces, gain, weight, down=None):
    scratch = [
        pltpu.VMEM((2, 38, COLS, 128), F32),
        pltpu.VMEM((2, 4, 19, PITCH, 256), BF16),
        pltpu.VMEM((16, 256, 256), BF16),
        pltpu.SemaphoreType.DMA(()),
    ]
    if own:
        scratch += [pltpu.VMEM((2, 38, COLS, 128), F32), pltpu.VMEM((2, 2, 19, PITCH, 256), BF16)]
        out = shape((18, PITCH, 256), F32)
    else:
        scratch += [pltpu.VMEM((FLAT, 256), F32)]
        out = shape((FLAT, 256), BF16)
    return call(
        functools.partial(fine_kernel, own),
        out,
        [VM] * 6 + [HB] + ([VM] if own else []),
        scratch,
        flops=2_000_000_000,
        name="fine_own" if own else "fine_next",
    )(*pieces, gain.reshape(1, 128), weight, *([down] if own else []))


def coarse_kernel(
    flag_ref, own_ref, got_ref, gain_ref, conv, down,
    near_ref, far_ref, latent_ref,
    got, reduced, act, shifted,
):
    gain = gain_ref[...]
    got[...] = got_ref[...].astype(F32)

    for row in range(18):
        value = own_ref[row, pl.ds(0, 40), :] + got[pl.ds(row * 34, 40), :]
        value = value.astype(BF16).astype(F32)
        active = silu(scaled(value, gain))
        for half in range(2):
            reduced[half, row, pl.ds(0, 40), :] = value[:, half * 128 : half * 128 + 128]
            act[half, row, pl.ds(0, 40), :] = active[:, half * 128 : half * 128 + 128]

    @pl.when(flag_ref[1] == 0)
    def _():
        act[:, 0] = jnp.zeros((2, PITCH, 128), F32)

    @pl.when(flag_ref[1] == 3)
    def _():
        act[:, 17] = jnp.zeros((2, PITCH, 128), F32)

    @pl.when(flag_ref[2] == 0)
    def _():
        act[:, :, pl.ds(0, 1), :] = jnp.zeros((2, 18, 1, 128), F32)

    @pl.when(flag_ref[2] == 7)
    def _():
        act[:, :, pl.ds(33, 1), :] = jnp.zeros((2, 18, 1, 128), F32)

    def build(row, carry):
        for v in range(4):
            halves = [act[half, row, pl.ds(v, 16, stride=2), :] for half in range(2)]
            shifted[v, row] = jnp.concatenate(halves, -1).astype(BF16)
        return carry

    lax.fori_loop(0, 18, build, 0)
    sides = []
    for p in range(2):
        parts = [shifted[p + j, i : i + 16].reshape(256, 256) for i in range(3) for j in range(3)]
        sides.append(jnp.concatenate(parts, -1))
    lhs = jnp.concatenate(sides, 0)
    start = (flag_ref[0] == 0).astype(F32)
    c0 = dot(lhs, conv[0].reshape(2304, 256))
    c1 = dot(lhs, conv[1].reshape(2304, 256)) + c0 * start
    c2 = dot(lhs, conv[2].reshape(2304, 256)) + c1 * start
    plain = []
    for p in range(2):
        for row in range(16):
            halves = [reduced[half, row + 1, pl.ds(1 + p, 16, stride=2), :] for half in range(2)]
            plain.append(jnp.concatenate(halves, -1))
    c2 = c2 + jnp.concatenate(plain, 0)

    def folded(field):
        field = field.astype(BF16).reshape(2, 8, 2, 16, 256)
        parts = [field[p, :, r].reshape(128, 256) for r in range(2) for p in range(2)]
        return jnp.concatenate(parts, -1)

    far_ref[...] = dot(folded(c0), down[...]).astype(BF16)
    near_ref[...] = dot(folded(c1), down[...]).astype(BF16)
    latent_ref[...] = dot(folded(c2), down[...])


def coarse(flags, own, got, gain, conv, down):
    return call(
        coarse_kernel,
        (shape((128, 512), BF16), shape((128, 512), BF16), shape((128, 512), F32)),
        [SM] + [VM] * 5,
        [
            pltpu.VMEM((FLAT, 256), F32),
            pltpu.VMEM((2, 18, PITCH, 128), F32),
            pltpu.VMEM((2, 18, PITCH, 128), F32),
            pltpu.VMEM((4, 18, 16, 256), BF16),
        ],
        flops=2_200_000_000,
        name="coarse",
    )(flags, own, got, gain.reshape(1, 256), conv.reshape(3, 9, 256, 256), down)


def mix_kernel(query_ref, key_ref, value_ref, out_ref, score_ref, mix_ref):
    scores = lax.dot_general(query_ref[...], key_ref[...], (((1,), (1,)), ((), ())), preferred_element_type=F32)
    score_ref[...] = (scores * (1.0 / math.sqrt(512))).astype(BF16)
    mix_ref[...] = dot(value_ref[...], out_ref[...]).astype(BF16)


def latent_kernel(own_ref, near_ref, far_ref, gain_ref, score_ref, latent_ref, query_ref, copies_ref):
    latent = (own_ref[...] + near_ref[...].astype(F32) + far_ref[...].astype(F32)).astype(BF16)
    latent_ref[...] = latent
    normed = scaled(latent.astype(F32), gain_ref[...]).astype(BF16)
    for k in range(copies_ref.shape[0]):
        copies_ref[k] = normed
    query_ref[...] = dot(normed, score_ref[...]).astype(BF16)


def packed(values, level):
    level = jnp.broadcast_to(level, (level.shape[0], 128))
    high = level.astype(BF16)
    rest = level - high.astype(F32)
    middle = rest.astype(BF16)
    low = (rest - middle.astype(F32)).astype(BF16)
    lane = lax.broadcasted_iota(jnp.int32, level.shape, 1)
    parts = jnp.where(lane == 0, high.astype(F32), jnp.where(lane == 1, middle.astype(F32), low.astype(F32)))
    return jnp.concatenate([values.astype(BF16), parts.astype(BF16)], -1)


def level_of(block):
    parts = block[:, 512:].astype(F32)
    lane = lax.broadcasted_iota(jnp.int32, parts.shape, 1)
    return jnp.sum(jnp.where(lane < 3, parts, 0.0), -1, keepdims=True)


def joined(values, level, block):
    other = level_of(block)
    top = jnp.maximum(level, other)
    low = jnp.minimum(level, other)
    share = jax.nn.sigmoid(level - other)
    merged = values * share + block[:, :512].astype(F32) * (1.0 - share)
    return merged, top + jnp.log(1.0 + jnp.exp(low - top))


def attend_kernel(mine_ref, theirs_ref, keys_ref, mixed_ref, level_ref, sent_ref):
    queries = jnp.concatenate([mine_ref[...], theirs_ref[...]], 0)
    keys = keys_ref[...]
    scores = lax.dot_general(queries, keys, (((1,), (1,)), ((), ())), preferred_element_type=F32)
    top = jnp.max(scores, -1, keepdims=True)
    expo = jnp.exp(scores - top)
    total = jnp.sum(expo, -1, keepdims=True)
    mixed = dot(expo.astype(BF16), keys) / total
    level = top + jnp.log(total)
    mixed_ref[...] = mixed[:256]
    level_ref[...] = jnp.broadcast_to(level[:256], (256, 128))
    sent_ref[...] = packed(mixed[256:], level[256:])


def merge_kernel(mixed_ref, level_ref, got_ref, kept_ref, kept_level_ref, sent_ref):
    merged, level = joined(mixed_ref[...], level_ref[:, :1], got_ref[...])
    kept_ref[...] = merged[:128]
    kept_level_ref[...] = jnp.broadcast_to(level[:128], (128, 128))
    sent_ref[...] = packed(merged[128:], level[128:])


def finish_kernel(mixed_ref, level_ref, got_ref, latent_ref, mix_ref, out_ref):
    attended, _ = joined(mixed_ref[...], level_ref[:, :1], got_ref[...])
    out_ref[...] = (latent_ref[...].astype(F32) + dot(attended.astype(BF16), mix_ref[...])).astype(BF16)


def swapped(value, axis, count, first):
    pairs = []
    for low in range(first, count - 1, 2):
        pairs += [(low, low + 1), (low + 1, low)]
    return lax.ppermute(value, axis, pairs)


def sides(block, axis, dim, width, count):
    odd = lax.axis_index(axis) % 2
    last = block.shape[dim] - width
    inner = lax.dynamic_slice_in_dim(block, (1 - odd) * last, width, axis=dim)
    outer = lax.dynamic_slice_in_dim(block, odd * last, width, axis=dim)
    got_inner = swapped(inner, axis, count, 0)
    got_outer = swapped(outer, axis, count, 1)
    even = odd == 0
    return jnp.where(even, got_outer, got_inner), jnp.where(even, got_inner, got_outer)


def per_device(
    features, gain_fine, conv_fine, down_fine, gain_coarse, conv_coarse, down_coarse,
    gain_latent, w_query, w_key, w_value, w_out,
):
    tm = lax.axis_index("tm").astype(jnp.int32)
    flags = jnp.stack([tm, lax.axis_index(HEIGHT).astype(jnp.int32), lax.axis_index("width").astype(jnp.int32)])
    above, below = sides(features, HEIGHT, 1, 3, 4)
    weight_next = compose(False, flags, conv_fine, down_fine)
    above, below, weight_next = lax.optimization_barrier((above, below, weight_next))
    edge = [lax.slice_in_dim(part, 0, 4, axis=2) for part in (above, features, below)]
    far_edge = [lax.slice_in_dim(part, 60, 64, axis=2) for part in (above, features, below)]
    odd = lax.axis_index("width") % 2 == 1
    first, last = jnp.concatenate(edge, 1), jnp.concatenate(far_edge, 1)
    got_inner = swapped(jnp.where(odd, first, last), "width", 8, 0)
    got_outer = swapped(jnp.where(odd, last, first), "width", 8, 1)
    left, right = jnp.where(odd, got_inner, got_outer), jnp.where(odd, got_outer, got_inner)
    pieces = (features, above, below, left, right)
    weight_own = compose(True, flags, conv_fine, down_fine)
    left, right, weight_own = lax.optimization_barrier((left, right, weight_own))
    pieces = (features, above, below, left, right)
    sent = fine(False, pieces, gain_fine, weight_next)
    got = lax.ppermute(sent, "tm", [(i, i + 1) for i in range(7)])
    own = fine(True, pieces, gain_fine, weight_own, down_fine)
    near, far, latent_own = coarse(flags, own, got, gain_coarse, conv_coarse, down_coarse)
    near = lax.ppermute(near, "tm", [(i, i + 1) for i in range(7)])
    far = lax.ppermute(far, "tm", [(i, i + 2) for i in range(6)])
    square = shape((512, 512), BF16)
    w_score, w_mix = call(mix_kernel, (square, square), [VM] * 4, flops=540_000_000, name="mix")(
        w_query, w_key, w_value, w_out
    )
    near, far, w_score, w_mix = lax.optimization_barrier((near, far, w_score, w_mix))
    rows = shape((128, 512), BF16)
    latent_in, query, copies = call(
        latent_kernel, (rows, rows, shape((8, 128, 512), BF16)), [VM] * 5, flops=80_000_000, name="latent"
    )(latent_own, near, far, gain_latent.reshape(1, 512), w_score)
    queries = jnp.concatenate([query, swapped(query, "hx", 2, 0)], 0)
    their_queries = swapped(queries, "core", 2, 0)
    keys = lax.all_to_all(copies, GATHER, 0, 0, tiled=True).reshape(1024, 512)
    mixed, level, sent = call(
        attend_kernel,
        (shape((256, 512), F32), shape((256, 128), F32), shape((256, 640), BF16)),
        [VM] * 3,
        flops=1_100_000_000,
        name="attend",
    )(queries, their_queries, keys)
    got = swapped(sent, "core", 2, 0)
    mixed, level, sent = call(
        merge_kernel,
        (shape((128, 512), F32), shape((128, 128), F32), shape((128, 640), BF16)),
        [VM] * 3,
        flops=1_000_000,
        name="merge",
    )(mixed, level, got)
    got = swapped(sent, "hx", 2, 0)
    out = call(finish_kernel, rows, [VM] * 5, flops=70_000_000, name="finish")(mixed, level, got, latent_in, w_mix)
    return out.reshape(1, 8, 16, 512)


def solution(mesh):
    split = Mesh(mesh.devices.reshape(8, 2, 2, 8), ("tm", "hx", "core", "width"))
    placed = (P("tm", HEIGHT, "width", None),) + (P(),) * 11
    return jax.shard_map(
        per_device, mesh=split, in_specs=placed,
        out_specs=P("tm", HEIGHT, "width", None), check_vma=False,
    )
```

```python
import functools
import math

import jax
import jax.numpy as jnp
from jax import lax
from jax.experimental import pallas as pl
from jax.experimental.pallas import tpu as pltpu
from jax.sharding import Mesh, PartitionSpec as P

EPSILON = 1e-06
BF16 = jnp.bfloat16
F32 = jnp.float32
HEIGHT = ("hx", "core")
GATHER = "width"
VMEM_LIMIT = 32 * 1024 * 1024
VM = pl.BlockSpec(memory_space=pltpu.VMEM)
HB = pl.BlockSpec(memory_space=pltpu.HBM)
SM = pl.BlockSpec(memory_space=pltpu.SMEM)


def call(kernel, out, ins, scratch=(), flops=0, moved=4 << 20, name=None):
    return pl.pallas_call(
        kernel,
        out_shape=out,
        in_specs=ins,
        out_specs=jax.tree.map(lambda _: VM, out),
        scratch_shapes=list(scratch),
        compiler_params=pltpu.CompilerParams(vmem_limit_bytes=VMEM_LIMIT),
        cost_estimate=pl.CostEstimate(flops=flops, bytes_accessed=moved, transcendentals=0),
        name=name,
    )


def kept(value):
    return pltpu.with_memory_space_constraint(value, pltpu.HBM)


def shape(dims, dtype):
    return jax.ShapeDtypeStruct(dims, dtype)


def dot(a, b):
    return jnp.dot(a, b, preferred_element_type=F32)


def scaled(values, gain):
    mean = jnp.mean(values * values, axis=-1, keepdims=True)
    return values * lax.rsqrt(mean + EPSILON) * gain


def silu(values):
    return values * jax.nn.sigmoid(values)


def compose_kernel(own, flag_ref, conv_hbm, down_hbm, out_ref, acc, conv, down, sems):
    taps = 3 if own else 2
    fetch_down = pltpu.make_async_copy(down_hbm, down, sems.at[3])
    fetch_down.start()
    fetches = []
    for i in range(3):
        fetches.append(pltpu.make_async_copy(conv_hbm.at[pl.ds(0, taps), i], conv.at[pl.ds(0, taps), i], sems.at[i]))
        fetches[i].start()
    acc[...] = jnp.zeros_like(acc)
    start = flag_ref[0] == 0
    fetch_down.wait()
    for i in range(3):
        fetches[i].wait()
        k0, k1 = (conv[s, i].reshape(384, 128) for s in range(2))
        if own:
            k2 = conv[2, i].reshape(384, 128)
            f0, f1, f2 = (k.astype(F32) for k in (k0, k1, k2))
            k2s = jnp.where(start, f0 + f1 + f2, f2).astype(BF16)
            k1s = jnp.where(start, f0 + f1, f1).astype(BF16)
            wide, narrow, wide_at, narrow_at, half = jnp.concatenate([k2s, k1s], -1), k2, 0, 1, 1
        else:
            wide, narrow, wide_at, narrow_at, half = jnp.concatenate([k1, k0], -1), k0, 1, 0, 0
        for r in range(2):
            for c in range(2):
                at = (r * 2 + c) * 128
                halves = [down[f * 512 + at : f * 512 + at + 128, :] for f in range(2)]
                both = dot(wide, jnp.concatenate(halves, 0))
                one = dot(narrow, halves[half])
                for j in range(3):
                    tap = (i + r) * 4 + j + c
                    rows = slice(j * 128, j * 128 + 128)
                    acc[tap, wide_at * 128 : wide_at * 128 + 128, :] += both[rows]
                    acc[tap, narrow_at * 128 : narrow_at * 128 + 128, :] += one[rows]
    out_ref[...] = acc[...].astype(BF16)


def compose(own, tm, conv_fine, down_fine):
    return call(
        functools.partial(compose_kernel, own),
        shape((16, 256, 256), BF16),
        [SM, HB, HB],
        [
            pltpu.VMEM((16, 256, 256), F32),
            pltpu.VMEM((3, 3, 3, 128, 128), BF16),
            pltpu.VMEM((1024, 256), BF16),
            pltpu.SemaphoreType.DMA((4,)),
        ],
        flops=900_000_000,
        name="compose_own" if own else "compose_next",
    )(tm, kept(conv_fine.reshape(3, 3, 3, 128, 128)), kept(down_fine))


COLS = 104
PITCH = 48
FLAT = 624


def prepare_kernel(x_hbm, gain_ref, act_ref, first_ref, last_ref, x, sems):
    fetches = []
    for k in range(4):
        rows = pl.ds(k * 8, 8)
        fetches.append(pltpu.make_async_copy(x_hbm.at[:, rows], x.at[:, rows], sems.at[k]))
        fetches[k].start()
    gain = gain_ref[...].reshape(1, 1, 128)
    for k in range(4):
        fetches[k].wait()
        for f in range(2):
            for half in range(2):
                rows = pl.ds(k * 8 + half * 4, 4)
                act_ref[f, rows] = silu(scaled(x[f, rows].astype(F32), gain))
    first_ref[...] = x[:, :, 0:4]
    last_ref[...] = x[:, :, 60:64]


def prepare(features, gain):
    edge = shape((2, 32, 4, 128), BF16)
    return call(
        prepare_kernel,
        (shape((2, 32, 64, 128), F32), edge, edge),
        [HB, VM],
        [pltpu.VMEM((2, 32, 64, 128), BF16), pltpu.SemaphoreType.DMA((4,))],
        flops=10_000_000,
        name="prepare",
    )(kept(features), gain.reshape(1, 128))


def spread(field, up_ref, low_ref, left_ref, right_ref, change):
    for f in range(2):
        field[f, pl.ds(0, 3), pl.ds(8, 64), :] = change(up_ref[f].astype(F32))
        field[f, pl.ds(35, 3), pl.ds(8, 64), :] = change(low_ref[f].astype(F32))
        field[f, :, pl.ds(4, 4), :] = change(left_ref[f].astype(F32))
        field[f, :, pl.ds(72, 4), :] = change(right_ref[f].astype(F32))


GROUP = 6


def next_kernel(act_ref, up_ref, low_ref, left_ref, right_ref, gain_ref, weight_ref, out_ref, planes, act, flat):
    gain = gain_ref[...].reshape(1, 1, 128)
    spread(act, up_ref, low_ref, left_ref, right_ref, lambda values: silu(scaled(values, gain)))
    act[:, pl.ds(3, 32), pl.ds(8, 64), :] = act_ref[...]

    def build(q, carry):
        for rp in range(2):
            for v in range(4):
                both = [act[f, 2 * q + rp, pl.ds(5 + v, 40, stride=2), :].astype(BF16) for f in range(2)]
                planes[rp, v, q, pl.ds(0, 40), :] = jnp.concatenate(both, -1)
        return carry

    lax.fori_loop(0, 19, build, 0)
    for base in range(0, 18, GROUP):
        total = dot(taps_at(planes, base), weight_ref[...].reshape(4096, 256)).reshape(GROUP, PITCH, 256)
        for k in range(GROUP):
            flat[pl.ds((base + k) * 34, 34), :] = total[k, :34]
    flat[pl.ds(612, 12), :] = jnp.zeros((12, 256), F32)
    out_ref[...] = flat[...].astype(BF16)


def taps_at(planes, base):
    parts = []
    for u in range(4):
        for v in range(4):
            parts.append(planes[u % 2, v, pl.ds(base + u // 2, GROUP)].reshape(GROUP * PITCH, 256))
    return jnp.concatenate(parts, -1)


def own_kernel(x_ref, up_ref, low_ref, left_ref, right_ref, weight_ref, planes, down_ref, out_ref, raw, raw_planes):
    spread(raw, up_ref, low_ref, left_ref, right_ref, lambda values: values)
    raw[:, pl.ds(3, 32), pl.ds(8, 64), :] = x_ref[...].astype(F32)

    def build(q, carry):
        for rp in range(2):
            for v in range(2):
                both = [raw[f, 2 * q + rp, pl.ds(6 + v, 40, stride=2), :].astype(BF16) for f in range(2)]
                raw_planes[rp, v, q, pl.ds(0, 40), :] = jnp.concatenate(both, -1)
        return carry

    lax.fori_loop(0, 19, build, 0)
    folds = []
    for r in range(2):
        for c in range(2):
            for f in range(2):
                at = (f * 4 + r * 2 + c) * 128
                folds.append(down_ref[at : at + 128, :])
    fold_weight = jnp.concatenate(folds, 0)
    for base in range(0, 18, GROUP):
        parts = []
        for r in range(2):
            for c in range(2):
                rows = pl.ds(base + (r + 1) // 2, GROUP)
                parts.append(raw_planes[(r + 1) % 2, c, rows].reshape(GROUP * PITCH, 256))
        total = dot(taps_at(planes, base), weight_ref[...].reshape(4096, 256))
        total = total + dot(jnp.concatenate(parts, -1), fold_weight)
        out_ref[base : base + GROUP] = total.reshape(GROUP, PITCH, 256)


def fine_next(act, halos, gain, weight):
    return call(
        next_kernel,
        (shape((FLAT, 256), BF16), shape((2, 4, 19, PITCH, 256), BF16)),
        [VM] * 7,
        [pltpu.VMEM((2, 38, COLS, 128), F32), pltpu.VMEM((FLAT, 256), F32)],
        flops=1_800_000_000,
        name="fine_next",
    )(act, *halos, gain.reshape(1, 128), weight)


def fine_own(features, halos, weight, planes, down):
    return call(
        own_kernel,
        shape((18, PITCH, 256), F32),
        [VM] * 8,
        [pltpu.VMEM((2, 38, COLS, 128), F32), pltpu.VMEM((2, 2, 19, PITCH, 256), BF16)],
        flops=2_200_000_000,
        name="fine_own",
    )(features, *halos, weight, planes, down)


def folded(field):
    field = field.astype(BF16).reshape(2, 8, 2, 16, 256)
    parts = [field[p, :, r].reshape(128, 256) for r in range(2) for p in range(2)]
    return jnp.concatenate(parts, -1)


def windows(shifted):
    sides = []
    for p in range(2):
        parts = [shifted[p + j, i : i + 16].reshape(256, 256) for i in range(3) for j in range(3)]
        sides.append(jnp.concatenate(parts, -1))
    return jnp.concatenate(sides, 0)


def far_kernel(flag_ref, own_ref, got_ref, gain_ref, conv_ref, down_ref, far_ref, c0_ref, shifted, reduced, got, act):
    gain = gain_ref[...]
    got[...] = got_ref[...].astype(F32)
    for row in range(18):
        value = own_ref[row, pl.ds(0, 40), :] + got[pl.ds(row * 34, 40), :]
        value = value.astype(BF16).astype(F32)
        active = silu(scaled(value, gain))
        for half in range(2):
            reduced[half, row, pl.ds(0, 40), :] = value[:, half * 128 : half * 128 + 128]
            act[half, row, pl.ds(0, 40), :] = active[:, half * 128 : half * 128 + 128]

    @pl.when(flag_ref[1] == 0)
    def _():
        act[:, 0] = jnp.zeros((2, PITCH, 128), F32)

    @pl.when(flag_ref[1] == 3)
    def _():
        act[:, 17] = jnp.zeros((2, PITCH, 128), F32)

    @pl.when(flag_ref[2] == 0)
    def _():
        act[:, :, pl.ds(0, 1), :] = jnp.zeros((2, 18, 1, 128), F32)

    @pl.when(flag_ref[2] == 7)
    def _():
        act[:, :, pl.ds(33, 1), :] = jnp.zeros((2, 18, 1, 128), F32)

    def build(row, carry):
        for v in range(4):
            halves = [act[half, row, pl.ds(v, 16, stride=2), :] for half in range(2)]
            shifted[v, row] = jnp.concatenate(halves, -1).astype(BF16)
        return carry

    lax.fori_loop(0, 18, build, 0)
    c0 = dot(windows(shifted), conv_ref[0].reshape(2304, 256))
    c0_ref[...] = c0
    far_ref[...] = dot(folded(c0), down_ref[...]).astype(BF16)


def near_kernel(flag_ref, shifted, c0_ref, conv_ref, down_ref, near_ref, c1_ref):
    start = (flag_ref[0] == 0).astype(F32)
    c1 = dot(windows(shifted), conv_ref[1].reshape(2304, 256)) + c0_ref[...] * start
    c1_ref[...] = c1
    near_ref[...] = dot(folded(c1), down_ref[...]).astype(BF16)


def here_kernel(flag_ref, shifted, reduced, c1_ref, conv_ref, down_ref, latent_ref):
    start = (flag_ref[0] == 0).astype(F32)
    plain = []
    for p in range(2):
        for row in range(16):
            halves = [reduced[half, row + 1, pl.ds(1 + p, 16, stride=2), :] for half in range(2)]
            plain.append(jnp.concatenate(halves, -1))
    c2 = dot(windows(shifted), conv_ref[2].reshape(2304, 256)) + c1_ref[...] * start
    latent_ref[...] = dot(folded(c2 + jnp.concatenate(plain, 0)), down_ref[...])


def coarse(flags, own, got, gain, conv, down):
    conv = conv.reshape(3, 9, 256, 256)
    rows = shape((128, 512), BF16)
    field = shape((512, 256), F32)
    far, c0, shifted, reduced = call(
        far_kernel,
        (rows, field, shape((4, 18, 16, 256), BF16), shape((2, 18, PITCH, 128), F32)),
        [SM] + [VM] * 5,
        [pltpu.VMEM((FLAT, 256), F32), pltpu.VMEM((2, 18, PITCH, 128), F32)],
        flops=800_000_000,
        name="coarse_far",
    )(flags, own, got, gain.reshape(1, 256), conv, down)
    near, c1 = call(near_kernel, (rows, field), [SM] + [VM] * 4, flops=1000, moved=1000, name="coarse_near")(
        flags, shifted, c0, conv, down
    )
    latent = call(here_kernel, shape((128, 512), F32), [SM] + [VM] * 5, flops=1000, moved=1000, name="coarse_here")(
        flags, shifted, reduced, c1, conv, down
    )
    return near, far, latent


def mix_kernel(query_ref, key_ref, value_ref, out_ref, score_ref, mix_ref):
    scores = lax.dot_general(query_ref[...], key_ref[...], (((1,), (1,)), ((), ())), preferred_element_type=F32)
    score_ref[...] = (scores * (1.0 / math.sqrt(512))).astype(BF16)
    mix_ref[...] = dot(value_ref[...], out_ref[...]).astype(BF16)


def latent_kernel(own_ref, near_ref, far_ref, gain_ref, score_ref, latent_ref, query_ref, normed_ref):
    latent = (own_ref[...] + near_ref[...].astype(F32) + far_ref[...].astype(F32)).astype(BF16)
    latent_ref[...] = latent
    normed = scaled(latent.astype(F32), gain_ref[...]).astype(BF16)
    normed_ref[...] = normed
    query_ref[...] = dot(normed, score_ref[...]).astype(BF16)


def copies_kernel(normed_ref, copies_ref):
    for k in range(copies_ref.shape[0]):
        copies_ref[k] = normed_ref[...]


def packed(values, level):
    level = jnp.broadcast_to(level, (level.shape[0], 128))
    high = level.astype(BF16)
    rest = level - high.astype(F32)
    middle = rest.astype(BF16)
    low = (rest - middle.astype(F32)).astype(BF16)
    lane = lax.broadcasted_iota(jnp.int32, level.shape, 1)
    parts = jnp.where(lane == 0, high.astype(F32), jnp.where(lane == 1, middle.astype(F32), low.astype(F32)))
    return jnp.concatenate([values.astype(BF16), parts.astype(BF16)], -1)


def level_of(block):
    parts = block[:, 512:].astype(F32)
    lane = lax.broadcasted_iota(jnp.int32, parts.shape, 1)
    return jnp.sum(jnp.where(lane < 3, parts, 0.0), -1, keepdims=True)


def joined(values, level, block):
    other = level_of(block)
    top = jnp.maximum(level, other)
    low = jnp.minimum(level, other)
    share = jax.nn.sigmoid(level - other)
    merged = values * share + block[:, :512].astype(F32) * (1.0 - share)
    return merged, top + jnp.log(1.0 + jnp.exp(low - top))


def attend_kernel(mine_ref, theirs_ref, keys_ref, mixed_ref, level_ref, sent_ref):
    queries = jnp.concatenate([mine_ref[...], theirs_ref[...]], 0)
    keys = keys_ref[...]
    scores = lax.dot_general(queries, keys, (((1,), (1,)), ((), ())), preferred_element_type=F32)
    top = jnp.max(scores, -1, keepdims=True)
    expo = jnp.exp(scores - top)
    total = jnp.sum(expo, -1, keepdims=True)
    mixed = dot(expo.astype(BF16), keys) / total
    level = top + jnp.log(total)
    mixed_ref[...] = mixed[:256]
    level_ref[...] = jnp.broadcast_to(level[:256], (256, 128))
    sent_ref[...] = packed(mixed[256:], level[256:])


def merge_kernel(mixed_ref, level_ref, got_ref, kept_ref, kept_level_ref, sent_ref):
    merged, level = joined(mixed_ref[...], level_ref[:, :1], got_ref[...])
    kept_ref[...] = merged[:128]
    kept_level_ref[...] = jnp.broadcast_to(level[:128], (128, 128))
    sent_ref[...] = packed(merged[128:], level[128:])


def finish_kernel(mixed_ref, level_ref, got_ref, latent_ref, mix_ref, out_ref):
    attended, _ = joined(mixed_ref[...], level_ref[:, :1], got_ref[...])
    out_ref[...] = (latent_ref[...].astype(F32) + dot(attended.astype(BF16), mix_ref[...])).astype(BF16)


def swapped(value, axis, count, first):
    pairs = []
    for low in range(first, count - 1, 2):
        pairs += [(low, low + 1), (low + 1, low)]
    return lax.ppermute(value, axis, pairs)


def sides(block, axis, dim, width, count):
    odd = lax.axis_index(axis) % 2
    last = block.shape[dim] - width
    inner = lax.dynamic_slice_in_dim(block, (1 - odd) * last, width, axis=dim)
    outer = lax.dynamic_slice_in_dim(block, odd * last, width, axis=dim)
    got_inner = swapped(inner, axis, count, 0)
    got_outer = swapped(outer, axis, count, 1)
    even = odd == 0
    return jnp.where(even, got_outer, got_inner), jnp.where(even, got_inner, got_outer)


def per_device(
    features, gain_fine, conv_fine, down_fine, gain_coarse, conv_coarse, down_coarse,
    gain_latent, w_query, w_key, w_value, w_out,
):
    tm = lax.axis_index("tm").astype(jnp.int32)
    flags = jnp.stack([tm, lax.axis_index(HEIGHT).astype(jnp.int32), lax.axis_index("width").astype(jnp.int32)])
    above, below = sides(features, HEIGHT, 1, 3, 4)
    act, first, last = prepare(features, gain_fine)
    above, below, act, first, last = lax.optimization_barrier((above, below, act, first, last))
    first = jnp.concatenate([above[:, :, :4], first, below[:, :, :4]], 1)
    last = jnp.concatenate([above[:, :, 60:], last, below[:, :, 60:]], 1)
    odd = lax.axis_index("width") % 2 == 1
    got_inner = swapped(jnp.where(odd, first, last), "width", 8, 0)
    got_outer = swapped(jnp.where(odd, last, first), "width", 8, 1)
    weight_next = compose(False, flags, conv_fine, down_fine)
    got_inner, got_outer, weight_next = lax.optimization_barrier((got_inner, got_outer, weight_next))
    left, right = jnp.where(odd, got_inner, got_outer), jnp.where(odd, got_outer, got_inner)
    halos = (above, below, left, right)
    sent, planes = fine_next(act, halos, gain_fine, weight_next)
    got = lax.ppermute(sent, "tm", [(i, i + 1) for i in range(7)])
    weight_own = compose(True, flags, conv_fine, down_fine)
    own = fine_own(features, halos, weight_own, planes, down_fine)
    near, far, latent_own = coarse(flags, own, got, gain_coarse, conv_coarse, down_coarse)
    far = lax.ppermute(far, "tm", [(i, i + 2) for i in range(6)])
    near = lax.ppermute(near, "tm", [(i, i + 1) for i in range(7)])
    square = shape((512, 512), BF16)
    w_score, w_mix = call(mix_kernel, (square, square), [VM] * 4, flops=1000, moved=1000, name="mix")(
        w_query, w_key, w_value, w_out
    )
    near, far, latent_own, w_score, w_mix = lax.optimization_barrier((near, far, latent_own, w_score, w_mix))
    rows = shape((128, 512), BF16)
    latent_in, query, normed = call(
        latent_kernel, (rows, rows, rows), [VM] * 5, flops=80_000_000, name="latent"
    )(latent_own, near, far, gain_latent.reshape(1, 512), w_score)
    copies = call(copies_kernel, shape((8, 128, 512), BF16), [VM], name="copies")(normed)
    queries = jnp.concatenate([query, swapped(query, "hx", 2, 0)], 0)
    their_queries = swapped(queries, "core", 2, 0)
    keys = lax.all_to_all(copies, GATHER, 0, 0, tiled=True).reshape(1024, 512)
    mixed, level, sent = call(
        attend_kernel,
        (shape((256, 512), F32), shape((256, 128), F32), shape((256, 640), BF16)),
        [VM] * 3,
        flops=1_100_000_000,
        name="attend",
    )(queries, their_queries, keys)
    got = swapped(sent, "core", 2, 0)
    mixed, level, sent = call(
        merge_kernel,
        (shape((128, 512), F32), shape((128, 128), F32), shape((128, 640), BF16)),
        [VM] * 3,
        flops=1_000_000,
        name="merge",
    )(mixed, level, got)
    got = swapped(sent, "hx", 2, 0)
    out = call(finish_kernel, rows, [VM] * 5, flops=70_000_000, name="finish")(mixed, level, got, latent_in, w_mix)
    return out.reshape(1, 8, 16, 512)


def solution(mesh):
    split = Mesh(mesh.devices.reshape(8, 2, 2, 8), ("tm", "hx", "core", "width"))
    placed = (P("tm", HEIGHT, "width", None),) + (P(),) * 11
    return jax.shard_map(
        per_device, mesh=split, in_specs=placed,
        out_specs=P("tm", HEIGHT, "width", None), check_vma=False,
    )
```

```python
import functools
import math

import jax
import jax.numpy as jnp
from jax import lax
from jax.experimental import pallas as pl
from jax.experimental.pallas import tpu as pltpu
from jax.sharding import Mesh, PartitionSpec as P

EPSILON = 1e-06
BF16 = jnp.bfloat16
F32 = jnp.float32
HEIGHT = ("hx", "core")
WIDTH = ("y", "lx")
RING = ("hx", "lx")
VMEM_LIMIT = 32 * 1024 * 1024
VM = pl.BlockSpec(memory_space=pltpu.VMEM)
HB = pl.BlockSpec(memory_space=pltpu.HBM)
SM = pl.BlockSpec(memory_space=pltpu.SMEM)


def call(kernel, out, ins, scratch=(), flops=0, moved=4 << 20, name=None):
    return pl.pallas_call(
        kernel,
        out_shape=out,
        in_specs=ins,
        out_specs=jax.tree.map(lambda _: VM, out),
        scratch_shapes=list(scratch),
        compiler_params=pltpu.CompilerParams(vmem_limit_bytes=VMEM_LIMIT),
        cost_estimate=pl.CostEstimate(flops=flops, bytes_accessed=moved, transcendentals=0),
        name=name,
    )


def kept(value):
    return pltpu.with_memory_space_constraint(value, pltpu.HBM)


def shape(dims, dtype):
    return jax.ShapeDtypeStruct(dims, dtype)


def dot(a, b):
    return jnp.dot(a, b, preferred_element_type=F32)


def scaled(values, gain):
    mean = jnp.mean(values * values, axis=-1, keepdims=True)
    return values * lax.rsqrt(mean + EPSILON) * gain


def silu(values):
    return values * jax.nn.sigmoid(values)


def compose_kernel(own, flag_ref, conv_hbm, down_hbm, out_ref, acc, conv, down, sems):
    taps = 3 if own else 2
    fetch_down = pltpu.make_async_copy(down_hbm, down, sems.at[3])
    fetch_down.start()
    fetches = []
    for i in range(3):
        fetches.append(pltpu.make_async_copy(conv_hbm.at[pl.ds(0, taps), i], conv.at[pl.ds(0, taps), i], sems.at[i]))
        fetches[i].start()
    acc[...] = jnp.zeros_like(acc)
    start = flag_ref[0] == 0
    fetch_down.wait()
    for i in range(3):
        fetches[i].wait()
        k0, k1 = (conv[s, i].reshape(384, 128) for s in range(2))
        if own:
            k2 = conv[2, i].reshape(384, 128)
            f0, f1, f2 = (k.astype(F32) for k in (k0, k1, k2))
            k2s = jnp.where(start, f0 + f1 + f2, f2).astype(BF16)
            k1s = jnp.where(start, f0 + f1, f1).astype(BF16)
            wide, narrow, wide_at, narrow_at, half = jnp.concatenate([k2s, k1s], -1), k2, 0, 1, 1
        else:
            wide, narrow, wide_at, narrow_at, half = jnp.concatenate([k1, k0], -1), k0, 1, 0, 0
        for r in range(2):
            for c in range(2):
                at = (r * 2 + c) * 128
                halves = [down[f * 512 + at : f * 512 + at + 128, :] for f in range(2)]
                both = dot(wide, jnp.concatenate(halves, 0))
                one = dot(narrow, halves[half])
                for j in range(3):
                    tap = (i + r) * 4 + j + c
                    rows = slice(j * 128, j * 128 + 128)
                    acc[tap, wide_at * 128 : wide_at * 128 + 128, :] += both[rows]
                    acc[tap, narrow_at * 128 : narrow_at * 128 + 128, :] += one[rows]
    out_ref[...] = acc[...].astype(BF16)


def compose(own, tm, conv_fine, down_fine):
    return call(
        functools.partial(compose_kernel, own),
        shape((16, 256, 256), BF16),
        [SM, HB, HB],
        [
            pltpu.VMEM((16, 256, 256), F32),
            pltpu.VMEM((3, 3, 3, 128, 128), BF16),
            pltpu.VMEM((1024, 256), BF16),
            pltpu.SemaphoreType.DMA((4,)),
        ],
        flops=900_000_000,
        name="compose_own" if own else "compose_next",
    )(tm, kept(conv_fine.reshape(3, 3, 3, 128, 128)), kept(down_fine))


COLS = 104
PITCH = 48
FLAT = 624


def prepare_kernel(x_hbm, gain_hbm, act_ref, first_ref, last_ref, x, gain_ref, sems):
    fetches = []
    for k in range(4):
        rows = pl.ds(k * 8, 8)
        fetches.append(pltpu.make_async_copy(x_hbm.at[:, rows], x.at[:, rows], sems.at[k]))
        fetches[k].start()
    fetch_gain = pltpu.make_async_copy(gain_hbm, gain_ref, sems.at[4])
    fetch_gain.start()
    fetch_gain.wait()
    gain = gain_ref[...].reshape(1, 1, 128)
    for k in range(4):
        fetches[k].wait()
        for f in range(2):
            for half in range(2):
                rows = pl.ds(k * 8 + half * 4, 4)
                act_ref[f, rows] = silu(scaled(x[f, rows].astype(F32), gain))
    first_ref[...] = x[:, :, 0:4]
    last_ref[...] = x[:, :, 60:64]


def prepare(features, gain):
    edge = shape((2, 32, 4, 128), BF16)
    return call(
        prepare_kernel,
        (shape((2, 32, 64, 128), F32), edge, edge),
        [HB, HB],
        [pltpu.VMEM((2, 32, 64, 128), BF16), pltpu.VMEM((1, 128), F32), pltpu.SemaphoreType.DMA((5,))],
        flops=10_000_000,
        name="prepare",
    )(kept(features), kept(gain.reshape(1, 128)))


def spread(field, up_ref, low_ref, left_ref, right_ref, change):
    for f in range(2):
        field[f, pl.ds(0, 3), pl.ds(8, 64), :] = change(up_ref[f].astype(F32))
        field[f, pl.ds(35, 3), pl.ds(8, 64), :] = change(low_ref[f].astype(F32))
        field[f, :, pl.ds(4, 4), :] = change(left_ref[f].astype(F32))
        field[f, :, pl.ds(72, 4), :] = change(right_ref[f].astype(F32))


GROUP = 6


def next_kernel(act_ref, up_ref, low_ref, left_ref, right_ref, gain_ref, weight_ref, out_ref, planes, act, flat):
    gain = gain_ref[...].reshape(1, 1, 128)
    spread(act, up_ref, low_ref, left_ref, right_ref, lambda values: silu(scaled(values, gain)))
    act[:, pl.ds(3, 32), pl.ds(8, 64), :] = act_ref[...]

    def build(q, carry):
        for rp in range(2):
            for v in range(4):
                both = [act[f, 2 * q + rp, pl.ds(5 + v, 40, stride=2), :].astype(BF16) for f in range(2)]
                planes[rp, v, q, pl.ds(0, 40), :] = jnp.concatenate(both, -1)
        return carry

    lax.fori_loop(0, 19, build, 0)
    for base in range(0, 18, GROUP):
        total = dot(taps_at(planes, base), weight_ref[...].reshape(4096, 256)).reshape(GROUP, PITCH, 256)
        for k in range(GROUP):
            flat[pl.ds((base + k) * 34, 34), :] = total[k, :34]
    flat[pl.ds(612, 12), :] = jnp.zeros((12, 256), F32)
    out_ref[...] = flat[...].astype(BF16)


def taps_at(planes, base):
    parts = []
    for u in range(4):
        for v in range(4):
            parts.append(planes[u % 2, v, pl.ds(base + u // 2, GROUP)].reshape(GROUP * PITCH, 256))
    return jnp.concatenate(parts, -1)


def own_kernel(x_ref, up_ref, low_ref, left_ref, right_ref, weight_ref, planes, down_ref, out_ref, raw, raw_planes):
    spread(raw, up_ref, low_ref, left_ref, right_ref, lambda values: values)
    raw[:, pl.ds(3, 32), pl.ds(8, 64), :] = x_ref[...].astype(F32)

    def build(q, carry):
        for rp in range(2):
            for v in range(2):
                both = [raw[f, 2 * q + rp, pl.ds(6 + v, 40, stride=2), :].astype(BF16) for f in range(2)]
                raw_planes[rp, v, q, pl.ds(0, 40), :] = jnp.concatenate(both, -1)
        return carry

    lax.fori_loop(0, 19, build, 0)
    folds = []
    for r in range(2):
        for c in range(2):
            for f in range(2):
                at = (f * 4 + r * 2 + c) * 128
                folds.append(down_ref[at : at + 128, :])
    fold_weight = jnp.concatenate(folds, 0)
    for base in range(0, 18, GROUP):
        parts = []
        for r in range(2):
            for c in range(2):
                rows = pl.ds(base + (r + 1) // 2, GROUP)
                parts.append(raw_planes[(r + 1) % 2, c, rows].reshape(GROUP * PITCH, 256))
        total = dot(taps_at(planes, base), weight_ref[...].reshape(4096, 256))
        total = total + dot(jnp.concatenate(parts, -1), fold_weight)
        out_ref[base : base + GROUP] = total.reshape(GROUP, PITCH, 256)


def fine_next(act, halos, gain, weight):
    return call(
        next_kernel,
        (shape((FLAT, 256), BF16), shape((2, 4, 19, PITCH, 256), BF16)),
        [VM] * 7,
        [pltpu.VMEM((2, 38, COLS, 128), F32), pltpu.VMEM((FLAT, 256), F32)],
        flops=1_800_000_000,
        name="fine_next",
    )(act, *halos, gain.reshape(1, 128), weight)


def fine_own(features, halos, weight, planes, down):
    return call(
        own_kernel,
        shape((18, PITCH, 256), F32),
        [VM] * 8,
        [pltpu.VMEM((2, 38, COLS, 128), F32), pltpu.VMEM((2, 2, 19, PITCH, 256), BF16)],
        flops=2_200_000_000,
        name="fine_own",
    )(features, *halos, weight, planes, down)


def folded(field):
    field = field.astype(BF16).reshape(2, 8, 2, 16, 256)
    parts = [field[p, :, r].reshape(128, 256) for r in range(2) for p in range(2)]
    return jnp.concatenate(parts, -1)


def sent_kernel(
    flag_ref, own_ref, got_ref, gain_ref, conv_ref, down_ref, far_ref, near_ref, c1_ref, windows, reduced, got, act
):
    gain = gain_ref[...]
    got[...] = got_ref[...].astype(F32)
    for row in range(18):
        value = own_ref[row, pl.ds(0, 40), :] + got[pl.ds(row * 34, 40), :]
        value = value.astype(BF16).astype(F32)
        active = silu(scaled(value, gain))
        for half in range(2):
            reduced[half, row, pl.ds(0, 40), :] = value[:, half * 128 : half * 128 + 128]
            act[half, row, pl.ds(0, 40), :] = active[:, half * 128 : half * 128 + 128]

    @pl.when(flag_ref[1] == 0)
    def _():
        act[:, 0] = jnp.zeros((2, PITCH, 128), F32)

    @pl.when(flag_ref[1] == 3)
    def _():
        act[:, 17] = jnp.zeros((2, PITCH, 128), F32)

    @pl.when(flag_ref[2] == 0)
    def _():
        act[:, :, pl.ds(0, 1), :] = jnp.zeros((2, 18, 1, 128), F32)

    @pl.when(flag_ref[2] == 7)
    def _():
        act[:, :, pl.ds(33, 1), :] = jnp.zeros((2, 18, 1, 128), F32)

    for row in range(18):
        for v in range(4):
            halves = [act[half, row, pl.ds(v, 16, stride=2), :] for half in range(2)]
            cells = jnp.concatenate(halves, -1).astype(BF16)
            for p in range(2):
                for i in range(3):
                    if 0 <= v - p < 3 and 0 <= row - i < 16:
                        tap = i * 3 + v - p
                        windows[pl.ds((p * 16 + row - i) * 16, 16), pl.ds(tap * 256, 256)] = cells
    start = (flag_ref[0] == 0).astype(F32)
    lhs = windows[...]
    c0 = dot(lhs, conv_ref[0].reshape(2304, 256))
    c1 = dot(lhs, conv_ref[1].reshape(2304, 256)) + c0 * start
    c1_ref[...] = c1
    both = dot(jnp.concatenate([folded(c0), folded(c1)], 0), down_ref[...]).astype(BF16)
    far_ref[...] = both[:128]
    near_ref[...] = both[128:]


def here_kernel(flag_ref, windows, reduced, c1_ref, conv_ref, down_ref, latent_ref):
    start = (flag_ref[0] == 0).astype(F32)
    plain = []
    for p in range(2):
        for row in range(16):
            halves = [reduced[half, row + 1, pl.ds(1 + p, 16, stride=2), :] for half in range(2)]
            plain.append(jnp.concatenate(halves, -1))
    c2 = dot(windows[...], conv_ref[2].reshape(2304, 256)) + c1_ref[...] * start
    latent_ref[...] = dot(folded(c2 + jnp.concatenate(plain, 0)), down_ref[...])


def coarse(flags, own, got, gain, conv, down):
    conv = conv.reshape(3, 9, 256, 256)
    rows = shape((128, 512), BF16)
    field = shape((512, 256), F32)
    far, near, c1, windows, reduced = call(
        sent_kernel,
        (rows, rows, field, shape((512, 2304), BF16), shape((2, 18, PITCH, 128), F32)),
        [SM] + [VM] * 5,
        [pltpu.VMEM((FLAT, 256), F32), pltpu.VMEM((2, 18, PITCH, 128), F32)],
        flops=1_500_000_000,
        name="coarse_sent",
    )(flags, own, got, gain.reshape(1, 256), conv, down)
    latent = call(here_kernel, shape((128, 512), F32), [SM] + [VM] * 5, flops=1000, moved=1000, name="coarse_here")(
        flags, windows, reduced, c1, conv, down
    )
    return near, far, latent


def mix_kernel(query_ref, key_ref, value_ref, out_ref, score_ref, mix_ref):
    scores = lax.dot_general(query_ref[...], key_ref[...], (((1,), (1,)), ((), ())), preferred_element_type=F32)
    score_ref[...] = (scores * (1.0 / math.sqrt(512))).astype(BF16)
    mix_ref[...] = dot(value_ref[...], out_ref[...]).astype(BF16)


def latent_kernel(own_ref, near_ref, far_ref, gain_ref, score_ref, latent_ref, query_ref, copies_ref):
    latent = (own_ref[...] + near_ref[...].astype(F32) + far_ref[...].astype(F32)).astype(BF16)
    latent_ref[...] = latent
    normed = scaled(latent.astype(F32), gain_ref[...]).astype(BF16)
    for k in range(copies_ref.shape[0]):
        copies_ref[k] = normed
    query_ref[...] = dot(normed, score_ref[...]).astype(BF16)


def packed(values, level):
    across = jnp.broadcast_to(level, (128, 128)).T[:16]
    high = across.astype(BF16).astype(F32)
    middle = (across - high).astype(BF16).astype(F32)
    low = across - high - middle
    row = lax.broadcasted_iota(jnp.int32, (16, 128), 0)
    parts = jnp.where(row == 0, high, jnp.where(row == 1, middle, jnp.where(row == 2, low, 0.0)))
    last = jnp.concatenate([parts, jnp.zeros((16, 384), F32)], -1)
    return jnp.concatenate([values, last], 0).astype(BF16)


def level_of(block):
    across = jnp.sum(block[128:, :128].astype(F32), 0, keepdims=True)
    return jnp.broadcast_to(across, (128, 128)).T[:, :1]


def softmax_part(queries, keys):
    scores = lax.dot_general(queries, keys, (((1,), (1,)), ((), ())), preferred_element_type=F32)
    top = jnp.max(scores, -1, keepdims=True)
    expo = jnp.exp(scores - top)
    total = jnp.sum(expo, -1, keepdims=True)
    return dot(expo.astype(BF16), keys) / total, top + jnp.log(total)


def attend_theirs_kernel(q1_ref, q2_ref, q3_ref, keys_ref, other_keys_ref, *sent):
    queries = jnp.concatenate([q1_ref[...], q2_ref[...], q3_ref[...]], 0)
    keys = jnp.concatenate([keys_ref[...], other_keys_ref[...]], 0)
    mixed, level = softmax_part(queries, keys)
    for k in range(3):
        rows = slice(128 * k, 128 * (k + 1))
        sent[k][...] = packed(mixed[rows], level[rows])


def attend_mine_kernel(queries_ref, keys_ref, other_keys_ref, mixed_ref, level_ref):
    keys = jnp.concatenate([keys_ref[...], other_keys_ref[...]], 0)
    mixed, level = softmax_part(queries_ref[...], keys)
    mixed_ref[...] = mixed
    level_ref[...] = jnp.broadcast_to(level, (128, 128))


def finish_kernel(mixed_ref, level_ref, got1_ref, got2_ref, got3_ref, latent_ref, mix_ref, out_ref):
    blocks = [ref[...] for ref in (got1_ref, got2_ref, got3_ref)]
    levels = [level_ref[:, :1]] + [level_of(block) for block in blocks]
    values = [mixed_ref[...]] + [block[:128].astype(F32) for block in blocks]
    top = functools.reduce(jnp.maximum, levels)
    shares = [jnp.exp(level - top) for level in levels]
    summed = sum(value * share for value, share in zip(values, shares))
    attended = summed / sum(shares)
    out_ref[...] = (latent_ref[...].astype(F32) + dot(attended.astype(BF16), mix_ref[...])).astype(BF16)


def swapped(value, axis, count, first):
    pairs = []
    for low in range(first, count - 1, 2):
        pairs += [(low, low + 1), (low + 1, low)]
    return lax.ppermute(value, axis, pairs)


def turned(value, step):
    return lax.ppermute(value, RING, [(i, (i + step) % 4) for i in range(4)])


def sides(block, axis, dim, width, count):
    odd = lax.axis_index(axis) % 2
    last = block.shape[dim] - width
    inner = lax.dynamic_slice_in_dim(block, (1 - odd) * last, width, axis=dim)
    outer = lax.dynamic_slice_in_dim(block, odd * last, width, axis=dim)
    got_inner = swapped(inner, axis, count, 0)
    got_outer = swapped(outer, axis, count, 1)
    even = odd == 0
    return jnp.where(even, got_outer, got_inner), jnp.where(even, got_inner, got_outer)


def per_device(
    features, gain_fine, conv_fine, down_fine, gain_coarse, conv_coarse, down_coarse,
    gain_latent, w_query, w_key, w_value, w_out,
):
    rows = shape((128, 512), BF16)
    tm = lax.axis_index("tm").astype(jnp.int32)
    flags = jnp.stack([tm, lax.axis_index(HEIGHT).astype(jnp.int32), lax.axis_index(WIDTH).astype(jnp.int32)])
    above, below = sides(features, HEIGHT, 1, 3, 4)
    act, first, last = prepare(features, gain_fine)
    above, below, act, first, last = lax.optimization_barrier((above, below, act, first, last))
    first = jnp.concatenate([above[:, :, :4], first, below[:, :, :4]], 1)
    last = jnp.concatenate([above[:, :, 60:], last, below[:, :, 60:]], 1)
    odd = lax.axis_index(WIDTH) % 2 == 1
    got_inner = swapped(jnp.where(odd, first, last), WIDTH, 8, 0)
    got_outer = swapped(jnp.where(odd, last, first), WIDTH, 8, 1)
    weight_next = compose(False, flags, conv_fine, down_fine)
    got_inner, got_outer, weight_next = lax.optimization_barrier((got_inner, got_outer, weight_next))
    left, right = jnp.where(odd, got_inner, got_outer), jnp.where(odd, got_outer, got_inner)
    halos = (above, below, left, right)
    sent, planes = fine_next(act, halos, gain_fine, weight_next)
    got = lax.ppermute(sent, "tm", [(i, i + 1) for i in range(7)])
    weight_own = compose(True, flags, conv_fine, down_fine)
    own = fine_own(features, halos, weight_own, planes, down_fine)
    square = shape((512, 512), BF16)
    w_score, w_mix = call(mix_kernel, (square, square), [VM] * 4, flops=1000, moved=1000, name="mix")(
        w_query, w_key, w_value, w_out
    )
    got, own, w_score, w_mix = lax.optimization_barrier((got, own, w_score, w_mix))
    near, far, latent_own = coarse(flags, own, got, gain_coarse, conv_coarse, down_coarse)
    far = lax.ppermute(far, "tm", [(i, i + 2) for i in range(6)])
    near = lax.ppermute(near, "tm", [(i, i + 1) for i in range(7)])
    near, far, latent_own = lax.optimization_barrier((near, far, latent_own))
    latent_in, query, copies = call(
        latent_kernel, (rows, rows, shape((4, 128, 512), BF16)), [VM] * 5, flops=80_000_000, name="latent"
    )(latent_own, near, far, gain_latent.reshape(1, 512), w_score)
    keys = lax.all_to_all(copies, "y", 0, 0, tiled=True).reshape(512, 512)
    asked = [turned(query, step) for step in (1, 2, 3)]
    keys, *asked = lax.optimization_barrier((keys, *asked))
    other_keys = swapped(keys, "core", 2, 0)
    sent = call(
        attend_theirs_kernel, (shape((144, 512), BF16),) * 3, [VM] * 5, flops=800_000_000, name="attend_theirs"
    )(*asked, keys, other_keys)
    mixed, level = call(
        attend_mine_kernel,
        (shape((128, 512), F32), shape((128, 128), F32)),
        [VM] * 3,
        flops=300_000_000,
        name="attend_mine",
    )(query, keys, other_keys)
    got = [turned(block, -step) for step, block in zip((1, 2, 3), sent)]
    out = call(finish_kernel, rows, [VM] * 7, flops=70_000_000, name="finish")(mixed, level, *got, latent_in, w_mix)
    return out.reshape(1, 8, 16, 512)


def solution(mesh):
    split = Mesh(mesh.devices.reshape(8, 2, 2, 4, 2), ("tm", "hx", "core", "y", "lx"))
    placed = (P("tm", HEIGHT, WIDTH, None),) + (P(),) * 11
    return jax.shard_map(
        per_device, mesh=split, in_specs=placed,
        out_specs=P("tm", HEIGHT, WIDTH, None), check_vma=False,
    )
```

```python
import functools
import math

import jax
import jax.numpy as jnp
from jax import lax
from jax.experimental import pallas as pl
from jax.experimental.pallas import tpu as pltpu
from jax.sharding import Mesh, PartitionSpec as P

EPSILON = 1e-06
BF16 = jnp.bfloat16
F32 = jnp.float32
HEIGHT = ("hx", "core")
WIDTH = ("y", "lx")
RING = ("hx", "lx")
VMEM_LIMIT = 32 * 1024 * 1024
VM = pl.BlockSpec(memory_space=pltpu.VMEM)
HB = pl.BlockSpec(memory_space=pltpu.HBM)
SM = pl.BlockSpec(memory_space=pltpu.SMEM)


def call(kernel, out, ins, scratch=(), flops=0, moved=4 << 20, name=None):
    return pl.pallas_call(
        kernel,
        out_shape=out,
        in_specs=ins,
        out_specs=jax.tree.map(lambda _: VM, out),
        scratch_shapes=list(scratch),
        compiler_params=pltpu.CompilerParams(vmem_limit_bytes=VMEM_LIMIT),
        cost_estimate=pl.CostEstimate(flops=flops, bytes_accessed=moved, transcendentals=0),
        name=name,
    )


def kept(value):
    return pltpu.with_memory_space_constraint(value, pltpu.HBM)


def shape(dims, dtype):
    return jax.ShapeDtypeStruct(dims, dtype)


def dot(a, b):
    return jnp.dot(a, b, preferred_element_type=F32)


def scaled(values, gain):
    mean = jnp.mean(values * values, axis=-1, keepdims=True)
    return values * lax.rsqrt(mean + EPSILON) * gain


def silu(values):
    return values * jax.nn.sigmoid(values)


def compose_kernel(own, flag_ref, conv, down, out_ref, acc):
    acc[...] = jnp.zeros_like(acc)
    start = flag_ref[0] == 0
    for i in range(3):
        k0, k1 = (conv[s, i].reshape(384, 128) for s in range(2))
        if own:
            k2 = conv[2, i].reshape(384, 128)
            f0, f1, f2 = (k.astype(F32) for k in (k0, k1, k2))
            k2s = jnp.where(start, f0 + f1 + f2, f2).astype(BF16)
            k1s = jnp.where(start, f0 + f1, f1).astype(BF16)
            wide, narrow, wide_at, narrow_at, half = jnp.concatenate([k2s, k1s], -1), k2, 0, 1, 1
        else:
            wide, narrow, wide_at, narrow_at, half = jnp.concatenate([k1, k0], -1), k0, 1, 0, 0
        for r in range(2):
            for c in range(2):
                at = (r * 2 + c) * 128
                halves = [down[f * 512 + at : f * 512 + at + 128, :] for f in range(2)]
                both = dot(wide, jnp.concatenate(halves, 0))
                one = dot(narrow, halves[half])
                for j in range(3):
                    tap = (i + r) * 4 + j + c
                    rows = slice(j * 128, j * 128 + 128)
                    acc[tap, wide_at * 128 : wide_at * 128 + 128, :] += both[rows]
                    acc[tap, narrow_at * 128 : narrow_at * 128 + 128, :] += one[rows]
    out_ref[...] = acc[...].astype(BF16)


def compose(own, tm, conv_fine, down_fine):
    return call(
        functools.partial(compose_kernel, own),
        shape((16, 256, 256), BF16),
        [SM, VM, VM],
        [pltpu.VMEM((16, 256, 256), F32)],
        flops=900_000_000,
        name="compose_own" if own else "compose_next",
    )(tm, conv_fine, down_fine)


COLS = 104
PITCH = 48
FLAT = 624


def edges_kernel(odd_ref, x_hbm, inner_ref, outer_ref, sems):
    odd = odd_ref[0]
    inner = pltpu.make_async_copy(x_hbm.at[:, pl.ds((1 - odd) * 29, 3)], inner_ref, sems.at[0])
    outer = pltpu.make_async_copy(x_hbm.at[:, pl.ds(odd * 29, 3)], outer_ref, sems.at[1])
    inner.start()
    outer.start()
    inner.wait()
    outer.wait()


def prepare_kernel(
    x_hbm, gain_hbm, conv_hbm, down_hbm, act_ref, first_ref, last_ref, conv_ref, down_ref, x, gain_ref, sems
):
    fetches = []
    for k in range(4):
        rows = pl.ds(k * 8, 8)
        fetches.append(pltpu.make_async_copy(x_hbm.at[:, rows], x.at[:, rows], sems.at[k]))
        fetches[k].start()
    fetch_gain = pltpu.make_async_copy(gain_hbm, gain_ref, sems.at[4])
    fetch_gain.start()
    weights = [pltpu.make_async_copy(conv_hbm, conv_ref, sems.at[5]), pltpu.make_async_copy(down_hbm, down_ref, sems.at[6])]
    for fetch in weights:
        fetch.start()
    fetch_gain.wait()
    gain = gain_ref[...].reshape(1, 1, 128)
    for k in range(4):
        fetches[k].wait()
        for f in range(2):
            for half in range(2):
                rows = pl.ds(k * 8 + half * 4, 4)
                act_ref[f, rows] = silu(scaled(x[f, rows].astype(F32), gain))
    first_ref[...] = x[:, :, 0:4]
    last_ref[...] = x[:, :, 60:64]
    for fetch in weights:
        fetch.wait()


def prepare(features, gain, conv, down):
    edge = shape((2, 32, 4, 128), BF16)
    return call(
        prepare_kernel,
        (shape((2, 32, 64, 128), F32), edge, edge, shape((3, 3, 3, 128, 128), BF16), shape((1024, 256), BF16)),
        [HB] * 4,
        [pltpu.VMEM((2, 32, 64, 128), BF16), pltpu.VMEM((1, 128), F32), pltpu.SemaphoreType.DMA((7,))],
        flops=10_000_000,
        name="prepare",
    )(kept(features), kept(gain.reshape(1, 128)), kept(conv.reshape(3, 3, 3, 128, 128)), kept(down))


def spread(field, up_ref, low_ref, left_ref, right_ref, change):
    for f in range(2):
        field[f, pl.ds(0, 3), pl.ds(8, 64), :] = change(up_ref[f].astype(F32))
        field[f, pl.ds(35, 3), pl.ds(8, 64), :] = change(low_ref[f].astype(F32))
        field[f, :, pl.ds(4, 4), :] = change(left_ref[f].astype(F32))
        field[f, :, pl.ds(72, 4), :] = change(right_ref[f].astype(F32))


GROUP = 6


def next_kernel(act_ref, up_ref, low_ref, left_ref, right_ref, gain_ref, weight_ref, out_ref, planes, act, flat):
    gain = gain_ref[...].reshape(1, 1, 128)
    spread(act, up_ref, low_ref, left_ref, right_ref, lambda values: silu(scaled(values, gain)))
    act[:, pl.ds(3, 32), pl.ds(8, 64), :] = act_ref[...]

    def build(q):
        for rp in range(2):
            for v in range(4):
                both = [act[f, 2 * q + rp, pl.ds(5 + v, 40, stride=2), :].astype(BF16) for f in range(2)]
                planes[rp, v, q, pl.ds(0, 40), :] = jnp.concatenate(both, -1)

    built = 0
    for base in range(0, 18, GROUP):
        while built < base + GROUP + 1:
            build(built)
            built += 1
        total = dot(taps_at(planes, base), weight_ref[...].reshape(4096, 256)).reshape(GROUP, PITCH, 256)
        for k in range(GROUP):
            flat[pl.ds((base + k) * 34, 34), :] = total[k, :34]
    flat[pl.ds(612, 12), :] = jnp.zeros((12, 256), F32)
    out_ref[...] = flat[...].astype(BF16)


def taps_at(planes, base):
    parts = []
    for u in range(4):
        for v in range(4):
            parts.append(planes[u % 2, v, pl.ds(base + u // 2, GROUP)].reshape(GROUP * PITCH, 256))
    return jnp.concatenate(parts, -1)


def own_kernel(x_ref, up_ref, low_ref, left_ref, right_ref, weight_ref, planes, down_ref, out_ref, raw, raw_planes):
    spread(raw, up_ref, low_ref, left_ref, right_ref, lambda values: values)
    raw[:, pl.ds(3, 32), pl.ds(8, 64), :] = x_ref[...].astype(F32)

    def build(q):
        for rp in range(2):
            for v in range(2):
                both = [raw[f, 2 * q + rp, pl.ds(6 + v, 40, stride=2), :].astype(BF16) for f in range(2)]
                raw_planes[rp, v, q, pl.ds(0, 40), :] = jnp.concatenate(both, -1)

    folds = []
    for r in range(2):
        for c in range(2):
            for f in range(2):
                at = (f * 4 + r * 2 + c) * 128
                folds.append(down_ref[at : at + 128, :])
    fold_weight = jnp.concatenate(folds, 0)
    built = 0
    for base in range(0, 18, GROUP):
        while built < base + GROUP + 1:
            build(built)
            built += 1
        parts = []
        for r in range(2):
            for c in range(2):
                rows = pl.ds(base + (r + 1) // 2, GROUP)
                parts.append(raw_planes[(r + 1) % 2, c, rows].reshape(GROUP * PITCH, 256))
        total = dot(taps_at(planes, base), weight_ref[...].reshape(4096, 256))
        total = total + dot(jnp.concatenate(parts, -1), fold_weight)
        out_ref[base : base + GROUP] = total.reshape(GROUP, PITCH, 256)


def fine_next(act, halos, gain, weight):
    return call(
        next_kernel,
        (shape((FLAT, 256), BF16), shape((2, 4, 19, PITCH, 256), BF16)),
        [VM] * 7,
        [pltpu.VMEM((2, 38, COLS, 128), F32), pltpu.VMEM((FLAT, 256), F32)],
        flops=1_800_000_000,
        name="fine_next",
    )(act, *halos, gain.reshape(1, 128), weight)


def fine_own(features, halos, weight, planes, down):
    return call(
        own_kernel,
        shape((18, PITCH, 256), F32),
        [VM] * 8,
        [pltpu.VMEM((2, 38, COLS, 128), F32), pltpu.VMEM((2, 2, 19, PITCH, 256), BF16)],
        flops=2_200_000_000,
        name="fine_own",
    )(features, *halos, weight, planes, down)


def folded(field):
    field = field.astype(BF16).reshape(2, 2, 4, 2, 16, 256)
    parts = [field[:, p, :, r].reshape(128, 256) for r in range(2) for p in range(2)]
    return jnp.concatenate(parts, -1)


def sent_kernel(
    flag_ref, own_ref, got_ref, gain_ref, conv_ref, down_ref, far_ref, near_ref, c1_ref, windows, reduced, got, act
):
    gain = gain_ref[...]
    got[...] = got_ref[...].astype(F32)
    start = (flag_ref[0] == 0).astype(F32)
    col = lax.broadcasted_iota(jnp.int32, (40, 128), 0)
    inside = ((col > 0) | (flag_ref[2] > 0)) & ((col < 33) | (flag_ref[2] < 7))
    inside = inside.astype(F32)
    ends = {0: (flag_ref[1] > 0).astype(F32), 17: (flag_ref[1] < 3).astype(F32)}
    fields = []
    done = 0
    for part in range(2):
        for row in range(done, 10 + 8 * part):
            value = own_ref[row, pl.ds(0, 40), :] + got[pl.ds(row * 34, 40), :]
            value = value.astype(BF16).astype(F32)
            active = silu(scaled(value, gain))
            keep = inside * ends[row] if row in ends else inside
            for half in range(2):
                reduced[half, row, pl.ds(0, 40), :] = value[:, half * 128 : half * 128 + 128]
                act[half, row, pl.ds(0, 40), :] = active[:, half * 128 : half * 128 + 128] * keep
        done = 10 + 8 * part
        for row in range(8 * part, 8 * part + 10):
            for v in range(4):
                halves = [act[half, row, pl.ds(v, 16, stride=2), :] for half in range(2)]
                cells = jnp.concatenate(halves, -1).astype(BF16)
                for p in range(2):
                    for i in range(3):
                        at = row - i - 8 * part
                        if 0 <= v - p < 3 and 0 <= at < 8:
                            tap = i * 3 + v - p
                            windows[pl.ds(((part * 2 + p) * 8 + at) * 16, 16), pl.ds(tap * 256, 256)] = cells
        lhs = windows[pl.ds(part * 256, 256), :]
        fields.append([dot(lhs, conv_ref[s].reshape(2304, 256)) for s in range(2)])
    c0 = jnp.concatenate([fields[0][0], fields[1][0]], 0)
    c1 = jnp.concatenate([fields[0][1], fields[1][1]], 0) + c0 * start
    c1_ref[...] = c1
    both = dot(jnp.concatenate([folded(c0), folded(c1)], 0), down_ref[...]).astype(BF16)
    far_ref[...] = both[:128]
    near_ref[...] = both[128:]


def here_kernel(flag_ref, windows, reduced, c1_ref, conv_ref, down_ref, latent_ref):
    start = (flag_ref[0] == 0).astype(F32)
    plain = []
    for part in range(2):
        for p in range(2):
            for row in range(8 * part, 8 * part + 8):
                halves = [reduced[half, row + 1, pl.ds(1 + p, 16, stride=2), :] for half in range(2)]
                plain.append(jnp.concatenate(halves, -1))
    c2 = dot(windows[...], conv_ref[2].reshape(2304, 256)) + c1_ref[...] * start
    latent_ref[...] = dot(folded(c2 + jnp.concatenate(plain, 0)), down_ref[...])


def coarse(flags, own, got, gain, conv, down):
    conv = conv.reshape(3, 9, 256, 256)
    rows = shape((128, 512), BF16)
    field = shape((512, 256), F32)
    far, near, c1, windows, reduced = call(
        sent_kernel,
        (rows, rows, field, shape((512, 2304), BF16), shape((2, 18, PITCH, 128), F32)),
        [SM] + [VM] * 5,
        [pltpu.VMEM((FLAT, 256), F32), pltpu.VMEM((2, 18, PITCH, 128), F32)],
        flops=1_500_000_000,
        name="coarse_sent",
    )(flags, own, got, gain.reshape(1, 256), conv, down)
    latent = call(here_kernel, shape((128, 512), F32), [SM] + [VM] * 5, flops=1000, moved=1000, name="coarse_here")(
        flags, windows, reduced, c1, conv, down
    )
    return near, far, latent


def mix_kernel(query_ref, key_ref, value_ref, out_ref, score_ref, mix_ref):
    scores = lax.dot_general(query_ref[...], key_ref[...], (((1,), (1,)), ((), ())), preferred_element_type=F32)
    score_ref[...] = (scores * (1.0 / math.sqrt(512))).astype(BF16)
    mix_ref[...] = dot(value_ref[...], out_ref[...]).astype(BF16)


def latent_kernel(own_ref, near_ref, far_ref, gain_ref, score_ref, latent_ref, query_ref, copies_ref):
    latent = (own_ref[...] + near_ref[...].astype(F32) + far_ref[...].astype(F32)).astype(BF16)
    latent_ref[...] = latent
    normed = scaled(latent.astype(F32), gain_ref[...]).astype(BF16)
    for k in range(copies_ref.shape[0]):
        copies_ref[k] = normed
    query_ref[...] = dot(normed, score_ref[...]).astype(BF16)


def packed(values, level):
    across = jnp.broadcast_to(level, (128, 128)).T[:16]
    high = across.astype(BF16).astype(F32)
    middle = (across - high).astype(BF16).astype(F32)
    low = across - high - middle
    row = lax.broadcasted_iota(jnp.int32, (16, 128), 0)
    parts = jnp.where(row == 0, high, jnp.where(row == 1, middle, jnp.where(row == 2, low, 0.0)))
    last = jnp.concatenate([parts, jnp.zeros((16, 384), F32)], -1)
    return jnp.concatenate([values, last], 0).astype(BF16)


def level_of(block):
    across = jnp.sum(block[128:, :128].astype(F32), 0, keepdims=True)
    return jnp.broadcast_to(across, (128, 128)).T[:, :1]


def softmax_part(queries, keys):
    scores = lax.dot_general(queries, keys, (((1,), (1,)), ((), ())), preferred_element_type=F32)
    top = jnp.max(scores, -1, keepdims=True)
    expo = jnp.exp(scores - top)
    total = jnp.sum(expo, -1, keepdims=True)
    return dot(expo.astype(BF16), keys) / total, top + jnp.log(total)


def attend_theirs_kernel(q1_ref, q2_ref, q3_ref, keys_ref, other_keys_ref, *sent):
    queries = jnp.concatenate([q1_ref[...], q2_ref[...], q3_ref[...]], 0)
    keys = jnp.concatenate([keys_ref[...], other_keys_ref[...]], 0)
    mixed, level = softmax_part(queries, keys)
    for k in range(3):
        rows = slice(128 * k, 128 * (k + 1))
        sent[k][...] = packed(mixed[rows], level[rows])


def attend_mine_kernel(queries_ref, keys_ref, other_keys_ref, mixed_ref, level_ref):
    keys = jnp.concatenate([keys_ref[...], other_keys_ref[...]], 0)
    mixed, level = softmax_part(queries_ref[...], keys)
    mixed_ref[...] = mixed
    level_ref[...] = jnp.broadcast_to(level, (128, 128))


def finish_kernel(mixed_ref, level_ref, got1_ref, got2_ref, got3_ref, latent_ref, mix_ref, out_ref):
    blocks = [ref[...] for ref in (got1_ref, got2_ref, got3_ref)]
    levels = [level_ref[:, :1]] + [level_of(block) for block in blocks]
    values = [mixed_ref[...]] + [block[:128].astype(F32) for block in blocks]
    top = functools.reduce(jnp.maximum, levels)
    shares = [jnp.exp(level - top) for level in levels]
    summed = sum(value * share for value, share in zip(values, shares))
    attended = summed / sum(shares)
    out_ref[...] = (latent_ref[...].astype(F32) + dot(attended.astype(BF16), mix_ref[...])).astype(BF16)


def swapped(value, axis, count, first):
    pairs = []
    for low in range(first, count - 1, 2):
        pairs += [(low, low + 1), (low + 1, low)]
    return lax.ppermute(value, axis, pairs)


def turned(value, step):
    return lax.ppermute(value, RING, [(i, (i + step) % 4) for i in range(4)])


def sides(block, axis, count):
    odd = lax.axis_index(axis) % 2
    rows = shape((2, 3, 64, 128), BF16)
    inner, outer = call(
        edges_kernel, (rows, rows), [SM, HB], [pltpu.SemaphoreType.DMA((2,))], flops=1000, name="edges"
    )(odd.astype(jnp.int32).reshape(1), kept(block))
    got_inner = swapped(inner, axis, count, 0)
    got_outer = swapped(outer, axis, count, 1)
    even = odd == 0
    return jnp.where(even, got_outer, got_inner), jnp.where(even, got_inner, got_outer)


def per_device(
    features, gain_fine, conv_fine, down_fine, gain_coarse, conv_coarse, down_coarse,
    gain_latent, w_query, w_key, w_value, w_out,
):
    rows = shape((128, 512), BF16)
    tm = lax.axis_index("tm").astype(jnp.int32)
    flags = jnp.stack([tm, lax.axis_index(HEIGHT).astype(jnp.int32), lax.axis_index(WIDTH).astype(jnp.int32)])
    above, below = sides(features, HEIGHT, 4)
    act, first, last, conv_here, down_here = prepare(features, gain_fine, conv_fine, down_fine)
    above, below, act, first, last = lax.optimization_barrier((above, below, act, first, last))
    first = jnp.concatenate([above[:, :, :4], first, below[:, :, :4]], 1)
    last = jnp.concatenate([above[:, :, 60:], last, below[:, :, 60:]], 1)
    odd = lax.axis_index(WIDTH) % 2 == 1
    got_inner = swapped(jnp.where(odd, first, last), WIDTH, 8, 0)
    got_outer = swapped(jnp.where(odd, last, first), WIDTH, 8, 1)
    weight_next = compose(False, flags, conv_here, down_here)
    got_inner, got_outer, weight_next = lax.optimization_barrier((got_inner, got_outer, weight_next))
    left, right = jnp.where(odd, got_inner, got_outer), jnp.where(odd, got_outer, got_inner)
    halos = (above, below, left, right)
    sent, planes = fine_next(act, halos, gain_fine, weight_next)
    sent, conv_here, down_here = lax.optimization_barrier((sent, conv_here, down_here))
    got = lax.ppermute(sent, "tm", [(i, i + 1) for i in range(7)])
    weight_own = compose(True, flags, conv_here, down_here)
    own = fine_own(features, halos, weight_own, planes, down_here)
    square = shape((512, 512), BF16)
    w_score, w_mix = call(mix_kernel, (square, square), [VM] * 4, flops=1000, moved=1000, name="mix")(
        w_query, w_key, w_value, w_out
    )
    got, own, w_score, w_mix = lax.optimization_barrier((got, own, w_score, w_mix))
    near, far, latent_own = coarse(flags, own, got, gain_coarse, conv_coarse, down_coarse)
    far = lax.ppermute(far, "tm", [(i, i + 2) for i in range(6)])
    near = lax.ppermute(near, "tm", [(i, i + 1) for i in range(7)])
    latent_in, query, copies = call(
        latent_kernel, (rows, rows, shape((4, 128, 512), BF16)), [VM] * 5, flops=80_000_000, name="latent"
    )(latent_own, near, far, gain_latent.reshape(1, 512), w_score)
    keys = lax.all_to_all(copies, "y", 0, 0, tiled=True).reshape(512, 512)
    asked = [turned(query, step) for step in (1, 2, 3)]
    keys, *asked = lax.optimization_barrier((keys, *asked))
    other_keys = swapped(keys, "core", 2, 0)
    sent = call(
        attend_theirs_kernel, (shape((144, 512), BF16),) * 3, [VM] * 5, flops=800_000_000, name="attend_theirs"
    )(*asked, keys, other_keys)
    mixed, level = call(
        attend_mine_kernel,
        (shape((128, 512), F32), shape((128, 128), F32)),
        [VM] * 3,
        flops=300_000_000,
        name="attend_mine",
    )(query, keys, other_keys)
    got = [turned(block, -step) for step, block in zip((1, 2, 3), sent)]
    out = call(finish_kernel, rows, [VM] * 7, flops=70_000_000, name="finish")(mixed, level, *got, latent_in, w_mix)
    return out.reshape(1, 8, 16, 512)


def solution(mesh):
    split = Mesh(mesh.devices.reshape(8, 2, 2, 4, 2), ("tm", "hx", "core", "y", "lx"))
    placed = (P("tm", HEIGHT, WIDTH, None),) + (P(),) * 11
    return jax.shard_map(
        per_device, mesh=split, in_specs=placed,
        out_specs=P("tm", HEIGHT, WIDTH, None), check_vma=False,
    )
```

```python
import functools
import math

import jax
import jax.numpy as jnp
from jax import lax
from jax.experimental import pallas as pl
from jax.experimental.pallas import tpu as pltpu
from jax.sharding import Mesh, PartitionSpec as P

EPSILON = 1e-06
BF16 = jnp.bfloat16
F32 = jnp.float32
HEIGHT = ("hx", "core")
WIDTH = ("y", "lx")
RING = ("hx", "lx")
VMEM_LIMIT = 32 * 1024 * 1024
VM = pl.BlockSpec(memory_space=pltpu.VMEM)
HB = pl.BlockSpec(memory_space=pltpu.HBM)
SM = pl.BlockSpec(memory_space=pltpu.SMEM)


def call(kernel, out, ins, scratch=(), flops=0, moved=4 << 20, name=None):
    return pl.pallas_call(
        kernel,
        out_shape=out,
        in_specs=ins,
        out_specs=jax.tree.map(lambda _: VM, out),
        scratch_shapes=list(scratch),
        compiler_params=pltpu.CompilerParams(vmem_limit_bytes=VMEM_LIMIT),
        cost_estimate=pl.CostEstimate(flops=flops, bytes_accessed=moved, transcendentals=0),
        name=name,
    )


def kept(value):
    return pltpu.with_memory_space_constraint(value, pltpu.HBM)


def shape(dims, dtype):
    return jax.ShapeDtypeStruct(dims, dtype)


def dot(a, b):
    return jnp.dot(a, b, preferred_element_type=F32)


def scaled(values, gain):
    mean = jnp.mean(values * values, axis=-1, keepdims=True)
    return values * lax.rsqrt(mean + EPSILON) * gain


def silu(values):
    return values * jax.nn.sigmoid(values)


def compose_kernel(own, flag_ref, conv, down, out_ref, acc):
    acc[...] = jnp.zeros_like(acc)
    start = flag_ref[0] == 0
    for i in range(3):
        k0, k1 = (conv[s, i].reshape(384, 128) for s in range(2))
        if own:
            k2 = conv[2, i].reshape(384, 128)
            f0, f1, f2 = (k.astype(F32) for k in (k0, k1, k2))
            k2s = jnp.where(start, f0 + f1 + f2, f2).astype(BF16)
            k1s = jnp.where(start, f0 + f1, f1).astype(BF16)
            wide, narrow, wide_at, narrow_at, half = jnp.concatenate([k2s, k1s], -1), k2, 0, 1, 1
        else:
            wide, narrow, wide_at, narrow_at, half = jnp.concatenate([k1, k0], -1), k0, 1, 0, 0
        for r in range(2):
            for c in range(2):
                at = (r * 2 + c) * 128
                halves = [down[f * 512 + at : f * 512 + at + 128, :] for f in range(2)]
                both = dot(wide, jnp.concatenate(halves, 0))
                one = dot(narrow, halves[half])
                for j in range(3):
                    tap = (i + r) * 4 + j + c
                    rows = slice(j * 128, j * 128 + 128)
                    acc[tap, wide_at * 128 : wide_at * 128 + 128, :] += both[rows]
                    acc[tap, narrow_at * 128 : narrow_at * 128 + 128, :] += one[rows]
    out_ref[...] = acc[...].astype(BF16)


def compose(own, tm, conv_fine, down_fine):
    return call(
        functools.partial(compose_kernel, own),
        shape((16, 256, 256), BF16),
        [SM, VM, VM],
        [pltpu.VMEM((16, 256, 256), F32)],
        flops=900_000_000,
        name="compose_own" if own else "compose_next",
    )(tm, conv_fine, down_fine)


COLS = 104
PITCH = 48
FLAT = 624


def edges_kernel(odd_ref, x_hbm, inner_ref, outer_ref, sems):
    odd = odd_ref[0]
    inner = pltpu.make_async_copy(x_hbm.at[:, pl.ds((1 - odd) * 29, 3)], inner_ref, sems.at[0])
    outer = pltpu.make_async_copy(x_hbm.at[:, pl.ds(odd * 29, 3)], outer_ref, sems.at[1])
    inner.start()
    outer.start()
    inner.wait()
    outer.wait()


def prepare_kernel(
    x_hbm, gain_hbm, conv_hbm, down_hbm, act_ref, first_ref, last_ref, conv_ref, down_ref, x, gain_ref, sems
):
    fetches = []
    for k in range(4):
        rows = pl.ds(k * 8, 8)
        fetches.append(pltpu.make_async_copy(x_hbm.at[:, rows], x.at[:, rows], sems.at[k]))
        fetches[k].start()
    fetch_gain = pltpu.make_async_copy(gain_hbm, gain_ref, sems.at[4])
    fetch_gain.start()
    weights = [pltpu.make_async_copy(conv_hbm, conv_ref, sems.at[5]), pltpu.make_async_copy(down_hbm, down_ref, sems.at[6])]
    for fetch in weights:
        fetch.start()
    fetch_gain.wait()
    gain = gain_ref[...].reshape(1, 1, 128)
    for k in range(4):
        fetches[k].wait()
        for f in range(2):
            for half in range(2):
                rows = pl.ds(k * 8 + half * 4, 4)
                act_ref[f, rows] = silu(scaled(x[f, rows].astype(F32), gain))
    first_ref[...] = x[:, :, 0:4]
    last_ref[...] = x[:, :, 60:64]
    for fetch in weights:
        fetch.wait()


def prepare(features, gain, conv, down):
    edge = shape((2, 32, 4, 128), BF16)
    return call(
        prepare_kernel,
        (shape((2, 32, 64, 128), F32), edge, edge, shape((3, 3, 3, 128, 128), BF16), shape((1024, 256), BF16)),
        [HB] * 4,
        [pltpu.VMEM((2, 32, 64, 128), BF16), pltpu.VMEM((1, 128), F32), pltpu.SemaphoreType.DMA((7,))],
        flops=10_000_000,
        name="prepare",
    )(kept(features), kept(gain.reshape(1, 128)), kept(conv.reshape(3, 3, 3, 128, 128)), kept(down))


def spread(field, up_ref, low_ref, left_ref, right_ref, change):
    for f in range(2):
        field[f, pl.ds(0, 3), pl.ds(8, 64), :] = change(up_ref[f].astype(F32))
        field[f, pl.ds(35, 3), pl.ds(8, 64), :] = change(low_ref[f].astype(F32))
        field[f, :, pl.ds(4, 4), :] = change(left_ref[f].astype(F32))
        field[f, :, pl.ds(72, 4), :] = change(right_ref[f].astype(F32))


GROUP = 6


def next_kernel(act_ref, up_ref, low_ref, left_ref, right_ref, gain_ref, weight_ref, out_ref, planes, act, flat):
    gain = gain_ref[...].reshape(1, 1, 128)
    spread(act, up_ref, low_ref, left_ref, right_ref, lambda values: silu(scaled(values, gain)))
    act[:, pl.ds(3, 32), pl.ds(8, 64), :] = act_ref[...]

    def build(q):
        for rp in range(2):
            for v in range(4):
                both = [act[f, 2 * q + rp, pl.ds(5 + v, 40, stride=2), :].astype(BF16) for f in range(2)]
                planes[rp, v, q, pl.ds(0, 40), :] = jnp.concatenate(both, -1)

    built = 0
    for base in range(0, 18, GROUP):
        while built < base + GROUP + 1:
            build(built)
            built += 1
        total = dot(taps_at(planes, base), weight_ref[...].reshape(4096, 256)).reshape(GROUP, PITCH, 256)
        for k in range(GROUP):
            flat[pl.ds((base + k) * 34, 34), :] = total[k, :34]
    flat[pl.ds(612, 12), :] = jnp.zeros((12, 256), F32)
    out_ref[...] = flat[...].astype(BF16)


def taps_at(planes, base):
    parts = []
    for u in range(4):
        for v in range(4):
            parts.append(planes[u % 2, v, pl.ds(base + u // 2, GROUP)].reshape(GROUP * PITCH, 256))
    return jnp.concatenate(parts, -1)


def own_kernel(x_ref, up_ref, low_ref, left_ref, right_ref, weight_ref, planes, down_ref, out_ref, raw, raw_planes):
    spread(raw, up_ref, low_ref, left_ref, right_ref, lambda values: values)
    raw[:, pl.ds(3, 32), pl.ds(8, 64), :] = x_ref[...].astype(F32)

    def build(q):
        for rp in range(2):
            for v in range(2):
                both = [raw[f, 2 * q + rp, pl.ds(6 + v, 40, stride=2), :].astype(BF16) for f in range(2)]
                raw_planes[rp, v, q, pl.ds(0, 40), :] = jnp.concatenate(both, -1)

    folds = []
    for r in range(2):
        for c in range(2):
            for f in range(2):
                at = (f * 4 + r * 2 + c) * 128
                folds.append(down_ref[at : at + 128, :])
    fold_weight = jnp.concatenate(folds, 0)
    built = 0
    for base in range(0, 18, GROUP):
        while built < base + GROUP + 1:
            build(built)
            built += 1
        parts = []
        for r in range(2):
            for c in range(2):
                rows = pl.ds(base + (r + 1) // 2, GROUP)
                parts.append(raw_planes[(r + 1) % 2, c, rows].reshape(GROUP * PITCH, 256))
        total = dot(taps_at(planes, base), weight_ref[...].reshape(4096, 256))
        total = total + dot(jnp.concatenate(parts, -1), fold_weight)
        out_ref[base : base + GROUP] = total.reshape(GROUP, PITCH, 256)


def fine_next(act, halos, gain, weight):
    return call(
        next_kernel,
        (shape((FLAT, 256), BF16), shape((2, 4, 19, PITCH, 256), BF16)),
        [VM] * 7,
        [pltpu.VMEM((2, 38, COLS, 128), F32), pltpu.VMEM((FLAT, 256), F32)],
        flops=1_800_000_000,
        name="fine_next",
    )(act, *halos, gain.reshape(1, 128), weight)


def fine_own(features, halos, weight, planes, down):
    return call(
        own_kernel,
        shape((18, PITCH, 256), F32),
        [VM] * 8,
        [pltpu.VMEM((2, 38, COLS, 128), F32), pltpu.VMEM((2, 2, 19, PITCH, 256), BF16)],
        flops=2_200_000_000,
        name="fine_own",
    )(features, *halos, weight, planes, down)


def folded(field):
    field = field.astype(BF16).reshape(2, 2, 4, 2, 16, 256)
    parts = [field[:, p, :, r].reshape(128, 256) for r in range(2) for p in range(2)]
    return jnp.concatenate(parts, -1)


def sent_kernel(
    flag_ref, own_ref, got_ref, gain_ref, conv_ref, down_ref, far_ref, near_ref, c1_ref, windows, reduced, got, act
):
    gain = gain_ref[...]
    got[...] = got_ref[...].astype(F32)
    start = (flag_ref[0] == 0).astype(F32)
    col = lax.broadcasted_iota(jnp.int32, (40, 128), 0)
    inside = ((col > 0) | (flag_ref[2] > 0)) & ((col < 33) | (flag_ref[2] < 7))
    inside = inside.astype(F32)
    ends = {0: (flag_ref[1] > 0).astype(F32), 17: (flag_ref[1] < 3).astype(F32)}
    fields = []
    done = 0
    for part in range(2):
        for row in range(done, 10 + 8 * part):
            value = own_ref[row, pl.ds(0, 40), :] + got[pl.ds(row * 34, 40), :]
            value = value.astype(BF16).astype(F32)
            active = silu(scaled(value, gain))
            keep = inside * ends[row] if row in ends else inside
            for half in range(2):
                reduced[half, row, pl.ds(0, 40), :] = value[:, half * 128 : half * 128 + 128]
                act[half, row, pl.ds(0, 40), :] = active[:, half * 128 : half * 128 + 128] * keep
        done = 10 + 8 * part
        for row in range(8 * part, 8 * part + 10):
            for v in range(4):
                halves = [act[half, row, pl.ds(v, 16, stride=2), :] for half in range(2)]
                cells = jnp.concatenate(halves, -1).astype(BF16)
                for p in range(2):
                    for i in range(3):
                        at = row - i - 8 * part
                        if 0 <= v - p < 3 and 0 <= at < 8:
                            tap = i * 3 + v - p
                            windows[pl.ds(((part * 2 + p) * 8 + at) * 16, 16), pl.ds(tap * 256, 256)] = cells
        lhs = windows[pl.ds(part * 256, 256), :]
        fields.append([dot(lhs, conv_ref[s].reshape(2304, 256)) for s in range(2)])
    c0 = jnp.concatenate([fields[0][0], fields[1][0]], 0)
    c1 = jnp.concatenate([fields[0][1], fields[1][1]], 0) + c0 * start
    c1_ref[...] = c1
    both = dot(jnp.concatenate([folded(c0), folded(c1)], 0), down_ref[...]).astype(BF16)
    far_ref[...] = both[:128]
    near_ref[...] = both[128:]


def here_kernel(flag_ref, windows, reduced, c1_ref, conv_ref, down_ref, latent_ref):
    start = (flag_ref[0] == 0).astype(F32)
    plain = []
    for part in range(2):
        for p in range(2):
            for row in range(8 * part, 8 * part + 8):
                halves = [reduced[half, row + 1, pl.ds(1 + p, 16, stride=2), :] for half in range(2)]
                plain.append(jnp.concatenate(halves, -1))
    c2 = dot(windows[...], conv_ref[2].reshape(2304, 256)) + c1_ref[...] * start
    latent_ref[...] = dot(folded(c2 + jnp.concatenate(plain, 0)), down_ref[...])


def coarse(flags, own, got, gain, conv, down):
    conv = conv.reshape(3, 9, 256, 256)
    rows = shape((128, 512), BF16)
    field = shape((512, 256), F32)
    far, near, c1, windows, reduced = call(
        sent_kernel,
        (rows, rows, field, shape((512, 2304), BF16), shape((2, 18, PITCH, 128), F32)),
        [SM] + [VM] * 5,
        [pltpu.VMEM((FLAT, 256), F32), pltpu.VMEM((2, 18, PITCH, 128), F32)],
        flops=1_500_000_000,
        name="coarse_sent",
    )(flags, own, got, gain.reshape(1, 256), conv, down)
    latent = call(here_kernel, shape((128, 512), F32), [SM] + [VM] * 5, flops=1000, moved=1000, name="coarse_here")(
        flags, windows, reduced, c1, conv, down
    )
    return near, far, latent


def mix_kernel(query_ref, key_ref, value_ref, out_ref, score_ref, mix_ref):
    scores = lax.dot_general(query_ref[...], key_ref[...], (((1,), (1,)), ((), ())), preferred_element_type=F32)
    score_ref[...] = (scores * (1.0 / math.sqrt(512))).astype(BF16)
    mix_ref[...] = dot(value_ref[...], out_ref[...]).astype(BF16)


def latent_kernel(own_ref, near_ref, far_ref, gain_ref, score_ref, latent_ref, query_ref, copies_ref):
    latent = (own_ref[...] + near_ref[...].astype(F32) + far_ref[...].astype(F32)).astype(BF16)
    latent_ref[...] = latent
    normed = scaled(latent.astype(F32), gain_ref[...]).astype(BF16)
    for k in range(copies_ref.shape[0]):
        copies_ref[k] = normed
    query_ref[...] = dot(normed, score_ref[...]).astype(BF16)


def packed(values, level):
    across = jnp.broadcast_to(level, (128, 128)).T[:16]
    high = across.astype(BF16).astype(F32)
    middle = (across - high).astype(BF16).astype(F32)
    low = across - high - middle
    row = lax.broadcasted_iota(jnp.int32, (16, 128), 0)
    parts = jnp.where(row == 0, high, jnp.where(row == 1, middle, jnp.where(row == 2, low, 0.0)))
    last = jnp.concatenate([parts, jnp.zeros((16, 384), F32)], -1)
    return jnp.concatenate([values, last], 0).astype(BF16)


def level_of(block):
    across = jnp.sum(block[128:, :128].astype(F32), 0, keepdims=True)
    return jnp.broadcast_to(across, (128, 128)).T[:, :1]


def softmax_part(queries, keys):
    scores = lax.dot_general(queries, keys, (((1,), (1,)), ((), ())), preferred_element_type=F32)
    top = jnp.max(scores, -1, keepdims=True)
    expo = jnp.exp(scores - top)
    total = jnp.sum(expo, -1, keepdims=True)
    return dot(expo.astype(BF16), keys) / total, top + jnp.log(total)


def attend_two_kernel(q1_ref, q2_ref, keys_ref, other_keys_ref, sent1_ref, sent2_ref):
    keys = jnp.concatenate([keys_ref[...], other_keys_ref[...]], 0)
    mixed, level = softmax_part(jnp.concatenate([q1_ref[...], q2_ref[...]], 0), keys)
    sent1_ref[...] = packed(mixed[:128], level[:128])
    sent2_ref[...] = packed(mixed[128:], level[128:])


def attend_last_kernel(q3_ref, mine_ref, keys_ref, other_keys_ref, sent3_ref, mixed_ref, level_ref):
    keys = jnp.concatenate([keys_ref[...], other_keys_ref[...]], 0)
    mixed, level = softmax_part(jnp.concatenate([q3_ref[...], mine_ref[...]], 0), keys)
    sent3_ref[...] = packed(mixed[:128], level[:128])
    mixed_ref[...] = mixed[128:]
    level_ref[...] = jnp.broadcast_to(level[128:], (128, 128))


def finish_kernel(mixed_ref, level_ref, got1_ref, got2_ref, got3_ref, latent_ref, mix_ref, out_ref):
    blocks = [ref[...] for ref in (got1_ref, got2_ref, got3_ref)]
    levels = [level_ref[:, :1]] + [level_of(block) for block in blocks]
    values = [mixed_ref[...]] + [block[:128].astype(F32) for block in blocks]
    top = functools.reduce(jnp.maximum, levels)
    shares = [jnp.exp(level - top) for level in levels]
    summed = sum(value * share for value, share in zip(values, shares))
    attended = summed / sum(shares)
    out_ref[...] = (latent_ref[...].astype(F32) + dot(attended.astype(BF16), mix_ref[...])).astype(BF16)


def swapped(value, axis, count, first):
    pairs = []
    for low in range(first, count - 1, 2):
        pairs += [(low, low + 1), (low + 1, low)]
    return lax.ppermute(value, axis, pairs)


def turned(value, step):
    return lax.ppermute(value, RING, [(i, (i + step) % 4) for i in range(4)])


def sides(block, axis, count):
    odd = lax.axis_index(axis) % 2
    rows = shape((2, 3, 64, 128), BF16)
    inner, outer = call(
        edges_kernel, (rows, rows), [SM, HB], [pltpu.SemaphoreType.DMA((2,))], flops=1000, name="edges"
    )(odd.astype(jnp.int32).reshape(1), kept(block))
    got_inner = swapped(inner, axis, count, 0)
    got_outer = swapped(outer, axis, count, 1)
    even = odd == 0
    return jnp.where(even, got_outer, got_inner), jnp.where(even, got_inner, got_outer)


def per_device(
    features, gain_fine, conv_fine, down_fine, gain_coarse, conv_coarse, down_coarse,
    gain_latent, w_query, w_key, w_value, w_out,
):
    rows = shape((128, 512), BF16)
    tm = lax.axis_index("tm").astype(jnp.int32)
    flags = jnp.stack([tm, lax.axis_index(HEIGHT).astype(jnp.int32), lax.axis_index(WIDTH).astype(jnp.int32)])
    above, below = sides(features, HEIGHT, 4)
    act, first, last, conv_here, down_here = prepare(features, gain_fine, conv_fine, down_fine)
    above, below, act, first, last = lax.optimization_barrier((above, below, act, first, last))
    first = jnp.concatenate([above[:, :, :4], first, below[:, :, :4]], 1)
    last = jnp.concatenate([above[:, :, 60:], last, below[:, :, 60:]], 1)
    odd = lax.axis_index(WIDTH) % 2 == 1
    got_inner = swapped(jnp.where(odd, first, last), WIDTH, 8, 0)
    got_outer = swapped(jnp.where(odd, last, first), WIDTH, 8, 1)
    weight_next = compose(False, flags, conv_here, down_here)
    got_inner, got_outer, weight_next = lax.optimization_barrier((got_inner, got_outer, weight_next))
    left, right = jnp.where(odd, got_inner, got_outer), jnp.where(odd, got_outer, got_inner)
    halos = (above, below, left, right)
    sent, planes = fine_next(act, halos, gain_fine, weight_next)
    sent, conv_here, down_here = lax.optimization_barrier((sent, conv_here, down_here))
    got = lax.ppermute(sent, "tm", [(i, i + 1) for i in range(7)])
    weight_own = compose(True, flags, conv_here, down_here)
    own = fine_own(features, halos, weight_own, planes, down_here)
    square = shape((512, 512), BF16)
    w_score, w_mix = call(mix_kernel, (square, square), [VM] * 4, flops=1000, moved=1000, name="mix")(
        w_query, w_key, w_value, w_out
    )
    got, own, w_score, w_mix = lax.optimization_barrier((got, own, w_score, w_mix))
    near, far, latent_own = coarse(flags, own, got, gain_coarse, conv_coarse, down_coarse)
    far = lax.ppermute(far, "tm", [(i, i + 2) for i in range(6)])
    near = lax.ppermute(near, "tm", [(i, i + 1) for i in range(7)])
    latent_in, query, copies = call(
        latent_kernel, (rows, rows, shape((4, 128, 512), BF16)), [VM] * 5, flops=80_000_000, name="latent"
    )(latent_own, near, far, gain_latent.reshape(1, 512), w_score)
    keys = lax.all_to_all(copies, "y", 0, 0, tiled=True).reshape(512, 512)
    asked = [turned(query, step) for step in (1, 2, 3)]
    keys, asked[0], asked[1] = lax.optimization_barrier((keys, asked[0], asked[1]))
    other_keys = swapped(keys, "core", 2, 0)
    block = shape((144, 512), BF16)
    sent1, sent2 = call(attend_two_kernel, (block, block), [VM] * 4, flops=550_000_000, name="attend_two")(
        asked[0], asked[1], keys, other_keys
    )
    sent3, mixed, level = call(
        attend_last_kernel,
        (block, shape((128, 512), F32), shape((128, 128), F32)),
        [VM] * 4,
        flops=550_000_000,
        name="attend_last",
    )(asked[2], query, keys, other_keys)
    sent = (sent1, sent2, sent3)
    got = [turned(block, -step) for step, block in zip((1, 2, 3), sent)]
    out = call(finish_kernel, rows, [VM] * 7, flops=70_000_000, name="finish")(mixed, level, *got, latent_in, w_mix)
    return out.reshape(1, 8, 16, 512)


def solution(mesh):
    split = Mesh(mesh.devices.reshape(8, 2, 2, 4, 2), ("tm", "hx", "core", "y", "lx"))
    placed = (P("tm", HEIGHT, WIDTH, None),) + (P(),) * 11
    return jax.shard_map(
        per_device, mesh=split, in_specs=placed,
        out_specs=P("tm", HEIGHT, WIDTH, None), check_vma=False,
    )
```

```python
import functools
import math

import jax
import jax.numpy as jnp
from jax import lax
from jax.experimental import pallas as pl
from jax.experimental.pallas import tpu as pltpu
from jax.sharding import Mesh, PartitionSpec as P

EPSILON = 1e-06
BF16 = jnp.bfloat16
F32 = jnp.float32
HEIGHT = ("hx", "core")
WIDTH = ("y", "lx")
RING = ("hx", "lx")
VMEM_LIMIT = 32 * 1024 * 1024
VM = pl.BlockSpec(memory_space=pltpu.VMEM)
HB = pl.BlockSpec(memory_space=pltpu.HBM)
SM = pl.BlockSpec(memory_space=pltpu.SMEM)


def call(kernel, out, ins, scratch=(), flops=0, moved=4 << 20, name=None):
    return pl.pallas_call(
        kernel,
        out_shape=out,
        in_specs=ins,
        out_specs=jax.tree.map(lambda _: VM, out),
        scratch_shapes=list(scratch),
        compiler_params=pltpu.CompilerParams(vmem_limit_bytes=VMEM_LIMIT),
        cost_estimate=pl.CostEstimate(flops=flops, bytes_accessed=moved, transcendentals=0),
        name=name,
    )


def kept(value):
    return pltpu.with_memory_space_constraint(value, pltpu.HBM)


def shape(dims, dtype):
    return jax.ShapeDtypeStruct(dims, dtype)


def dot(a, b):
    return jnp.dot(a, b, preferred_element_type=F32)


def scaled(values, gain):
    mean = jnp.mean(values * values, axis=-1, keepdims=True)
    return values * lax.rsqrt(mean + EPSILON) * gain


def silu(values):
    return values * jax.nn.sigmoid(values)


def compose_kernel(own, flag_ref, conv, down, out_ref, acc):
    acc[...] = jnp.zeros_like(acc)
    start = flag_ref[0] == 0
    for i in range(3):
        k0, k1 = (conv[s, i].reshape(384, 128) for s in range(2))
        if own:
            k2 = conv[2, i].reshape(384, 128)
            f0, f1, f2 = (k.astype(F32) for k in (k0, k1, k2))
            k2s = jnp.where(start, f0 + f1 + f2, f2).astype(BF16)
            k1s = jnp.where(start, f0 + f1, f1).astype(BF16)
            wide, narrow, wide_at, narrow_at, half = jnp.concatenate([k2s, k1s], -1), k2, 0, 1, 1
        else:
            wide, narrow, wide_at, narrow_at, half = jnp.concatenate([k1, k0], -1), k0, 1, 0, 0
        for r in range(2):
            for c in range(2):
                at = (r * 2 + c) * 128
                halves = [down[f * 512 + at : f * 512 + at + 128, :] for f in range(2)]
                both = dot(wide, jnp.concatenate(halves, 0))
                one = dot(narrow, halves[half])
                for j in range(3):
                    tap = (i + r) * 4 + j + c
                    rows = slice(j * 128, j * 128 + 128)
                    acc[tap, wide_at * 128 : wide_at * 128 + 128, :] += both[rows]
                    acc[tap, narrow_at * 128 : narrow_at * 128 + 128, :] += one[rows]
    out_ref[...] = acc[...].astype(BF16)


def compose(own, tm, conv_fine, down_fine):
    return call(
        functools.partial(compose_kernel, own),
        shape((16, 256, 256), BF16),
        [SM, VM, VM],
        [pltpu.VMEM((16, 256, 256), F32)],
        flops=900_000_000,
        name="compose_own" if own else "compose_next",
    )(tm, conv_fine, down_fine)


COLS = 104
PITCH = 48
FLAT = 624


def edges_kernel(odd_ref, x_hbm, inner_ref, outer_ref, sems):
    odd = odd_ref[0]
    inner = pltpu.make_async_copy(x_hbm.at[:, pl.ds((1 - odd) * 29, 3)], inner_ref, sems.at[0])
    outer = pltpu.make_async_copy(x_hbm.at[:, pl.ds(odd * 29, 3)], outer_ref, sems.at[1])
    inner.start()
    outer.start()
    inner.wait()
    outer.wait()


def prepare_kernel(
    x_hbm, gain_hbm, conv_hbm, down_hbm, act_ref, first_ref, last_ref, conv_ref, down_ref, x, gain_ref, sems
):
    fetches = []
    for k in range(4):
        rows = pl.ds(k * 8, 8)
        fetches.append(pltpu.make_async_copy(x_hbm.at[:, rows], x.at[:, rows], sems.at[k]))
        fetches[k].start()
    fetch_gain = pltpu.make_async_copy(gain_hbm, gain_ref, sems.at[4])
    fetch_gain.start()
    weights = [pltpu.make_async_copy(conv_hbm, conv_ref, sems.at[5]), pltpu.make_async_copy(down_hbm, down_ref, sems.at[6])]
    for fetch in weights:
        fetch.start()
    fetch_gain.wait()
    gain = gain_ref[...].reshape(1, 1, 128)
    for k in range(4):
        fetches[k].wait()
        for f in range(2):
            for half in range(2):
                rows = pl.ds(k * 8 + half * 4, 4)
                act_ref[f, rows] = silu(scaled(x[f, rows].astype(F32), gain))
    first_ref[...] = x[:, :, 0:4]
    last_ref[...] = x[:, :, 60:64]
    for fetch in weights:
        fetch.wait()


def prepare(features, gain, conv, down):
    edge = shape((2, 32, 4, 128), BF16)
    return call(
        prepare_kernel,
        (shape((2, 32, 64, 128), F32), edge, edge, shape((3, 3, 3, 128, 128), BF16), shape((1024, 256), BF16)),
        [HB] * 4,
        [pltpu.VMEM((2, 32, 64, 128), BF16), pltpu.VMEM((1, 128), F32), pltpu.SemaphoreType.DMA((7,))],
        flops=10_000_000,
        name="prepare",
    )(kept(features), kept(gain.reshape(1, 128)), kept(conv.reshape(3, 3, 3, 128, 128)), kept(down))


def spread(field, up_ref, low_ref, left_ref, right_ref, change):
    for f in range(2):
        field[f, pl.ds(0, 3), pl.ds(8, 64), :] = change(up_ref[f].astype(F32))
        field[f, pl.ds(35, 3), pl.ds(8, 64), :] = change(low_ref[f].astype(F32))
        field[f, :, pl.ds(4, 4), :] = change(left_ref[f].astype(F32))
        field[f, :, pl.ds(72, 4), :] = change(right_ref[f].astype(F32))


GROUP = 6


def next_kernel(act_ref, up_ref, low_ref, left_ref, right_ref, gain_ref, weight_ref, out_ref, planes, act, flat):
    gain = gain_ref[...].reshape(1, 1, 128)
    spread(act, up_ref, low_ref, left_ref, right_ref, lambda values: silu(scaled(values, gain)))
    act[:, pl.ds(3, 32), pl.ds(8, 64), :] = act_ref[...]

    def build(q):
        for rp in range(2):
            for v in range(4):
                both = [act[f, 2 * q + rp, pl.ds(5 + v, 40, stride=2), :].astype(BF16) for f in range(2)]
                planes[rp, v, q, pl.ds(0, 40), :] = jnp.concatenate(both, -1)

    built = 0
    for base in range(0, 18, GROUP):
        while built < base + GROUP + 1:
            build(built)
            built += 1
        total = dot(taps_at(planes, base), weight_ref[...].reshape(4096, 256)).reshape(GROUP, PITCH, 256)
        for k in range(GROUP):
            flat[pl.ds((base + k) * 34, 34), :] = total[k, :34]
    flat[pl.ds(612, 12), :] = jnp.zeros((12, 256), F32)
    out_ref[...] = flat[...].astype(BF16)


def taps_at(planes, base):
    parts = []
    for u in range(4):
        for v in range(4):
            parts.append(planes[u % 2, v, pl.ds(base + u // 2, GROUP)].reshape(GROUP * PITCH, 256))
    return jnp.concatenate(parts, -1)


def own_kernel(x_ref, up_ref, low_ref, left_ref, right_ref, weight_ref, planes, down_ref, out_ref, raw, raw_planes):
    spread(raw, up_ref, low_ref, left_ref, right_ref, lambda values: values)
    raw[:, pl.ds(3, 32), pl.ds(8, 64), :] = x_ref[...].astype(F32)

    def build(q):
        for rp in range(2):
            for v in range(2):
                both = [raw[f, 2 * q + rp, pl.ds(6 + v, 40, stride=2), :].astype(BF16) for f in range(2)]
                raw_planes[rp, v, q, pl.ds(0, 40), :] = jnp.concatenate(both, -1)

    folds = []
    for r in range(2):
        for c in range(2):
            for f in range(2):
                at = (f * 4 + r * 2 + c) * 128
                folds.append(down_ref[at : at + 128, :])
    fold_weight = jnp.concatenate(folds, 0)
    built = 0
    for base in range(0, 18, GROUP):
        while built < base + GROUP + 1:
            build(built)
            built += 1
        parts = []
        for r in range(2):
            for c in range(2):
                rows = pl.ds(base + (r + 1) // 2, GROUP)
                parts.append(raw_planes[(r + 1) % 2, c, rows].reshape(GROUP * PITCH, 256))
        total = dot(taps_at(planes, base), weight_ref[...].reshape(4096, 256))
        total = total + dot(jnp.concatenate(parts, -1), fold_weight)
        out_ref[base : base + GROUP] = total.reshape(GROUP, PITCH, 256)


def fine_next(act, halos, gain, weight):
    return call(
        next_kernel,
        (shape((FLAT, 256), BF16), shape((2, 4, 19, PITCH, 256), BF16)),
        [VM] * 7,
        [pltpu.VMEM((2, 38, COLS, 128), F32), pltpu.VMEM((FLAT, 256), F32)],
        flops=1_800_000_000,
        name="fine_next",
    )(act, *halos, gain.reshape(1, 128), weight)


def fine_own(features, halos, weight, planes, down):
    return call(
        own_kernel,
        shape((18, PITCH, 256), F32),
        [VM] * 8,
        [pltpu.VMEM((2, 38, COLS, 128), F32), pltpu.VMEM((2, 2, 19, PITCH, 256), BF16)],
        flops=2_200_000_000,
        name="fine_own",
    )(features, *halos, weight, planes, down)


def folded(field):
    field = field.astype(BF16).reshape(2, 2, 4, 2, 16, 256)
    parts = [field[:, p, :, r].reshape(128, 256) for r in range(2) for p in range(2)]
    return jnp.concatenate(parts, -1)


def sent_kernel(
    flag_ref, own_ref, got_ref, gain_ref, conv_ref, down_ref, far_ref, near_ref, c1_ref, windows, reduced, got, act
):
    gain = gain_ref[...]
    got[...] = got_ref[...].astype(F32)
    start = (flag_ref[0] == 0).astype(F32)
    col = lax.broadcasted_iota(jnp.int32, (40, 128), 0)
    inside = ((col > 0) | (flag_ref[2] > 0)) & ((col < 33) | (flag_ref[2] < 7))
    inside = inside.astype(F32)
    ends = {0: (flag_ref[1] > 0).astype(F32), 17: (flag_ref[1] < 3).astype(F32)}
    fields = []
    done = 0
    for part in range(2):
        for row in range(done, 10 + 8 * part):
            value = own_ref[row, pl.ds(0, 40), :] + got[pl.ds(row * 34, 40), :]
            value = value.astype(BF16).astype(F32)
            active = silu(scaled(value, gain))
            keep = inside * ends[row] if row in ends else inside
            for half in range(2):
                reduced[half, row, pl.ds(0, 40), :] = value[:, half * 128 : half * 128 + 128]
                act[half, row, pl.ds(0, 40), :] = active[:, half * 128 : half * 128 + 128] * keep
        done = 10 + 8 * part
        for row in range(8 * part, 8 * part + 10):
            for v in range(4):
                halves = [act[half, row, pl.ds(v, 16, stride=2), :] for half in range(2)]
                cells = jnp.concatenate(halves, -1).astype(BF16)
                for p in range(2):
                    for i in range(3):
                        at = row - i - 8 * part
                        if 0 <= v - p < 3 and 0 <= at < 8:
                            tap = i * 3 + v - p
                            windows[pl.ds(((part * 2 + p) * 8 + at) * 16, 16), pl.ds(tap * 256, 256)] = cells
        lhs = windows[pl.ds(part * 256, 256), :]
        fields.append([dot(lhs, conv_ref[s].reshape(2304, 256)) for s in range(2)])
    c0 = jnp.concatenate([fields[0][0], fields[1][0]], 0)
    c1 = jnp.concatenate([fields[0][1], fields[1][1]], 0) + c0 * start
    c1_ref[...] = c1
    both = dot(jnp.concatenate([folded(c0), folded(c1)], 0), down_ref[...]).astype(BF16)
    far_ref[...] = both[:128]
    near_ref[...] = both[128:]


def here_kernel(flag_ref, windows, reduced, c1_ref, conv_ref, down_ref, latent_ref):
    start = (flag_ref[0] == 0).astype(F32)
    plain = []
    for part in range(2):
        for p in range(2):
            for row in range(8 * part, 8 * part + 8):
                halves = [reduced[half, row + 1, pl.ds(1 + p, 16, stride=2), :] for half in range(2)]
                plain.append(jnp.concatenate(halves, -1))
    c2 = dot(windows[...], conv_ref[2].reshape(2304, 256)) + c1_ref[...] * start
    latent_ref[...] = dot(folded(c2 + jnp.concatenate(plain, 0)), down_ref[...])


def coarse(flags, own, got, gain, conv, down):
    conv = conv.reshape(3, 9, 256, 256)
    rows = shape((128, 512), BF16)
    field = shape((512, 256), F32)
    far, near, c1, windows, reduced = call(
        sent_kernel,
        (rows, rows, field, shape((512, 2304), BF16), shape((2, 18, PITCH, 128), F32)),
        [SM] + [VM] * 5,
        [pltpu.VMEM((FLAT, 256), F32), pltpu.VMEM((2, 18, PITCH, 128), F32)],
        flops=1_500_000_000,
        name="coarse_sent",
    )(flags, own, got, gain.reshape(1, 256), conv, down)
    latent = call(here_kernel, shape((128, 512), F32), [SM] + [VM] * 5, flops=1000, moved=1000, name="coarse_here")(
        flags, windows, reduced, c1, conv, down
    )
    return near, far, latent


def mix_kernel(query_ref, key_ref, value_ref, out_ref, score_ref, mix_ref):
    scores = lax.dot_general(query_ref[...], key_ref[...], (((1,), (1,)), ((), ())), preferred_element_type=F32)
    score_ref[...] = (scores * (1.0 / math.sqrt(512))).astype(BF16)
    mix_ref[...] = dot(value_ref[...], out_ref[...]).astype(BF16)


def latent_kernel(own_ref, near_ref, far_ref, gain_ref, score_ref, latent_ref, query_ref, copies_ref):
    latent = (own_ref[...] + near_ref[...].astype(F32) + far_ref[...].astype(F32)).astype(BF16)
    latent_ref[...] = latent
    normed = scaled(latent.astype(F32), gain_ref[...]).astype(BF16)
    for k in range(copies_ref.shape[0]):
        copies_ref[k] = normed
    query_ref[...] = dot(normed, score_ref[...]).astype(BF16)


def packed(values, level):
    across = jnp.broadcast_to(level, (128, 128)).T[:16]
    high = across.astype(BF16).astype(F32)
    middle = (across - high).astype(BF16).astype(F32)
    low = across - high - middle
    row = lax.broadcasted_iota(jnp.int32, (16, 128), 0)
    parts = jnp.where(row == 0, high, jnp.where(row == 1, middle, jnp.where(row == 2, low, 0.0)))
    last = jnp.concatenate([parts, jnp.zeros((16, 384), F32)], -1)
    return jnp.concatenate([values, last], 0).astype(BF16)


def level_of(block):
    across = jnp.sum(block[128:, :128].astype(F32), 0, keepdims=True)
    return jnp.broadcast_to(across, (128, 128)).T[:, :1]


def softmax_part(queries, keys):
    scores = lax.dot_general(queries, keys, (((1,), (1,)), ((), ())), preferred_element_type=F32)
    top = jnp.max(scores, -1, keepdims=True)
    expo = jnp.exp(scores - top)
    total = jnp.sum(expo, -1, keepdims=True)
    return dot(expo.astype(BF16), keys) / total, top + jnp.log(total)


def attend_two_kernel(q1_ref, q2_ref, keys_ref, other_keys_ref, sent1_ref, sent2_ref):
    keys = jnp.concatenate([keys_ref[...], other_keys_ref[...]], 0)
    mixed, level = softmax_part(jnp.concatenate([q1_ref[...], q2_ref[...]], 0), keys)
    sent1_ref[...] = packed(mixed[:128], level[:128])
    sent2_ref[...] = packed(mixed[128:], level[128:])


def attend_last_kernel(q3_ref, mine_ref, keys_ref, other_keys_ref, sent3_ref, mixed_ref, level_ref):
    keys = jnp.concatenate([keys_ref[...], other_keys_ref[...]], 0)
    mixed, level = softmax_part(jnp.concatenate([q3_ref[...], mine_ref[...]], 0), keys)
    sent3_ref[...] = packed(mixed[:128], level[:128])
    mixed_ref[...] = mixed[128:]
    level_ref[...] = jnp.broadcast_to(level[128:], (128, 128))


def finish_kernel(mixed_ref, level_ref, got1_ref, got2_ref, got3_ref, latent_ref, mix_ref, out_ref):
    blocks = [ref[...] for ref in (got1_ref, got2_ref, got3_ref)]
    levels = [level_ref[:, :1]] + [level_of(block) for block in blocks]
    values = [mixed_ref[...]] + [block[:128].astype(F32) for block in blocks]
    top = functools.reduce(jnp.maximum, levels)
    shares = [jnp.exp(level - top) for level in levels]
    summed = sum(value * share for value, share in zip(values, shares))
    attended = summed / sum(shares)
    out_ref[...] = (latent_ref[...].astype(F32) + dot(attended.astype(BF16), mix_ref[...])).astype(BF16)


def swapped(value, axis, count, first):
    pairs = []
    for low in range(first, count - 1, 2):
        pairs += [(low, low + 1), (low + 1, low)]
    return lax.ppermute(value, axis, pairs)


def turned(value, step):
    return lax.ppermute(value, RING, [(i, (i + step) % 4) for i in range(4)])


def sides(block, axis, count):
    odd = lax.axis_index(axis) % 2
    rows = shape((2, 3, 64, 128), BF16)
    inner, outer = call(
        edges_kernel, (rows, rows), [SM, HB], [pltpu.SemaphoreType.DMA((2,))], flops=1000, name="edges"
    )(odd.astype(jnp.int32).reshape(1), kept(block))
    got_inner = swapped(inner, axis, count, 0)
    got_outer = swapped(outer, axis, count, 1)
    even = odd == 0
    return jnp.where(even, got_outer, got_inner), jnp.where(even, got_inner, got_outer)


def per_device(
    features, gain_fine, conv_fine, down_fine, gain_coarse, conv_coarse, down_coarse,
    gain_latent, w_query, w_key, w_value, w_out,
):
    rows = shape((128, 512), BF16)
    tm = lax.axis_index("tm").astype(jnp.int32)
    flags = jnp.stack([tm, lax.axis_index(HEIGHT).astype(jnp.int32), lax.axis_index(WIDTH).astype(jnp.int32)])
    above, below = sides(features, HEIGHT, 4)
    act, first, last, conv_here, down_here = prepare(features, gain_fine, conv_fine, down_fine)
    above, below, act, first, last = lax.optimization_barrier((above, below, act, first, last))
    first = jnp.concatenate([above[:, :, :4], first, below[:, :, :4]], 1)
    last = jnp.concatenate([above[:, :, 60:], last, below[:, :, 60:]], 1)
    odd = lax.axis_index(WIDTH) % 2 == 1
    got_inner = swapped(jnp.where(odd, first, last), WIDTH, 8, 0)
    got_outer = swapped(jnp.where(odd, last, first), WIDTH, 8, 1)
    weight_next = compose(False, flags, conv_here, down_here)
    got_inner, got_outer, weight_next = lax.optimization_barrier((got_inner, got_outer, weight_next))
    left, right = jnp.where(odd, got_inner, got_outer), jnp.where(odd, got_outer, got_inner)
    halos = (above, below, left, right)
    sent, planes = fine_next(act, halos, gain_fine, weight_next)
    sent, conv_here, down_here = lax.optimization_barrier((sent, conv_here, down_here))
    got = lax.ppermute(sent, "tm", [(i, i + 1) for i in range(7)])
    weight_own = compose(True, flags, conv_here, down_here)
    own = fine_own(features, halos, weight_own, planes, down_here)
    square = shape((512, 512), BF16)
    w_score, w_mix = call(mix_kernel, (square, square), [VM] * 4, flops=1000, moved=1000, name="mix")(
        w_query, w_key, w_value, w_out
    )
    got, own, w_score, w_mix = lax.optimization_barrier((got, own, w_score, w_mix))
    near, far, latent_own = coarse(flags, own, got, gain_coarse, conv_coarse, down_coarse)
    far = lax.ppermute(far, "tm", [(i, i + 2) for i in range(6)])
    near = lax.ppermute(near, "tm", [(i, i + 1) for i in range(7)])
    latent_in, query, copies = call(
        latent_kernel, (rows, rows, shape((4, 128, 512), BF16)), [VM] * 5, flops=80_000_000, name="latent"
    )(latent_own, near, far, gain_latent.reshape(1, 512), w_score)
    keys = lax.all_to_all(copies, "y", 0, 0, tiled=True).reshape(512, 512)
    two, back, ahead = (turned(query, step) for step in (2, 3, 1))
    keys, two, back = lax.optimization_barrier((keys, two, back))
    other_keys = swapped(keys, "core", 2, 0)
    block = shape((144, 512), BF16)
    sent_two, sent_back = call(attend_two_kernel, (block, block), [VM] * 4, flops=550_000_000, name="attend_two")(
        two, back, keys, other_keys
    )
    sent_ahead, mixed, level = call(
        attend_last_kernel,
        (block, shape((128, 512), F32), shape((128, 128), F32)),
        [VM] * 4,
        flops=550_000_000,
        name="attend_last",
    )(ahead, query, keys, other_keys)
    got = [turned(part, -step) for step, part in ((2, sent_two), (3, sent_back), (1, sent_ahead))]
    out = call(finish_kernel, rows, [VM] * 7, flops=70_000_000, name="finish")(mixed, level, *got, latent_in, w_mix)
    return out.reshape(1, 8, 16, 512)


def solution(mesh):
    split = Mesh(mesh.devices.reshape(8, 2, 2, 4, 2), ("tm", "hx", "core", "y", "lx"))
    placed = (P("tm", HEIGHT, WIDTH, None),) + (P(),) * 11
    return jax.shard_map(
        per_device, mesh=split, in_specs=placed,
        out_specs=P("tm", HEIGHT, WIDTH, None), check_vma=False,
    )
```

```python
import functools
import math

import jax
import jax.numpy as jnp
from jax import lax
from jax.experimental import pallas as pl
from jax.experimental.pallas import tpu as pltpu
from jax.sharding import Mesh, PartitionSpec as P

EPSILON = 1e-06
BF16 = jnp.bfloat16
F32 = jnp.float32
HEIGHT = ("hx", "core")
WIDTH = ("y", "lx")
RING = ("hx", "lx")
VMEM_LIMIT = 32 * 1024 * 1024
VM = pl.BlockSpec(memory_space=pltpu.VMEM)
HB = pl.BlockSpec(memory_space=pltpu.HBM)
SM = pl.BlockSpec(memory_space=pltpu.SMEM)


def call(kernel, out, ins, scratch=(), flops=0, moved=4 << 20, name=None):
    return pl.pallas_call(
        kernel,
        out_shape=out,
        in_specs=ins,
        out_specs=jax.tree.map(lambda _: VM, out),
        scratch_shapes=list(scratch),
        compiler_params=pltpu.CompilerParams(vmem_limit_bytes=VMEM_LIMIT),
        cost_estimate=pl.CostEstimate(flops=flops, bytes_accessed=moved, transcendentals=0),
        name=name,
    )


def kept(value):
    return pltpu.with_memory_space_constraint(value, pltpu.HBM)


def shape(dims, dtype):
    return jax.ShapeDtypeStruct(dims, dtype)


def dot(a, b):
    return jnp.dot(a, b, preferred_element_type=F32)


def scaled(values, gain):
    mean = jnp.mean(values * values, axis=-1, keepdims=True)
    return values * lax.rsqrt(mean + EPSILON) * gain


def silu(values):
    return values * jax.nn.sigmoid(values)


def compose_kernel(own, flag_ref, conv, down, out_ref, acc):
    acc[...] = jnp.zeros_like(acc)
    start = flag_ref[0] == 0
    for i in range(3):
        k0, k1 = (conv[s, i].reshape(384, 128) for s in range(2))
        if own:
            k2 = conv[2, i].reshape(384, 128)
            f0, f1, f2 = (k.astype(F32) for k in (k0, k1, k2))
            k2s = jnp.where(start, f0 + f1 + f2, f2).astype(BF16)
            k1s = jnp.where(start, f0 + f1, f1).astype(BF16)
            wide, narrow, wide_at, narrow_at, half = jnp.concatenate([k2s, k1s], -1), k2, 0, 1, 1
        else:
            wide, narrow, wide_at, narrow_at, half = jnp.concatenate([k1, k0], -1), k0, 1, 0, 0
        for r in range(2):
            for c in range(2):
                at = (r * 2 + c) * 128
                halves = [down[f * 512 + at : f * 512 + at + 128, :] for f in range(2)]
                both = dot(wide, jnp.concatenate(halves, 0))
                one = dot(narrow, halves[half])
                for j in range(3):
                    tap = (i + r) * 4 + j + c
                    rows = slice(j * 128, j * 128 + 128)
                    acc[tap, wide_at * 128 : wide_at * 128 + 128, :] += both[rows]
                    acc[tap, narrow_at * 128 : narrow_at * 128 + 128, :] += one[rows]
    out_ref[...] = acc[...].astype(BF16)


def compose(own, tm, conv_fine, down_fine):
    return call(
        functools.partial(compose_kernel, own),
        shape((16, 256, 256), BF16),
        [SM, VM, VM],
        [pltpu.VMEM((16, 256, 256), F32)],
        flops=900_000_000,
        name="compose_own" if own else "compose_next",
    )(tm, conv_fine, down_fine)


COLS = 104
PITCH = 48
FLAT = 624


def edges_kernel(odd_ref, x_hbm, inner_ref, outer_ref, sems):
    odd = odd_ref[0]
    inner = pltpu.make_async_copy(x_hbm.at[:, pl.ds((1 - odd) * 29, 3)], inner_ref, sems.at[0])
    outer = pltpu.make_async_copy(x_hbm.at[:, pl.ds(odd * 29, 3)], outer_ref, sems.at[1])
    inner.start()
    outer.start()
    inner.wait()
    outer.wait()


def prepare_kernel(
    x_hbm, gain_hbm, conv_hbm, down_hbm, act_ref, first_ref, last_ref, conv_ref, down_ref, x, gain_ref, sems
):
    fetches = []
    for k in range(4):
        rows = pl.ds(k * 8, 8)
        fetches.append(pltpu.make_async_copy(x_hbm.at[:, rows], x.at[:, rows], sems.at[k]))
        fetches[k].start()
    fetch_gain = pltpu.make_async_copy(gain_hbm, gain_ref, sems.at[4])
    fetch_gain.start()
    weights = [pltpu.make_async_copy(conv_hbm, conv_ref, sems.at[5]), pltpu.make_async_copy(down_hbm, down_ref, sems.at[6])]
    for fetch in weights:
        fetch.start()
    fetch_gain.wait()
    gain = gain_ref[...].reshape(1, 1, 128)
    for k in range(4):
        fetches[k].wait()
        for f in range(2):
            for half in range(2):
                rows = pl.ds(k * 8 + half * 4, 4)
                act_ref[f, rows] = silu(scaled(x[f, rows].astype(F32), gain))
    first_ref[...] = x[:, :, 0:4]
    last_ref[...] = x[:, :, 60:64]
    for fetch in weights:
        fetch.wait()


def prepare(features, gain, conv, down):
    edge = shape((2, 32, 4, 128), BF16)
    return call(
        prepare_kernel,
        (shape((2, 32, 64, 128), F32), edge, edge, shape((3, 3, 3, 128, 128), BF16), shape((1024, 256), BF16)),
        [HB] * 4,
        [pltpu.VMEM((2, 32, 64, 128), BF16), pltpu.VMEM((1, 128), F32), pltpu.SemaphoreType.DMA((7,))],
        flops=10_000_000,
        name="prepare",
    )(kept(features), kept(gain.reshape(1, 128)), kept(conv.reshape(3, 3, 3, 128, 128)), kept(down))


def spread(field, up_ref, low_ref, left_ref, right_ref, change):
    for f in range(2):
        field[f, pl.ds(0, 3), pl.ds(8, 64), :] = change(up_ref[f].astype(F32))
        field[f, pl.ds(35, 3), pl.ds(8, 64), :] = change(low_ref[f].astype(F32))
        field[f, :, pl.ds(4, 4), :] = change(left_ref[f].astype(F32))
        field[f, :, pl.ds(72, 4), :] = change(right_ref[f].astype(F32))


GROUP = 6


def next_kernel(act_ref, up_ref, low_ref, left_ref, right_ref, gain_ref, weight_ref, out_ref, planes, act, flat):
    gain = gain_ref[...].reshape(1, 1, 128)
    spread(act, up_ref, low_ref, left_ref, right_ref, lambda values: silu(scaled(values, gain)))
    act[:, pl.ds(3, 32), pl.ds(8, 64), :] = act_ref[...]

    def build(q):
        for rp in range(2):
            for v in range(4):
                both = [act[f, 2 * q + rp, pl.ds(5 + v, 40, stride=2), :].astype(BF16) for f in range(2)]
                planes[rp, v, q, pl.ds(0, 40), :] = jnp.concatenate(both, -1)

    built = 0
    for base in range(0, 18, GROUP):
        while built < base + GROUP + 1:
            build(built)
            built += 1
        total = dot(taps_at(planes, base), weight_ref[...].reshape(4096, 256)).reshape(GROUP, PITCH, 256)
        for k in range(GROUP):
            flat[pl.ds((base + k) * 34, 34), :] = total[k, :34]
    flat[pl.ds(612, 12), :] = jnp.zeros((12, 256), F32)
    out_ref[...] = flat[...].astype(BF16)


def taps_at(planes, base):
    parts = []
    for u in range(4):
        for v in range(4):
            parts.append(planes[u % 2, v, pl.ds(base + u // 2, GROUP)].reshape(GROUP * PITCH, 256))
    return jnp.concatenate(parts, -1)


def own_kernel(x_ref, up_ref, low_ref, left_ref, right_ref, weight_ref, planes, down_ref, out_ref, raw, raw_planes):
    spread(raw, up_ref, low_ref, left_ref, right_ref, lambda values: values)
    raw[:, pl.ds(3, 32), pl.ds(8, 64), :] = x_ref[...].astype(F32)

    def build(q):
        for rp in range(2):
            for v in range(2):
                both = [raw[f, 2 * q + rp, pl.ds(6 + v, 40, stride=2), :].astype(BF16) for f in range(2)]
                raw_planes[rp, v, q, pl.ds(0, 40), :] = jnp.concatenate(both, -1)

    folds = []
    for r in range(2):
        for c in range(2):
            for f in range(2):
                at = (f * 4 + r * 2 + c) * 128
                folds.append(down_ref[at : at + 128, :])
    fold_weight = jnp.concatenate(folds, 0)
    built = 0
    for base in range(0, 18, GROUP):
        while built < base + GROUP + 1:
            build(built)
            built += 1
        parts = []
        for r in range(2):
            for c in range(2):
                rows = pl.ds(base + (r + 1) // 2, GROUP)
                parts.append(raw_planes[(r + 1) % 2, c, rows].reshape(GROUP * PITCH, 256))
        total = dot(taps_at(planes, base), weight_ref[...].reshape(4096, 256))
        total = total + dot(jnp.concatenate(parts, -1), fold_weight)
        out_ref[base : base + GROUP] = total.reshape(GROUP, PITCH, 256)


def fine_next(act, halos, gain, weight):
    return call(
        next_kernel,
        (shape((FLAT, 256), BF16), shape((2, 4, 19, PITCH, 256), BF16)),
        [VM] * 7,
        [pltpu.VMEM((2, 38, COLS, 128), F32), pltpu.VMEM((FLAT, 256), F32)],
        flops=1_800_000_000,
        name="fine_next",
    )(act, *halos, gain.reshape(1, 128), weight)


def fine_own(features, halos, weight, planes, down):
    return call(
        own_kernel,
        shape((18, PITCH, 256), F32),
        [VM] * 8,
        [pltpu.VMEM((2, 38, COLS, 128), F32), pltpu.VMEM((2, 2, 19, PITCH, 256), BF16)],
        flops=2_200_000_000,
        name="fine_own",
    )(features, *halos, weight, planes, down)


def folded(field):
    field = field.astype(BF16).reshape(2, 2, 4, 2, 16, 256)
    parts = [field[:, p, :, r].reshape(128, 256) for r in range(2) for p in range(2)]
    return jnp.concatenate(parts, -1)


def sent_kernel(
    flag_ref, own_ref, got_ref, gain_ref, conv_ref, down_ref, far_ref, near_ref, c1_ref, windows, reduced, got, act
):
    gain = gain_ref[...]
    got[...] = got_ref[...].astype(F32)
    start = (flag_ref[0] == 0).astype(F32)
    col = lax.broadcasted_iota(jnp.int32, (40, 128), 0)
    inside = ((col > 0) | (flag_ref[2] > 0)) & ((col < 33) | (flag_ref[2] < 7))
    inside = inside.astype(F32)
    ends = {0: (flag_ref[1] > 0).astype(F32), 17: (flag_ref[1] < 3).astype(F32)}
    fields = []
    done = 0
    for part in range(2):
        for row in range(done, 10 + 8 * part):
            value = own_ref[row, pl.ds(0, 40), :] + got[pl.ds(row * 34, 40), :]
            value = value.astype(BF16).astype(F32)
            active = silu(scaled(value, gain))
            keep = inside * ends[row] if row in ends else inside
            for half in range(2):
                reduced[half, row, pl.ds(0, 40), :] = value[:, half * 128 : half * 128 + 128]
                act[half, row, pl.ds(0, 40), :] = active[:, half * 128 : half * 128 + 128] * keep
        done = 10 + 8 * part
        for row in range(8 * part, 8 * part + 10):
            for v in range(4):
                halves = [act[half, row, pl.ds(v, 16, stride=2), :] for half in range(2)]
                cells = jnp.concatenate(halves, -1).astype(BF16)
                for p in range(2):
                    for i in range(3):
                        at = row - i - 8 * part
                        if 0 <= v - p < 3 and 0 <= at < 8:
                            tap = i * 3 + v - p
                            windows[pl.ds(((part * 2 + p) * 8 + at) * 16, 16), pl.ds(tap * 256, 256)] = cells
        lhs = windows[pl.ds(part * 256, 256), :]
        fields.append([dot(lhs, conv_ref[s].reshape(2304, 256)) for s in range(2)])
    c0 = jnp.concatenate([fields[0][0], fields[1][0]], 0)
    c1 = jnp.concatenate([fields[0][1], fields[1][1]], 0) + c0 * start
    c1_ref[...] = c1
    both = dot(jnp.concatenate([folded(c0), folded(c1)], 0), down_ref[...]).astype(BF16)
    far_ref[...] = both[:128]
    near_ref[...] = both[128:]


def here_kernel(flag_ref, windows, reduced, c1_ref, conv_ref, down_ref, latent_ref):
    start = (flag_ref[0] == 0).astype(F32)
    plain = []
    for part in range(2):
        for p in range(2):
            for row in range(8 * part, 8 * part + 8):
                halves = [reduced[half, row + 1, pl.ds(1 + p, 16, stride=2), :] for half in range(2)]
                plain.append(jnp.concatenate(halves, -1))
    c2 = dot(windows[...], conv_ref[2].reshape(2304, 256)) + c1_ref[...] * start
    latent_ref[...] = dot(folded(c2 + jnp.concatenate(plain, 0)), down_ref[...])


def coarse(flags, own, got, gain, conv, down):
    conv = conv.reshape(3, 9, 256, 256)
    rows = shape((128, 512), BF16)
    field = shape((512, 256), F32)
    far, near, c1, windows, reduced = call(
        sent_kernel,
        (rows, rows, field, shape((512, 2304), BF16), shape((2, 18, PITCH, 128), F32)),
        [SM] + [VM] * 5,
        [pltpu.VMEM((FLAT, 256), F32), pltpu.VMEM((2, 18, PITCH, 128), F32)],
        flops=1_500_000_000,
        name="coarse_sent",
    )(flags, own, got, gain.reshape(1, 256), conv, down)
    latent = call(here_kernel, shape((128, 512), F32), [SM] + [VM] * 5, flops=1000, moved=1000, name="coarse_here")(
        flags, windows, reduced, c1, conv, down
    )
    return near, far, latent


def mix_kernel(query_ref, key_ref, value_ref, out_ref, score_ref, mix_ref):
    scores = lax.dot_general(query_ref[...], key_ref[...], (((1,), (1,)), ((), ())), preferred_element_type=F32)
    score_ref[...] = (scores * (1.0 / math.sqrt(512))).astype(BF16)
    mix_ref[...] = dot(value_ref[...], out_ref[...]).astype(BF16)


def latent_kernel(own_ref, near_ref, far_ref, gain_ref, score_ref, latent_ref, query_ref, copies_ref):
    latent = (own_ref[...] + near_ref[...].astype(F32) + far_ref[...].astype(F32)).astype(BF16)
    latent_ref[...] = latent
    normed = scaled(latent.astype(F32), gain_ref[...]).astype(BF16)
    for k in range(copies_ref.shape[0]):
        copies_ref[k] = normed
    query_ref[...] = dot(normed, score_ref[...]).astype(BF16)


def packed(values, level):
    across = jnp.broadcast_to(level, (128, 128)).T[:16]
    high = across.astype(BF16).astype(F32)
    middle = (across - high).astype(BF16).astype(F32)
    low = across - high - middle
    row = lax.broadcasted_iota(jnp.int32, (16, 128), 0)
    parts = jnp.where(row == 0, high, jnp.where(row == 1, middle, jnp.where(row == 2, low, 0.0)))
    last = jnp.concatenate([parts, jnp.zeros((16, 384), F32)], -1)
    return jnp.concatenate([values, last], 0).astype(BF16)


def level_of(block):
    across = jnp.sum(block[128:, :128].astype(F32), 0, keepdims=True)
    return jnp.broadcast_to(across, (128, 128)).T[:, :1]


def softmax_part(queries, *parts):
    scores = [
        lax.dot_general(queries, keys, (((1,), (1,)), ((), ())), preferred_element_type=F32) for keys in parts
    ]
    top = functools.reduce(jnp.maximum, [jnp.max(score, -1, keepdims=True) for score in scores])
    expos = [jnp.exp(score - top) for score in scores]
    total = sum(jnp.sum(expo, -1, keepdims=True) for expo in expos)
    summed = sum(dot(expo.astype(BF16), keys) for expo, keys in zip(expos, parts))
    return summed * (1.0 / total), top + jnp.log(total)


def attend_two_kernel(q1_ref, q2_ref, keys_ref, other_keys_ref, sent1_ref, sent2_ref):
    keys = (keys_ref[...], other_keys_ref[...])
    mixed, level = softmax_part(jnp.concatenate([q1_ref[...], q2_ref[...]], 0), *keys)
    sent1_ref[...] = packed(mixed[:128], level[:128])
    sent2_ref[...] = packed(mixed[128:], level[128:])


def attend_last_kernel(q3_ref, mine_ref, keys_ref, other_keys_ref, sent3_ref, mixed_ref, level_ref):
    keys = (keys_ref[...], other_keys_ref[...])
    mixed, level = softmax_part(jnp.concatenate([q3_ref[...], mine_ref[...]], 0), *keys)
    sent3_ref[...] = packed(mixed[:128], level[:128])
    mixed_ref[...] = mixed[128:]
    level_ref[...] = jnp.broadcast_to(level[128:], (128, 128))


def finish_kernel(mixed_ref, level_ref, got1_ref, got2_ref, got3_ref, latent_ref, mix_ref, out_ref):
    blocks = [ref[...] for ref in (got1_ref, got2_ref, got3_ref)]
    levels = [level_ref[:, :1]] + [level_of(block) for block in blocks]
    values = [mixed_ref[...]] + [block[:128].astype(F32) for block in blocks]
    top = functools.reduce(jnp.maximum, levels)
    shares = [jnp.exp(level - top) for level in levels]
    summed = sum(value * share for value, share in zip(values, shares))
    attended = summed / sum(shares)
    out_ref[...] = (latent_ref[...].astype(F32) + dot(attended.astype(BF16), mix_ref[...])).astype(BF16)


def swapped(value, axis, count, first):
    pairs = []
    for low in range(first, count - 1, 2):
        pairs += [(low, low + 1), (low + 1, low)]
    return lax.ppermute(value, axis, pairs)


def turned(value, step):
    return lax.ppermute(value, RING, [(i, (i + step) % 4) for i in range(4)])


def sides(block, axis, count):
    odd = lax.axis_index(axis) % 2
    rows = shape((2, 3, 64, 128), BF16)
    inner, outer = call(
        edges_kernel, (rows, rows), [SM, HB], [pltpu.SemaphoreType.DMA((2,))], flops=1000, name="edges"
    )(odd.astype(jnp.int32).reshape(1), kept(block))
    got_inner = swapped(inner, axis, count, 0)
    got_outer = swapped(outer, axis, count, 1)
    even = odd == 0
    return jnp.where(even, got_outer, got_inner), jnp.where(even, got_inner, got_outer)


def per_device(
    features, gain_fine, conv_fine, down_fine, gain_coarse, conv_coarse, down_coarse,
    gain_latent, w_query, w_key, w_value, w_out,
):
    rows = shape((128, 512), BF16)
    tm = lax.axis_index("tm").astype(jnp.int32)
    flags = jnp.stack([tm, lax.axis_index(HEIGHT).astype(jnp.int32), lax.axis_index(WIDTH).astype(jnp.int32)])
    above, below = sides(features, HEIGHT, 4)
    act, first, last, conv_here, down_here = prepare(features, gain_fine, conv_fine, down_fine)
    above, below, act, first, last = lax.optimization_barrier((above, below, act, first, last))
    first = jnp.concatenate([above[:, :, :4], first, below[:, :, :4]], 1)
    last = jnp.concatenate([above[:, :, 60:], last, below[:, :, 60:]], 1)
    odd = lax.axis_index(WIDTH) % 2 == 1
    got_inner = swapped(jnp.where(odd, first, last), WIDTH, 8, 0)
    got_outer = swapped(jnp.where(odd, last, first), WIDTH, 8, 1)
    weight_next = compose(False, flags, conv_here, down_here)
    got_inner, got_outer, weight_next = lax.optimization_barrier((got_inner, got_outer, weight_next))
    left, right = jnp.where(odd, got_inner, got_outer), jnp.where(odd, got_outer, got_inner)
    halos = (above, below, left, right)
    sent, planes = fine_next(act, halos, gain_fine, weight_next)
    sent, conv_here, down_here = lax.optimization_barrier((sent, conv_here, down_here))
    got = lax.ppermute(sent, "tm", [(i, i + 1) for i in range(7)])
    weight_own = compose(True, flags, conv_here, down_here)
    own = fine_own(features, halos, weight_own, planes, down_here)
    square = shape((512, 512), BF16)
    w_score, w_mix = call(mix_kernel, (square, square), [VM] * 4, flops=1000, moved=1000, name="mix")(
        w_query, w_key, w_value, w_out
    )
    got, own, w_score, w_mix = lax.optimization_barrier((got, own, w_score, w_mix))
    near, far, latent_own = coarse(flags, own, got, gain_coarse, conv_coarse, down_coarse)
    far = lax.ppermute(far, "tm", [(i, i + 2) for i in range(6)])
    near = lax.ppermute(near, "tm", [(i, i + 1) for i in range(7)])
    latent_in, query, copies = call(
        latent_kernel, (rows, rows, shape((4, 128, 512), BF16)), [VM] * 5, flops=80_000_000, name="latent"
    )(latent_own, near, far, gain_latent.reshape(1, 512), w_score)
    keys = lax.all_to_all(copies, "y", 0, 0, tiled=True).reshape(512, 512)
    two, back, ahead = (turned(query, step) for step in (2, 3, 1))
    keys, two, back = lax.optimization_barrier((keys, two, back))
    other_keys = swapped(keys, "core", 2, 0)
    block = shape((144, 512), BF16)
    sent_two, sent_back = call(attend_two_kernel, (block, block), [VM] * 4, flops=550_000_000, name="attend_two")(
        two, back, keys, other_keys
    )
    sent_ahead, mixed, level = call(
        attend_last_kernel,
        (block, shape((128, 512), F32), shape((128, 128), F32)),
        [VM] * 4,
        flops=550_000_000,
        name="attend_last",
    )(ahead, query, keys, other_keys)
    got = [turned(part, -step) for step, part in ((2, sent_two), (3, sent_back), (1, sent_ahead))]
    out = call(finish_kernel, rows, [VM] * 7, flops=70_000_000, name="finish")(mixed, level, *got, latent_in, w_mix)
    return out.reshape(1, 8, 16, 512)


def solution(mesh):
    split = Mesh(mesh.devices.reshape(8, 2, 2, 4, 2), ("tm", "hx", "core", "y", "lx"))
    placed = (P("tm", HEIGHT, WIDTH, None),) + (P(),) * 11
    return jax.shard_map(
        per_device, mesh=split, in_specs=placed,
        out_specs=P("tm", HEIGHT, WIDTH, None), check_vma=False,
    )
```

```python
import functools
import math

import jax
import jax.numpy as jnp
from jax import lax
from jax.experimental import pallas as pl
from jax.experimental.pallas import tpu as pltpu
from jax.sharding import Mesh, PartitionSpec as P

EPSILON = 1e-06
BF16 = jnp.bfloat16
F32 = jnp.float32
HEIGHT = ("hx", "core")
WIDTH = ("y", "lx")
RING = ("hx", "lx")
VMEM_LIMIT = 32 * 1024 * 1024
VM = pl.BlockSpec(memory_space=pltpu.VMEM)
HB = pl.BlockSpec(memory_space=pltpu.HBM)
SM = pl.BlockSpec(memory_space=pltpu.SMEM)


def call(kernel, out, ins, scratch=(), flops=0, moved=4 << 20, name=None):
    return pl.pallas_call(
        kernel,
        out_shape=out,
        in_specs=ins,
        out_specs=jax.tree.map(lambda _: VM, out),
        scratch_shapes=list(scratch),
        compiler_params=pltpu.CompilerParams(vmem_limit_bytes=VMEM_LIMIT),
        cost_estimate=pl.CostEstimate(flops=flops, bytes_accessed=moved, transcendentals=0),
        name=name,
    )


def kept(value):
    return pltpu.with_memory_space_constraint(value, pltpu.HBM)


def shape(dims, dtype):
    return jax.ShapeDtypeStruct(dims, dtype)


def dot(a, b):
    return jnp.dot(a, b, preferred_element_type=F32)


def scaled(values, gain):
    mean = jnp.mean(values * values, axis=-1, keepdims=True)
    return values * lax.rsqrt(mean + EPSILON) * gain


def silu(values):
    return values * jax.nn.sigmoid(values)


def compose_kernel(own, flag_ref, conv, down, out_ref, acc):
    acc[...] = jnp.zeros_like(acc)
    start = flag_ref[0] == 0
    for i in range(3):
        k0, k1 = (conv[s, i].reshape(384, 128) for s in range(2))
        if own:
            k2 = conv[2, i].reshape(384, 128)
            f0, f1, f2 = (k.astype(F32) for k in (k0, k1, k2))
            k2s = jnp.where(start, f0 + f1 + f2, f2).astype(BF16)
            k1s = jnp.where(start, f0 + f1, f1).astype(BF16)
            wide, narrow, wide_at, narrow_at, half = jnp.concatenate([k2s, k1s], -1), k2, 0, 1, 1
        else:
            wide, narrow, wide_at, narrow_at, half = jnp.concatenate([k1, k0], -1), k0, 1, 0, 0
        for r in range(2):
            for c in range(2):
                at = (r * 2 + c) * 128
                halves = [down[f * 512 + at : f * 512 + at + 128, :] for f in range(2)]
                both = dot(wide, jnp.concatenate(halves, 0))
                one = dot(narrow, halves[half])
                for j in range(3):
                    tap = (i + r) * 4 + j + c
                    rows = slice(j * 128, j * 128 + 128)
                    acc[tap, wide_at * 128 : wide_at * 128 + 128, :] += both[rows]
                    acc[tap, narrow_at * 128 : narrow_at * 128 + 128, :] += one[rows]
    out_ref[...] = acc[...].astype(BF16)


def compose(own, tm, conv_fine, down_fine):
    return call(
        functools.partial(compose_kernel, own),
        shape((16, 256, 256), BF16),
        [SM, VM, VM],
        [pltpu.VMEM((16, 256, 256), F32)],
        flops=900_000_000,
        name="compose_own" if own else "compose_next",
    )(tm, conv_fine, down_fine)


COLS = 104
PITCH = 48
FLAT = 624


def edges_kernel(odd_ref, x_hbm, inner_ref, outer_ref, sems):
    odd = odd_ref[0]
    inner = pltpu.make_async_copy(x_hbm.at[:, pl.ds((1 - odd) * 29, 3)], inner_ref, sems.at[0])
    outer = pltpu.make_async_copy(x_hbm.at[:, pl.ds(odd * 29, 3)], outer_ref, sems.at[1])
    inner.start()
    outer.start()
    inner.wait()
    outer.wait()


def prepare_kernel(
    x_hbm, gain_hbm, conv_hbm, down_hbm, act_ref, first_ref, last_ref, conv_ref, down_ref, x, gain_ref, sems
):
    fetches = []
    for k in range(4):
        rows = pl.ds(k * 8, 8)
        fetches.append(pltpu.make_async_copy(x_hbm.at[:, rows], x.at[:, rows], sems.at[k]))
        fetches[k].start()
    fetch_gain = pltpu.make_async_copy(gain_hbm, gain_ref, sems.at[4])
    fetch_gain.start()
    weights = [pltpu.make_async_copy(conv_hbm, conv_ref, sems.at[5]), pltpu.make_async_copy(down_hbm, down_ref, sems.at[6])]
    for fetch in weights:
        fetch.start()
    fetch_gain.wait()
    gain = gain_ref[...].reshape(1, 1, 128)
    for k in range(4):
        fetches[k].wait()
        for f in range(2):
            for half in range(2):
                rows = pl.ds(k * 8 + half * 4, 4)
                act_ref[f, rows] = silu(scaled(x[f, rows].astype(F32), gain))
    first_ref[...] = x[:, :, 0:4]
    last_ref[...] = x[:, :, 60:64]
    for fetch in weights:
        fetch.wait()


def prepare(features, gain, conv, down):
    edge = shape((2, 32, 4, 128), BF16)
    return call(
        prepare_kernel,
        (shape((2, 32, 64, 128), F32), edge, edge, shape((3, 3, 3, 128, 128), BF16), shape((1024, 256), BF16)),
        [HB] * 4,
        [pltpu.VMEM((2, 32, 64, 128), BF16), pltpu.VMEM((1, 128), F32), pltpu.SemaphoreType.DMA((7,))],
        flops=10_000_000,
        name="prepare",
    )(kept(features), kept(gain.reshape(1, 128)), kept(conv.reshape(3, 3, 3, 128, 128)), kept(down))


def spread(field, up_ref, low_ref, left_ref, right_ref, change):
    for f in range(2):
        field[f, pl.ds(0, 3), pl.ds(8, 64), :] = change(up_ref[f].astype(F32))
        field[f, pl.ds(35, 3), pl.ds(8, 64), :] = change(low_ref[f].astype(F32))
        field[f, :, pl.ds(4, 4), :] = change(left_ref[f].astype(F32))
        field[f, :, pl.ds(72, 4), :] = change(right_ref[f].astype(F32))


GROUP = 6


def next_kernel(act_ref, up_ref, low_ref, left_ref, right_ref, gain_ref, weight_ref, out_ref, planes, act, flat):
    gain = gain_ref[...].reshape(1, 1, 128)
    spread(act, up_ref, low_ref, left_ref, right_ref, lambda values: silu(scaled(values, gain)))
    act[:, pl.ds(3, 32), pl.ds(8, 64), :] = act_ref[...]

    def build(q):
        for rp in range(2):
            for v in range(4):
                both = [act[f, 2 * q + rp, pl.ds(5 + v, 40, stride=2), :].astype(BF16) for f in range(2)]
                planes[rp, v, q, pl.ds(0, 40), :] = jnp.concatenate(both, -1)

    built = 0
    for base in range(0, 18, GROUP):
        while built < base + GROUP + 1:
            build(built)
            built += 1
        total = dot(taps_at(planes, base), weight_ref[...].reshape(4096, 256)).reshape(GROUP, PITCH, 256)
        for k in range(GROUP):
            flat[pl.ds((base + k) * 34, 34), :] = total[k, :34]
    flat[pl.ds(612, 12), :] = jnp.zeros((12, 256), F32)
    out_ref[...] = flat[...].astype(BF16)


def taps_at(planes, base):
    parts = []
    for u in range(4):
        for v in range(4):
            parts.append(planes[u % 2, v, pl.ds(base + u // 2, GROUP)].reshape(GROUP * PITCH, 256))
    return jnp.concatenate(parts, -1)


def own_kernel(x_ref, up_ref, low_ref, left_ref, right_ref, weight_ref, planes, down_ref, out_ref, raw, raw_planes):
    spread(raw, up_ref, low_ref, left_ref, right_ref, lambda values: values)
    raw[:, pl.ds(3, 32), pl.ds(8, 64), :] = x_ref[...].astype(F32)

    def build(q):
        for rp in range(2):
            for v in range(2):
                both = [raw[f, 2 * q + rp, pl.ds(6 + v, 40, stride=2), :].astype(BF16) for f in range(2)]
                raw_planes[rp, v, q, pl.ds(0, 40), :] = jnp.concatenate(both, -1)

    folds = []
    for r in range(2):
        for c in range(2):
            for f in range(2):
                at = (f * 4 + r * 2 + c) * 128
                folds.append(down_ref[at : at + 128, :])
    fold_weight = jnp.concatenate(folds, 0)
    built = 0
    for base in range(0, 18, GROUP):
        while built < base + GROUP + 1:
            build(built)
            built += 1
        parts = []
        for r in range(2):
            for c in range(2):
                rows = pl.ds(base + (r + 1) // 2, GROUP)
                parts.append(raw_planes[(r + 1) % 2, c, rows].reshape(GROUP * PITCH, 256))
        total = dot(taps_at(planes, base), weight_ref[...].reshape(4096, 256))
        total = total + dot(jnp.concatenate(parts, -1), fold_weight)
        out_ref[base : base + GROUP] = total.reshape(GROUP, PITCH, 256)


def fine_next(act, halos, gain, weight):
    return call(
        next_kernel,
        (shape((FLAT, 256), BF16), shape((2, 4, 19, PITCH, 256), BF16)),
        [VM] * 7,
        [pltpu.VMEM((2, 38, COLS, 128), F32), pltpu.VMEM((FLAT, 256), F32)],
        flops=1_800_000_000,
        name="fine_next",
    )(act, *halos, gain.reshape(1, 128), weight)


def fine_own(features, halos, weight, planes, down):
    return call(
        own_kernel,
        shape((18, PITCH, 256), F32),
        [VM] * 8,
        [pltpu.VMEM((2, 38, COLS, 128), F32), pltpu.VMEM((2, 2, 19, PITCH, 256), BF16)],
        flops=2_200_000_000,
        name="fine_own",
    )(features, *halos, weight, planes, down)


def folded(field):
    field = field.astype(BF16).reshape(2, 2, 4, 2, 16, 256)
    parts = [field[:, p, :, r].reshape(128, 256) for r in range(2) for p in range(2)]
    return jnp.concatenate(parts, -1)


def sent_kernel(
    flag_ref, own_ref, got_ref, gain_ref, conv_ref, down_ref, far_ref, near_ref, c1_ref, windows, reduced, got, act
):
    gain = gain_ref[...]
    got[...] = got_ref[...].astype(F32)
    start = (flag_ref[0] == 0).astype(F32)
    col = lax.broadcasted_iota(jnp.int32, (40, 128), 0)
    inside = ((col > 0) | (flag_ref[2] > 0)) & ((col < 33) | (flag_ref[2] < 7))
    inside = inside.astype(F32)
    ends = {0: (flag_ref[1] > 0).astype(F32), 17: (flag_ref[1] < 3).astype(F32)}
    fields = []
    done = 0
    for part in range(2):
        for row in range(done, 10 + 8 * part):
            value = own_ref[row, pl.ds(0, 40), :] + got[pl.ds(row * 34, 40), :]
            value = value.astype(BF16).astype(F32)
            active = silu(scaled(value, gain))
            keep = inside * ends[row] if row in ends else inside
            for half in range(2):
                reduced[half, row, pl.ds(0, 40), :] = value[:, half * 128 : half * 128 + 128]
                act[half, row, pl.ds(0, 40), :] = active[:, half * 128 : half * 128 + 128] * keep
        done = 10 + 8 * part
        for row in range(8 * part, 8 * part + 10):
            for v in range(4):
                halves = [act[half, row, pl.ds(v, 16, stride=2), :] for half in range(2)]
                cells = jnp.concatenate(halves, -1).astype(BF16)
                for p in range(2):
                    for i in range(3):
                        at = row - i - 8 * part
                        if 0 <= v - p < 3 and 0 <= at < 8:
                            tap = i * 3 + v - p
                            windows[pl.ds(((part * 2 + p) * 8 + at) * 16, 16), pl.ds(tap * 256, 256)] = cells
        lhs = windows[pl.ds(part * 256, 256), :]
        fields.append([dot(lhs, conv_ref[s].reshape(2304, 256)) for s in range(2)])
    c0 = jnp.concatenate([fields[0][0], fields[1][0]], 0)
    c1 = jnp.concatenate([fields[0][1], fields[1][1]], 0) + c0 * start
    c1_ref[...] = c1
    both = dot(jnp.concatenate([folded(c0), folded(c1)], 0), down_ref[...]).astype(BF16)
    far_ref[...] = both[:128]
    near_ref[...] = both[128:]


def here_kernel(flag_ref, windows, reduced, c1_ref, conv_ref, down_ref, latent_ref):
    start = (flag_ref[0] == 0).astype(F32)
    plain = []
    for part in range(2):
        for p in range(2):
            for row in range(8 * part, 8 * part + 8):
                halves = [reduced[half, row + 1, pl.ds(1 + p, 16, stride=2), :] for half in range(2)]
                plain.append(jnp.concatenate(halves, -1))
    c2 = dot(windows[...], conv_ref[2].reshape(2304, 256)) + c1_ref[...] * start
    latent_ref[...] = dot(folded(c2 + jnp.concatenate(plain, 0)), down_ref[...])


def coarse(flags, own, got, gain, conv, down):
    conv = conv.reshape(3, 9, 256, 256)
    rows = shape((128, 512), BF16)
    field = shape((512, 256), F32)
    far, near, c1, windows, reduced = call(
        sent_kernel,
        (rows, rows, field, shape((512, 2304), BF16), shape((2, 18, PITCH, 128), F32)),
        [SM] + [VM] * 5,
        [pltpu.VMEM((FLAT, 256), F32), pltpu.VMEM((2, 18, PITCH, 128), F32)],
        flops=1_500_000_000,
        name="coarse_sent",
    )(flags, own, got, gain.reshape(1, 256), conv, down)
    latent = call(here_kernel, shape((128, 512), F32), [SM] + [VM] * 5, flops=1000, moved=1000, name="coarse_here")(
        flags, windows, reduced, c1, conv, down
    )
    return near, far, latent


def mix_kernel(query_ref, key_ref, value_ref, out_ref, score_ref, mix_ref):
    scores = lax.dot_general(query_ref[...], key_ref[...], (((1,), (1,)), ((), ())), preferred_element_type=F32)
    score_ref[...] = (scores * (1.0 / math.sqrt(512))).astype(BF16)
    mix_ref[...] = dot(value_ref[...], out_ref[...]).astype(BF16)


def latent_kernel(own_ref, near_ref, far_ref, gain_ref, score_ref, latent_ref, query_ref, copies_ref):
    latent = (own_ref[...] + near_ref[...].astype(F32) + far_ref[...].astype(F32)).astype(BF16)
    latent_ref[...] = latent
    normed = scaled(latent.astype(F32), gain_ref[...]).astype(BF16)
    for k in range(copies_ref.shape[0]):
        copies_ref[k] = normed
    query_ref[...] = dot(normed, score_ref[...]).astype(BF16)


def packed(values, level):
    across = jnp.broadcast_to(level, (128, 128)).T[:16]
    high = across.astype(BF16).astype(F32)
    middle = (across - high).astype(BF16).astype(F32)
    low = across - high - middle
    row = lax.broadcasted_iota(jnp.int32, (16, 128), 0)
    parts = jnp.where(row == 0, high, jnp.where(row == 1, middle, jnp.where(row == 2, low, 0.0)))
    last = jnp.concatenate([parts, jnp.zeros((16, 384), F32)], -1)
    return jnp.concatenate([values, last], 0).astype(BF16)


def softmax_part(queries, *parts):
    scores = [
        lax.dot_general(queries, keys, (((1,), (1,)), ((), ())), preferred_element_type=F32) for keys in parts
    ]
    top = functools.reduce(jnp.maximum, [jnp.max(score, -1, keepdims=True) for score in scores])
    expos = [jnp.exp(score - top) for score in scores]
    total = sum(jnp.sum(expo, -1, keepdims=True) for expo in expos)
    summed = sum(dot(expo.astype(BF16), keys) for expo, keys in zip(expos, parts))
    return summed * (1.0 / total), top + jnp.log(total)


def attend_two_kernel(q1_ref, q2_ref, keys_ref, other_keys_ref, sent1_ref, sent2_ref):
    keys = (keys_ref[...], other_keys_ref[...])
    mixed, level = softmax_part(jnp.concatenate([q1_ref[...], q2_ref[...]], 0), *keys)
    sent1_ref[...] = packed(mixed[:128], level[:128])
    sent2_ref[...] = packed(mixed[128:], level[128:])


def attend_last_kernel(q3_ref, mine_ref, keys_ref, other_keys_ref, sent3_ref, mixed_ref, level_ref):
    keys = (keys_ref[...], other_keys_ref[...])
    mixed, level = softmax_part(jnp.concatenate([q3_ref[...], mine_ref[...]], 0), *keys)
    sent3_ref[...] = packed(mixed[:128], level[:128])
    mixed_ref[...] = mixed[128:]
    level_ref[...] = jnp.broadcast_to(level[128:], (128, 128))


def finish_kernel(mixed_ref, level_ref, got1_ref, got2_ref, got3_ref, latent_ref, mix_ref, out_ref):
    blocks = [ref[...] for ref in (got1_ref, got2_ref, got3_ref)]
    across = [jnp.sum(block[128:, :128].astype(F32), 0, keepdims=True) for block in blocks]
    turned_levels = jnp.concatenate(across + [jnp.zeros((125, 128), F32)], 0).T
    levels = [level_ref[:, :1]] + [turned_levels[:, k : k + 1] for k in range(3)]
    values = [mixed_ref[...]] + [block[:128].astype(F32) for block in blocks]
    top = functools.reduce(jnp.maximum, levels)
    shares = [jnp.exp(level - top) for level in levels]
    summed = sum(value * share for value, share in zip(values, shares))
    attended = summed / sum(shares)
    out_ref[...] = (latent_ref[...].astype(F32) + dot(attended.astype(BF16), mix_ref[...])).astype(BF16)


def swapped(value, axis, count, first):
    pairs = []
    for low in range(first, count - 1, 2):
        pairs += [(low, low + 1), (low + 1, low)]
    return lax.ppermute(value, axis, pairs)


def turned(value, step):
    return lax.ppermute(value, RING, [(i, (i + step) % 4) for i in range(4)])


def sides(block, axis, count):
    odd = lax.axis_index(axis) % 2
    rows = shape((2, 3, 64, 128), BF16)
    inner, outer = call(
        edges_kernel, (rows, rows), [SM, HB], [pltpu.SemaphoreType.DMA((2,))], flops=1000, name="edges"
    )(odd.astype(jnp.int32).reshape(1), kept(block))
    got_inner = swapped(inner, axis, count, 0)
    got_outer = swapped(outer, axis, count, 1)
    even = odd == 0
    return jnp.where(even, got_outer, got_inner), jnp.where(even, got_inner, got_outer)


def per_device(
    features, gain_fine, conv_fine, down_fine, gain_coarse, conv_coarse, down_coarse,
    gain_latent, w_query, w_key, w_value, w_out,
):
    rows = shape((128, 512), BF16)
    tm = lax.axis_index("tm").astype(jnp.int32)
    flags = jnp.stack([tm, lax.axis_index(HEIGHT).astype(jnp.int32), lax.axis_index(WIDTH).astype(jnp.int32)])
    above, below = sides(features, HEIGHT, 4)
    act, first, last, conv_here, down_here = prepare(features, gain_fine, conv_fine, down_fine)
    above, below, act, first, last = lax.optimization_barrier((above, below, act, first, last))
    first = jnp.concatenate([above[:, :, :4], first, below[:, :, :4]], 1)
    last = jnp.concatenate([above[:, :, 60:], last, below[:, :, 60:]], 1)
    odd = lax.axis_index(WIDTH) % 2 == 1
    got_inner = swapped(jnp.where(odd, first, last), WIDTH, 8, 0)
    got_outer = swapped(jnp.where(odd, last, first), WIDTH, 8, 1)
    weight_next = compose(False, flags, conv_here, down_here)
    got_inner, got_outer, weight_next = lax.optimization_barrier((got_inner, got_outer, weight_next))
    left, right = jnp.where(odd, got_inner, got_outer), jnp.where(odd, got_outer, got_inner)
    halos = (above, below, left, right)
    sent, planes = fine_next(act, halos, gain_fine, weight_next)
    sent, conv_here, down_here = lax.optimization_barrier((sent, conv_here, down_here))
    got = lax.ppermute(sent, "tm", [(i, i + 1) for i in range(7)])
    weight_own = compose(True, flags, conv_here, down_here)
    own = fine_own(features, halos, weight_own, planes, down_here)
    square = shape((512, 512), BF16)
    w_score, w_mix = call(mix_kernel, (square, square), [VM] * 4, flops=1000, moved=1000, name="mix")(
        w_query, w_key, w_value, w_out
    )
    got, own, w_score, w_mix = lax.optimization_barrier((got, own, w_score, w_mix))
    near, far, latent_own = coarse(flags, own, got, gain_coarse, conv_coarse, down_coarse)
    far = lax.ppermute(far, "tm", [(i, i + 2) for i in range(6)])
    near = lax.ppermute(near, "tm", [(i, i + 1) for i in range(7)])
    latent_in, query, copies = call(
        latent_kernel, (rows, rows, shape((4, 128, 512), BF16)), [VM] * 5, flops=80_000_000, name="latent"
    )(latent_own, near, far, gain_latent.reshape(1, 512), w_score)
    keys = lax.all_to_all(copies, "y", 0, 0, tiled=True).reshape(512, 512)
    two, back, ahead = (turned(query, step) for step in (2, 3, 1))
    keys, two, back = lax.optimization_barrier((keys, two, back))
    other_keys = swapped(keys, "core", 2, 0)
    block = shape((144, 512), BF16)
    sent_two, sent_back = call(attend_two_kernel, (block, block), [VM] * 4, flops=550_000_000, name="attend_two")(
        two, back, keys, other_keys
    )
    sent_ahead, mixed, level = call(
        attend_last_kernel,
        (block, shape((128, 512), F32), shape((128, 128), F32)),
        [VM] * 4,
        flops=550_000_000,
        name="attend_last",
    )(ahead, query, keys, other_keys)
    got = [turned(part, -step) for step, part in ((2, sent_two), (3, sent_back), (1, sent_ahead))]
    out = call(finish_kernel, rows, [VM] * 7, flops=70_000_000, name="finish")(mixed, level, *got, latent_in, w_mix)
    return out.reshape(1, 8, 16, 512)


def solution(mesh):
    split = Mesh(mesh.devices.reshape(8, 2, 2, 4, 2), ("tm", "hx", "core", "y", "lx"))
    placed = (P("tm", HEIGHT, WIDTH, None),) + (P(),) * 11
    return jax.shard_map(
        per_device, mesh=split, in_specs=placed,
        out_specs=P("tm", HEIGHT, WIDTH, None), check_vma=False,
    )
```
